32 devices in a mesh: seq: 2 (over core), head: 4 (over y, x), dp: 4 (over z).
Axes of the slice: x: 2, y: 2, z: 4, core: 2. Of those that a mesh axis runs over, the one named last changes fastest.
Arguments:
- tokens: bfloat16 [4, 4096, 768], P('dp', 'seq', 'head'), may hold values from -6 to 6
- attn_gain: bfloat16 [768], replicated, may hold values from 0.099609375 to 1.8984375
- attn_shift: bfloat16 [768], replicated, may hold values from -3 to 3
- qkv_weight: bfloat16 [768, 2304], P(None, 'head'), may hold values from -0.21875 to 0.21875
- qkv_bias: bfloat16 [2304], P('head'), may hold values from -3 to 3
- query_map: bfloat16 [12, 64, 64], P('head'), may hold values from -1.5 to 1.5
- key_map: bfloat16 [12, 64, 64], P('head'), may hold values from -1.5 to 1.5
- out_weight: bfloat16 [768, 768], P('head'), may hold values from -0.4375 to 0.4375
- out_bias: bfloat16 [768], P('head'), may hold values from -3 to 3
- mlp_gain: bfloat16 [768], replicated, may hold values from 0.099609375 to 1.8984375
- mlp_shift: bfloat16 [768], replicated, may hold values from -3 to 3
- up_weight: bfloat16 [768, 3072], P(None, 'head'), may hold values from -1 to 1
- up_bias: bfloat16 [3072], P('head'), may hold values from -3 to 3
- down_weight: bfloat16 [3072, 768], P('head'), may hold values from -0.4375 to 0.4375
- down_bias: bfloat16 [768], P('head'), may hold values from -3 to 3
- positions: int32 [4, 4096], P('dp', 'seq'), may hold values from 0 to 2048, as said below
- out_grad: bfloat16 [4, 4096, 768], P('dp', 'seq', 'head'), may hold values from -6 to 6
Outputs:
- block_out: bfloat16 [4, 4096, 768], P('dp', 'seq', 'head')
- tokens_grad: bfloat16 [4, 4096, 768], P('dp', 'seq', 'head')
- attngain_grad: float32 [768], P('head')
- attnshift_grad: float32 [768], P('head')
- qkvweight_grad: float32 [768, 2304], P(None, 'head')
- qkvbias_grad: float32 [2304], P('head')
- querymap_grad: float32 [12, 64, 64], P('head')
- keymap_grad: float32 [12, 64, 64], P('head')
- outweight_grad: float32 [768, 768], P('head')
- outbias_grad: float32 [768], P('head')
- mlpgain_grad: float32 [768], P('head')
- mlpshift_grad: float32 [768], P('head')
- upweight_grad: float32 [768, 3072], P(None, 'head')
- upbias_grad: float32 [3072], P('head')
- downweight_grad: float32 [3072, 768], P('head')
- downbias_grad: float32 [768], P('head')
The draws below stay inside these ranges and needn't reach their ends.
Inputs may be any that keep to these rules, and one draw needn't show every extreme that they name: positions[s, t] is 0 where a document begins, which includes t = 0, and one more than positions[s, t - 1] elsewhere.
All inputs are finite; a program needn't handle non-finite values.
Results may differ from the reference program's by a relative error of at most 0.029.
Values may be sent and summed in bfloat16 or wider, within the bound.
No kernel may reach another device: no remote copies, remote signals or barrier semaphores. Data moves between devices by JAX's collectives and lax.ppermute only.
A program may use at most 192 MiB of HBM per device.

```python
import jax
import jax.numpy as jnp
from jax import lax

D = 768
H = 12
HEAD = 64
FF = 3072
FEAT = 128
BLOCK = 64
TOK_DEV = 2048
LEN = 4096
SEQS = 4


def draw_positions(key, part):
    first_key = jax.random.fold_in(key, 11)
    last_key = jax.random.fold_in(key, 12)
    early = jax.random.randint(first_key, (SEQS, 2), 1, TOK_DEV // 2, dtype=jnp.int32)
    late = jax.random.randint(last_key, (SEQS, 2), LEN - TOK_DEV // 2, LEN, dtype=jnp.int32)
    early_edge = jnp.full((SEQS, 1), TOK_DEV // 2 - 1, jnp.int32)
    late_edge = jnp.full((SEQS, 1), LEN - TOK_DEV // 2, jnp.int32)
    starts = jnp.concatenate([jnp.zeros((SEQS, 1), jnp.int32), early, early_edge, late_edge, late], axis=1)
    token_index = jnp.arange(LEN, dtype=jnp.int32)
    begins = jnp.max(jnp.where(starts[:, :, None] <= token_index[None, None, :], starts[:, :, None], 0), axis=1)
    return (token_index[None, :] - begins).astype(jnp.int32)


def draw_up_weight(key, part):
    offset_key = jax.random.fold_in(key, 21)
    entry_key = jax.random.fold_in(key, 22)
    offsets = jnp.clip(jax.random.normal(offset_key, (1, FF), jnp.float32), -3.0, 3.0)
    entries = jnp.clip(jax.random.normal(entry_key, (D, FF), jnp.float32), -4.0, 4.0)
    scale = 1.0 / jnp.sqrt(jnp.float32(D))
    return ((offsets + entries) * scale).astype(jnp.bfloat16)


def block_scale(rng, dims, split, low, largest):
    factor_of = 1.0
    for axis_at, shards_of in split:
        steps = jax.random.uniform(jax.random.fold_in(jax.random.fold_in(rng, 6), axis_at), (shards_of,), jnp.float32, low / len(split), largest / len(split))
        factor_of = factor_of * jnp.repeat(jnp.exp(steps), dims[axis_at] // shards_of).reshape((-1,) + (1,) * (len(dims) - 1 - axis_at))
    return factor_of


def bell_draw(own_key, shape, spread, bound, pieces=(), kind=jnp.bfloat16):
    factor_of = block_scale(own_key, shape, pieces, -0.22, 0.18) if pieces else 1.0
    array = jax.random.normal(own_key, shape, jnp.float32) * spread * factor_of
    return jnp.minimum(jnp.maximum(array, -bound), bound).astype(kind)


def setup_inputs(seed: int = 0) -> dict:
    splits = jax.random.split(jax.random.key(seed), 18)
    return {
        "tokens": bell_draw(splits[0], (SEQS, LEN, D), 1.0, 6.0, ((0, 4), (1, 2), (2, 4))),
        "attn_gain": jnp.clip(1.0 + 0.18 * jax.random.normal(splits[1], (D,), jnp.float32), 0.099609375, 1.8984375).astype(jnp.bfloat16),
        "attn_shift": bell_draw(splits[2], (D,), 0.5, 3.0),
        "qkv_weight": bell_draw(splits[3], (D, 3 * D), D ** -0.5, 0.21875, ((1, 4),)),
        "qkv_bias": bell_draw(splits[4], (3 * D,), 0.5, 3.0, ((0, 4),)),
        "query_map": bell_draw(splits[5], (H, HEAD, HEAD), 0.25, 1.5, ((0, 4),)),
        "key_map": bell_draw(splits[6], (H, HEAD, HEAD), 0.25, 1.5, ((0, 4),)),
        "out_weight": bell_draw(splits[7], (D, D), (D // 4) ** -0.5, 0.4375, ((0, 4),)),
        "out_bias": bell_draw(splits[8], (D,), 0.5, 3.0, ((0, 4),)),
        "mlp_gain": jnp.clip(1.0 + 0.18 * jax.random.normal(splits[9], (D,), jnp.float32), 0.099609375, 1.8984375).astype(jnp.bfloat16),
        "mlp_shift": bell_draw(splits[10], (D,), 0.5, 3.0),
        "up_weight": draw_up_weight(jax.random.fold_in(splits[17], 71), 0),
        "up_bias": bell_draw(splits[12], (FF,), 0.5, 3.0, ((0, 4),)),
        "down_weight": bell_draw(splits[13], (FF, D), (FF // 16) ** -0.5, 0.4375, ((0, 4),)),
        "down_bias": bell_draw(splits[14], (D,), 0.5, 3.0, ((0, 4),)),
        "positions": draw_positions(jax.random.fold_in(splits[17], 71), 0),
        "out_grad": bell_draw(splits[16], (SEQS, LEN, D), 1.0, 6.0, ((0, 4), (1, 2), (2, 4))),
    }


eps = 1e-05
gelu_scale = 0.7978845608028654
highest = lax.Precision.HIGHEST

@jax.custom_vjp
def low(v):
    return lax.optimization_barrier(v.astype(jnp.bfloat16)).astype(jnp.float32)

@jax.custom_vjp
def low_back(v):
    return v

def low_keep(v):
    return (low(v), None)

def low_pass(kept, grad):
    return (grad,)

def back_keep(v):
    return (v, None)

def back_low(kept, grad):
    return (low(grad),)
low.defvjp(low_keep, low_pass)
low_back.defvjp(back_keep, back_low)

def layer_norm(values, gain, shift):
    center = values - lax.optimization_barrier(jnp.mean(values, axis=-1, keepdims=True))
    variance = lax.optimization_barrier(jnp.mean(center * center, axis=-1, keepdims=True))
    return center * lax.rsqrt(variance + eps) * gain + shift

def gelu(values):
    return 0.5 * values * (1.0 + jnp.tanh(gelu_scale * (values + 0.044715 * values * values * values)))

def feature_maps(logits):
    return jnp.concatenate([jax.nn.softmax(logits, axis=-1), jax.nn.softmax(-logits, axis=-1)], axis=-1)

def block_tables(positions):
    seq_count, length = positions.shape
    nblock = length // BLOCK
    token_index = jnp.arange(length, dtype=jnp.int32)
    doc_start = (token_index[None, :] - positions.astype(jnp.int32)).reshape(seq_count, nblock, BLOCK)
    block_index = token_index.reshape(nblock, BLOCK)
    block_first = block_index[:, 0]
    pair_mask = (block_index[None, :, None, :] <= block_index[None, :, :, None]) & (block_index[None, :, None, :] >= doc_start[:, :, :, None])
    included = (doc_start == doc_start[:, :, -1:]).astype(jnp.float32)
    resets = (doc_start[:, :, -1] >= block_first[None, :]).astype(jnp.float32)
    uses_state = (doc_start < block_first[None, :, None]).astype(jnp.float32)
    return (pair_mask, included, resets, uses_state)

def mixer(query_feat, key_feat, value_part, positions):
    seq_count, length = positions.shape
    nblock = length // BLOCK
    pair_mask, included, resets, uses_state = block_tables(positions)
    query_blocks = query_feat.reshape(seq_count, nblock, BLOCK, H, FEAT)
    key_blocks = key_feat.reshape(seq_count, nblock, BLOCK, H, FEAT)
    value_blocks = value_part.reshape(seq_count, nblock, BLOCK, H, HEAD)
    raw_scores = jnp.einsum('bnihf,bnjhf->bnhij', query_blocks, key_blocks, precision=highest)
    scores = jnp.where(pair_mask[:, :, None], low(low_back(raw_scores)), 0.0)
    numer = jnp.einsum('bnhij,bnjhe->bnihe', scores, value_blocks, precision=highest)
    denom = jnp.transpose(lax.optimization_barrier(jnp.sum(scores, axis=-1)), (0, 1, 3, 2))
    block_sums = jnp.einsum('bnj,bnjhf,bnjhe->bnhfe', included, key_blocks, value_blocks, precision=highest)
    block_totals = jnp.einsum('bnj,bnjhf->bnhf', included, key_blocks, precision=highest)

    def advance(carried, scanned):
        state_prev, norm_prev = carried
        sum_item, total_item, reset_item = scanned
        keep_prev = 1.0 - reset_item
        new_state = sum_item + keep_prev[:, None, None, None] * state_prev
        new_norm = total_item + keep_prev[:, None, None] * norm_prev
        return ((new_state, new_norm), (state_prev, norm_prev))
    initial = (jnp.zeros((seq_count, H, FEAT, HEAD), jnp.float32), jnp.zeros((seq_count, H, FEAT), jnp.float32))
    scanned_in = (jnp.moveaxis(block_sums, 1, 0), jnp.moveaxis(block_totals, 1, 0), jnp.moveaxis(resets, 1, 0))
    final_carry, entered = lax.scan(advance, initial, scanned_in)
    states = jnp.moveaxis(entered[0], 0, 1)
    norm_states = jnp.moveaxis(entered[1], 0, 1)
    numer = numer + uses_state[..., None, None] * jnp.einsum('bnihf,bnhfe->bnihe', query_blocks, states, precision=highest)
    denom = denom + uses_state[..., None] * jnp.einsum('bnihf,bnhf->bnih', query_blocks, norm_states, precision=highest)
    numer = low_back(numer)
    return (numer / denom[..., None]).reshape(seq_count, length, H, HEAD)

def forward(tokens, attn_gain, attn_shift, qkv_weight, qkv_bias, query_map, key_map, out_weight, out_bias, mlp_gain, mlp_shift, up_weight, up_bias, down_weight, down_bias, positions):
    seq_count = tokens.shape[0]
    length = tokens.shape[1]
    first_hidden = low(layer_norm(tokens, attn_gain, attn_shift))
    projected = (jnp.dot(first_hidden, qkv_weight, precision=highest) + qkv_bias).reshape(seq_count, length, H, 3, HEAD)
    query_part = low(low_back(projected[..., 0, :]))
    key_part = low(low_back(projected[..., 1, :]))
    value_part = low(low_back(projected[..., 2, :]))
    query_logit = low_back(jnp.einsum('slhe,hef->slhf', query_part, query_map, precision=highest))
    key_logit = low_back(jnp.einsum('slhe,hef->slhf', key_part, key_map, precision=highest))
    query_feat = low(feature_maps(query_logit))
    key_feat = low(feature_maps(key_logit))
    mixture = mixer(query_feat, key_feat, value_part, positions)
    attn_out = low_back(jnp.dot(low(mixture.reshape(seq_count, length, D)), out_weight, precision=highest) + out_bias)
    residual = tokens + attn_out
    second_hidden = low(layer_norm(low(residual), mlp_gain, mlp_shift))
    up_pre = low_back(jnp.dot(second_hidden, up_weight, precision=highest) + up_bias)
    return residual + jnp.dot(low(gelu(up_pre)), down_weight, precision=highest) + down_bias

def reference(tokens, attn_gain, attn_shift, qkv_weight, qkv_bias, query_map, key_map, out_weight, out_bias, mlp_gain, mlp_shift, up_weight, up_bias, down_weight, down_bias, positions, out_grad):
    floats = (tokens, attn_gain, attn_shift, qkv_weight, qkv_bias, query_map, key_map, out_weight, out_bias, mlp_gain, mlp_shift, up_weight, up_bias, down_weight, down_bias)
    floats = tuple((part.astype(jnp.float32) for part in floats))

    def wrapped(*values):
        return forward(*values, positions)
    block_out, pullback = jax.vjp(wrapped, *floats)
    grads = pullback(out_grad.astype(jnp.float32))
    return (block_out.astype(jnp.bfloat16), grads[0].astype(jnp.bfloat16), grads[1], grads[2], grads[3], grads[4], grads[5], grads[6], grads[7], grads[8], grads[9], grads[10], grads[11], grads[12], grads[13], grads[14])
```

```python
import functools

import jax
import jax.numpy as jnp
from jax import lax
from jax.experimental import pallas as pl
from jax.experimental.pallas import tpu as pltpu
from jax.sharding import PartitionSpec as P

eps = 1e-05
gelu_scale = 0.7978845608028654
bf = jnp.bfloat16
f32 = jnp.float32
AUG = 80


def nn(a, b):
    return lax.dot_general(a, b, (((1,), (0,)), ((), ())), preferred_element_type=f32)


def nt(a, b):
    return lax.dot_general(a, b, (((1,), (1,)), ((), ())), preferred_element_type=f32)


def tn(a, b):
    return lax.dot_general(a, b, (((0,), (0,)), ((), ())), preferred_element_type=f32)


def run_kernel(body, name, outs, scalars, *ins, flops=0, trans=0):
    moved = sum(a.size * a.dtype.itemsize for a in ins)
    moved += sum(o.size * jnp.dtype(o.dtype).itemsize for o in outs)
    return pl.pallas_call(
        body,
        out_shape=outs,
        in_specs=[pl.BlockSpec(memory_space=pltpu.SMEM)]
        + [pl.BlockSpec(memory_space=pltpu.VMEM)] * len(ins),
        out_specs=[pl.BlockSpec(memory_space=pltpu.VMEM)] * len(outs),
        compiler_params=pltpu.CompilerParams(vmem_limit_bytes=48 * 2**20),
        cost_estimate=pl.CostEstimate(flops=flops, bytes_accessed=moved, transcendentals=trans),
        name=name,
    )(scalars, *ins)


def half_rows(ref, half, size):
    return ref[pl.ds(pl.multiple_of(half * size, size), size), :]


def norm_columns(values):
    center = values - jnp.mean(values, axis=0, keepdims=True)
    inv_std = lax.rsqrt(jnp.mean(center * center, axis=0, keepdims=True) + eps)
    return center * inv_std, inv_std


def norm_columns_back(grad, normed, inv_std, gain):
    scaled = grad * gain
    return inv_std * (
        scaled
        - jnp.mean(scaled, axis=0, keepdims=True)
        - normed * jnp.mean(scaled * normed, axis=0, keepdims=True)
    )


def gelu_pair(up_pre):
    square = up_pre * up_pre
    tanh_value = jnp.tanh(gelu_scale * (up_pre + 0.044715 * square * up_pre))
    half_one = 0.5 * (1.0 + tanh_value)
    slope = half_one + 0.5 * up_pre * (1.0 - tanh_value * tanh_value) * gelu_scale * (
        1.0 + 3.0 * 0.044715 * square
    )
    return up_pre * half_one, slope


def soft_columns(logits):
    top = jnp.exp(logits - jnp.max(logits, axis=0, keepdims=True))
    return top / jnp.sum(top, axis=0, keepdims=True)


def ahead_mask(starts, rows, first_column, columns):
    j = lax.broadcasted_iota(jnp.int32, (rows, columns), 0)
    i = lax.broadcasted_iota(jnp.int32, (rows, columns), 1) + first_column
    return (j <= i) & (j >= starts[0:1, first_column : first_column + columns])


def first_norm_body(sc, x_ref, col_ref, hid_ref):
    normed, _ = norm_columns(x_ref[...].astype(f32))
    hid_ref[...] = (normed * col_ref[:, 0:1] + col_ref[:, 1:2]).astype(bf)


def turn_body(sc, a_ref, o_ref):
    o_ref[...] = a_ref[...].T


def project_body(hp, hs, sc, hid_ref, wm_ref, wt_ref, bias_ref, maps_ref, starts_ref,
                 proj_ref, qf_ref, kf_ref, va_ref, st_ref):
    s = sc[0]
    half = wm_ref.shape[1]
    proj = nn(wm_ref[...], half_rows(hid_ref, s, half)) + nn(wt_ref[...], half_rows(hid_ref, 1 - s, half))
    proj_ref[...] = (proj + bias_ref[...]).astype(bf)
    tokens = hid_ref.shape[1]
    starts = starts_ref[0:1, :]
    included = (starts == sc[1]).astype(f32)
    for i in range(hp):
        row = 3 * hs * i
        for part, out in ((0, qf_ref), (1, kf_ref)):
            own_map = maps_ref[(part * hp + i) * hs : (part * hp + i + 1) * hs, :]
            logits = tn(own_map, proj_ref[row + part * hs : row + (part + 1) * hs, :])
            out[i, 0:hs, :] = soft_columns(logits).astype(bf)
            out[i, hs : 2 * hs, :] = soft_columns(-logits).astype(bf)
        va_ref[i, 0:hs, :] = proj_ref[row + 2 * hs : row + 3 * hs, :]
        extra = lax.broadcasted_iota(jnp.int32, (AUG - hs, tokens), 0)
        va_ref[i, hs:AUG, :] = jnp.where(extra < 2, 1.0, 0.0).astype(bf)
        kept = (va_ref[i].astype(f32) * included).astype(bf)
        st_ref[i] = nt(kept, kf_ref[i]).astype(bf)


def causal_pieces(tokens):
    step = tokens // 2
    return ((0, step, step), (step, step, tokens))


def local_mix_body(hp, sc, qf_ref, kf_ref, va_ref, starts_ref, num_ref):
    tokens = qf_ref.shape[2]
    starts = starts_ref[...]
    for first, width, rows in causal_pieces(tokens):
        mask = ahead_mask(starts, rows, first, width)
        for i in range(hp):
            scores = tn(kf_ref[i, :, 0:rows], qf_ref[i, :, first : first + width])
            scores = jnp.where(mask, scores, 0.0).astype(bf)
            num_ref[i, :, first : first + width] = nn(va_ref[i, :, 0:rows], scores)


def weighted_states(sc, slots, own, refs, last, hp, piece, i):
    total = jnp.where(sc[last] > 0, refs[-1][piece * hp + i].astype(f32), 0.0)
    for m, (slot, ref) in enumerate(zip(slots, refs[:-1]), 1):
        total += jnp.where(sc[slot] > 0, ref[(piece ^ m) * hp + i].astype(f32), 0.0)
    return total.astype(bf)


def mix_out_body(hp, hs, nh, sc, *refs):
    num_refs, qf_refs, state_refs = refs[0:nh], refs[nh : 2 * nh], refs[2 * nh : 3 * nh]
    wm_refs, wt_refs = refs[3 * nh : 4 * nh], refs[4 * nh : 5 * nh]
    starts_ref, x_ref, col_ref, sin_ref, mixd_ref, mix_ref, res_ref, hidt_ref, hid_ref = refs[5 * nh :]
    s = sc[0]
    uses = starts_ref[0:1, :] < 0
    rows = hp * hs
    for j in range(nh):
        for i in range(hp):
            state = weighted_states(sc, range(2, 1 + nh), None, state_refs, 1 + nh, hp, j, i)
            sin_ref[j * hp + i] = state
            num = num_refs[j][i] + jnp.where(uses, nn(state, qf_refs[j][i]), 0.0)
            denom = num[hs : hs + 1, :]
            mixture = num[0:hs, :] / denom
            mixd_ref[j * hp + i, 0:hs, :] = mixture
            mixd_ref[j * hp + i, hs : hs + 8, :] = num[hs : hs + 8, :]
            mix_ref[j * rows + i * hs : j * rows + (i + 1) * hs, :] = mixture.astype(bf)
    half = wm_refs[0].shape[1]
    for which, w_refs in ((s, wm_refs), (1 - s, wt_refs)):
        out = tn(w_refs[0][...], mix_ref[0:rows, :])
        for j in range(1, nh):
            out += tn(w_refs[j][...], mix_ref[j * rows : (j + 1) * rows, :])
        at = pl.ds(pl.multiple_of(which * half, half), half)
        res_ref[at, :] = x_ref[at, :].astype(f32) + out + col_ref[at, 4:5]
    normed, _ = norm_columns(res_ref[...].astype(bf).astype(f32))
    hidden = (normed * col_ref[:, 2:3] + col_ref[:, 3:4]).astype(bf)
    hidt_ref[...] = hidden
    hid_ref[...] = hidden.T


def feed_body(first, sc, hid_ref, gy_ref, bm_ref, bt_ref, bias_ref, *refs):
    if first:
        out_ref, sg_ref = refs[0:2]
        rest = refs[2:]
    else:
        out_in, sg_in, out_ref, sg_ref = refs[0:4]
        rest = refs[4:]
    ub_ref = rest[-1]
    s = sc[0]
    half = bm_ref.shape[1] // 2
    out_total, sg_total = None, None
    for b, (which, blk) in enumerate(((s, bm_ref), (1 - s, bt_ref))):
        act_ref, ug_ref = rest[2 * b], rest[2 * b + 1]
        at = pl.ds(pl.multiple_of(which * half, half), half)
        up_pre = nn(hid_ref[...], blk[:, 0:half]) + bias_ref[0:1, at]
        value, slope = gelu_pair(up_pre)
        act_ref[...] = value.astype(bf)
        back = nt(gy_ref[:, 0:half], blk[0:half, half:]) + nt(gy_ref[:, half:], blk[half:, half:])
        up_grad = (back * slope).astype(bf)
        ug_ref[...] = up_grad
        ub_ref[0:8, at] = jnp.broadcast_to(jnp.sum(up_grad.astype(f32), axis=0, keepdims=True), (8, half))
        if b == 0 and first:
            out_ref[:, 0:half] = nn(act_ref[...], blk[0:half, half:])
            out_ref[:, half:] = nn(act_ref[...], blk[half:, half:])
            sg_ref[...] = nt(blk[:, 0:half], ug_ref[...])
        else:
            left, grad = (out_in, sg_in) if b == 0 else (out_ref, sg_ref)
            out_ref[:, 0:half] = left[:, 0:half] + nn(act_ref[...], blk[0:half, half:])
            out_ref[:, half:] = left[:, half:] + nn(act_ref[...], blk[half:, half:])
            sg_ref[...] = grad[...] + nt(blk[:, 0:half], ug_ref[...])


def block_out_body(sc, res_ref, out_ref, col_ref, o_ref):
    o_ref[...] = (res_ref[...] + out_ref[...].T + col_ref[:, 5:6]).astype(bf)


def sums_across(values):
    lane = lax.broadcasted_iota(jnp.int32, (values[0].shape[0], 128), 1)
    total = jnp.zeros((values[0].shape[0], 128), f32)
    for at, value in enumerate(values):
        total = jnp.where(lane == at, jnp.sum(value, axis=1, keepdims=True), total)
    return total


def second_back_body(hp, hs, nh, sc, *refs):
    sg_ref, res_ref, gyt_ref, col_ref, mixd_ref, starts_ref = refs[0:6]
    wm_refs, wt_refs, qf_refs = refs[6 : 6 + nh], refs[6 + nh : 6 + 2 * nh], refs[6 + 2 * nh : 6 + 3 * nh]
    rg_ref, ag_ref, vec_ref, na_ref, sgt_ref = refs[6 + 3 * nh :]
    s = sc[0]
    normed, inv_std = norm_columns(res_ref[...].astype(bf).astype(f32))
    sg = sg_ref[...]
    gy = gyt_ref[...].astype(f32)
    res_grad = gy + norm_columns_back(sg, normed, inv_std, col_ref[:, 2:3])
    rg_ref[...] = res_grad
    ag_ref[...] = res_grad.astype(bf)
    vec_ref[...] = sums_across((sg * normed, sg, ag_ref[...].astype(f32), gy))
    half = wm_refs[0].shape[1]
    tokens = sg_ref.shape[1]
    uses = (starts_ref[0:1, :] < 0).astype(f32)
    for j in range(nh):
        mg = nn(wm_refs[j][...], half_rows(ag_ref, s, half)) + nn(wt_refs[j][...], half_rows(ag_ref, 1 - s, half))
        for i in range(hp):
            own = mg[i * hs : (i + 1) * hs, :]
            num = own / mixd_ref[j * hp + i, hs : hs + 1, :]
            den = -jnp.sum(num * mixd_ref[j * hp + i, 0:hs, :], axis=0, keepdims=True)
            high = den.astype(bf).astype(f32)
            extra = lax.broadcasted_iota(jnp.int32, (AUG - hs, tokens), 0)
            extra = jnp.where(extra == 0, high, jnp.where(extra == 1, den - high, 0.0))
            na_ref[j * hp + i, 0:hs, :] = num.astype(bf)
            na_ref[j * hp + i, hs:AUG, :] = extra.astype(bf)
            kept = (na_ref[j * hp + i].astype(f32) * uses).astype(bf)
            grad = nt(kept, qf_refs[j][i])
            sgt_ref[j * hp + i] = grad.astype(bf)


def join_extra(state, hs):
    row = lax.broadcasted_iota(jnp.int32, state.shape, 0)
    both = state[hs : hs + 1, :] + state[hs + 1 : hs + 2, :]
    return jnp.where(row < hs, state, jnp.where(row == hs, both, 0.0))


def halves_back(feat, grad, hs):
    parts = []
    for k in range(2):
        soft = feat[k * hs : (k + 1) * hs, :].astype(f32)
        own = grad[k * hs : (k + 1) * hs, :]
        weight = jnp.sum(soft * own, axis=0, keepdims=True) / jnp.sum(soft, axis=0, keepdims=True)
        parts.append(soft * (own - weight))
    return (parts[0] - parts[1]).astype(bf)


def local_back_body(hp, hs, j, sc, qf_ref, kf_ref, va_ref, na_ref, sin_ref, starts_ref, ql_ref, kfg_ref, vg_ref):
    tokens = qf_ref.shape[2]
    starts = starts_ref[...]
    step = tokens // 2
    uses = starts[0:1, :] < 0
    masks = [ahead_mask(starts, rows, first, width) for first, width, rows in causal_pieces(tokens)]
    for i in range(hp):
        na = na_ref[j * hp + i]
        state = sin_ref[j * hp + i]
        through = tn(state, na)
        for which, (first, width, rows) in enumerate(causal_pieces(tokens)):
            at = slice(first, first + width)
            mask = masks[which]
            scores = jnp.where(mask, tn(kf_ref[i, :, 0:rows], qf_ref[i, :, at]), 0.0).astype(bf)
            sgrad = jnp.where(mask, tn(va_ref[i, :, 0:rows], na[:, at]), 0.0).astype(bf)
            qfg = nn(kf_ref[i, :, 0:rows], sgrad) + jnp.where(uses[:, at], through[:, at], 0.0)
            ql_ref[i, :, at] = halves_back(qf_ref[i, :, at], qfg, hs)
            kfg = nt(qf_ref[i, :, at], sgrad)
            vg = nt(na[:, at], scores)[0:hs, :]
            if which == 0:
                kfg_ref[i, :, 0:rows] = kfg
                vg_ref[i, :, 0:rows] = vg
            else:
                kfg_ref[i, :, 0:step] += kfg[:, 0:step]
                vg_ref[i, :, 0:step] += vg[:, 0:step]
                kfg_ref[i, :, step:] = kfg[:, step:]
                vg_ref[i, :, step:] = vg[:, step:]


def project_back_body(hp, hs, nh, j, first, sc, *refs):
    state_refs = refs[0:nh]
    kf_ref, va_ref, ql_ref, kfg_ref, vg_ref, proj_ref, maps_ref, wm_ref, wt_ref, starts_ref = refs[nh : nh + 10]
    rest = refs[nh + 10 :]
    if first:
        pg_ref, fg_ref, mg_ref, pb_ref = rest
    else:
        fg_in, pg_ref, fg_ref, mg_ref, pb_ref = rest
    s = sc[0]
    included = starts_ref[0:1, :] == sc[1]
    for i in range(hp):
        state = weighted_states(sc, range(2 + nh, 1 + 2 * nh), None, state_refs, 1 + 2 * nh, hp, j, i)
        state = join_extra(state.astype(f32), hs).astype(bf)
        kfg = kfg_ref[i] + jnp.where(included, tn(state, va_ref[i]), 0.0)
        vg = vg_ref[i] + jnp.where(included, nn(state, kf_ref[i])[0:hs, :], 0.0)
        klg = halves_back(kf_ref[i], kfg, hs)
        qlg = ql_ref[i]
        row = 3 * hs * i
        q_map = maps_ref[i * hs : (i + 1) * hs, :]
        k_map = maps_ref[(hp + i) * hs : (hp + i + 1) * hs, :]
        pg_ref[row : row + hs, :] = nn(q_map, qlg).astype(bf)
        pg_ref[row + hs : row + 2 * hs, :] = nn(k_map, klg).astype(bf)
        pg_ref[row + 2 * hs : row + 3 * hs, :] = vg.astype(bf)
        mg_ref[i * hs : (i + 1) * hs, :] = nt(proj_ref[row : row + hs, :], qlg)
        mg_ref[(hp + i) * hs : (hp + i + 1) * hs, :] = nt(proj_ref[row + hs : row + 2 * hs, :], klg)
    pb_ref[...] = sums_across((pg_ref[...].astype(f32),))
    half = wm_ref.shape[1]
    for which, w_ref in ((s, wm_ref), (1 - s, wt_ref)):
        at = pl.ds(pl.multiple_of(which * half, half), half)
        grad = tn(w_ref[...], pg_ref[...])
        fg_ref[at, :] = grad if first else fg_in[at, :] + grad


def first_back_body(sc, fg_ref, x_ref, rg_ref, col_ref, tg_ref, vec_ref):
    normed, inv_std = norm_columns(x_ref[...].astype(f32))
    fg = fg_ref[...]
    tg_ref[...] = (rg_ref[...] + norm_columns_back(fg, normed, inv_std, col_ref[:, 0:1])).astype(bf)
    vec_ref[...] = sums_across((fg * normed, fg))


def feed_grads_body(sc, hidt_ref, gyt_ref, ug_ref, act_ref, hidt2_ref, gyt2_ref, ug2_ref, act2_ref, o_ref):
    half = o_ref.shape[1] // 2
    o_ref[:, 0:half] = (nn(hidt_ref[...], ug_ref[...]) + nn(hidt2_ref[...], ug2_ref[...])).astype(bf)
    o_ref[:, half:] = (nn(gyt_ref[...], act_ref[...]) + nn(gyt2_ref[...], act2_ref[...])).astype(bf)


def rows_grads_body(sc, a_ref, b_ref, a2_ref, b2_ref, o_ref):
    half = b2_ref.shape[0]
    o_ref[...] = (nt(a_ref[...], half_rows(b_ref, sc[0], half)) + nt(a2_ref[...], b2_ref[...])).astype(bf)


def shape(dims, dtype):
    return jax.ShapeDtypeStruct(tuple(dims), dtype)


def swap(a, axis, k):
    n = lax.axis_size(axis)
    return lax.ppermute(a, axis, [(i, i ^ k) for i in range(n)])


def pieces_to_owners(a, axis):
    return lax.all_to_all(a, axis, 0, 0, tiled=True)


def chain_seq(part, forward, weight_of):
    n = lax.axis_size("seq")
    total = None
    for k in range(1, n):
        pairs = [(i, i + k) if forward else (i + k, i) for i in range(n - k)]
        sent = part if forward else part * weight_of(k).astype(part.dtype)
        got = lax.ppermute(sent, "seq", pairs)
        if n == 2:
            return got
        got = got.astype(f32) * (weight_of(k) if forward else 1.0)
        total = got if total is None else total + got
    return total.astype(bf)


def local(tokens, attn_gain, attn_shift, qkv_weight, qkv_bias, query_map, key_map, out_weight, out_bias,
          mlp_gain, mlp_shift, up_weight, up_bias, down_weight, down_bias, positions, out_grad):
    nh, ns, nz = lax.axis_size("head"), lax.axis_size("seq"), lax.axis_size("dp")
    length, width = tokens.shape[1], tokens.shape[2]
    model = width * nh
    half = model // 2
    hp, hs = query_map.shape[0], query_map.shape[1]
    heads = hp * nh
    pc = qkv_weight.shape[1]
    hidden = up_weight.shape[1]
    tok = length // nh
    h = lax.axis_index("head")
    s2 = lax.axis_index("seq") % 2
    peers = range(1, nh)

    def mine(a, axis):
        return lax.dynamic_slice_in_dim(a, s2 * (a.shape[axis] // 2), a.shape[axis] // 2, axis)

    def theirs(a, axis):
        return lax.dynamic_slice_in_dim(a, (1 - s2) * (a.shape[axis] // 2), a.shape[axis] // 2, axis)

    def to_chunks(a):
        a = a[0].T.reshape(width, nh, tok).transpose(1, 0, 2)
        return pieces_to_owners(a, "head").reshape(model, tok)

    x = to_chunks(tokens)
    small = jnp.concatenate(
        [query_map.reshape(-1, hs), key_map.reshape(-1, hs)]
        + [jnp.concatenate([qkv_bias, up_bias, out_bias, down_bias]).reshape(-1, hs)]
    )
    small = jnp.pad(small, ((0, -small.shape[0] % 16), (0, 0)))
    smalls = [small] + [swap(small, "head", m) for m in peers]

    qkv_t = qkv_weight.T
    qkv_m, qkv_o = [mine(qkv_t, 1)], [theirs(qkv_t, 1)]
    for m in peers:
        qkv_m.append(swap(qkv_m[0], "head", m))
        qkv_o.append(swap(qkv_m[m], "seq", 1))
    out_m, out_o = [mine(out_weight, 1)], [theirs(out_weight, 1)]
    blocks = []
    for pick in (mine, theirs):
        down = pick(down_weight, 0)
        blocks.append(
            jnp.concatenate([pick(up_weight, 1), jnp.concatenate([down[:, :half], down[:, half:]], axis=0)], axis=1)
        )
    tied, out_first, qkv_m[nh - 1] = lax.optimization_barrier((blocks[0], out_m[0], qkv_m[nh - 1]))
    for m in peers:
        out_m.append(swap(out_first, "head", m))
        out_o.append(swap(out_m[m], "seq", 1))
    blk_m, blk_o = [blocks[0]], [blocks[1]]
    for m in peers:
        blk_m.append(swap(tied, "head", m))
        blk_o.append(swap(blk_m[m], "seq", 1))
    gyt = to_chunks(out_grad)

    maps = [a[: 2 * hp * hs] for a in smalls]
    flat = [a[2 * hp * hs :].reshape(-1) for a in smalls]
    qkv_cols = [a[:pc].astype(f32)[:, None] for a in flat]
    up_rows = [a[pc : pc + hidden].astype(f32)[None, :] for a in flat]
    order = h ^ jnp.arange(nh)
    tail = jnp.stack([a[pc + hidden : pc + hidden + 2 * width] for a in flat])[order]
    cols = jnp.stack(
        [attn_gain, attn_shift, mlp_gain, mlp_shift, tail[:, :width].reshape(-1), tail[:, width:].reshape(-1)]
        + [jnp.zeros_like(attn_gain)] * 2,
        axis=1,
    ).astype(f32)

    run = positions[0]
    start_of = jnp.arange(length, dtype=jnp.int32) - run
    chunk_starts = lax.dynamic_slice_in_dim(start_of, h * tok, tok, 0) - h * tok
    starts = jnp.broadcast_to(chunk_starts[None, :], (8, tok))
    firsts = start_of[::tok]
    run_last = start_of[length - 1]
    other = [h ^ m for m in range(nh)]
    fwd = [(other[m] < h) & (firsts[h] <= (other[m] + 1) * tok - 1) for m in peers]
    bwd = [(other[m] > h) & (firsts[other[m]] <= (h + 1) * tok - 1) for m in peers]
    sc = jnp.stack(
        [s2, chunk_starts[tok - 1]]
        + [a.astype(jnp.int32) for a in fwd]
        + [(firsts[h] < 0).astype(jnp.int32)]
        + [a.astype(jnp.int32) for a in bwd]
        + [(run_last <= (h + 1) * tok - 1).astype(jnp.int32)]
    ).astype(jnp.int32)

    (hid,) = run_kernel(first_norm_body, "first_norm", [shape((model, tok), bf)], sc, x, cols, flops=model * tok * 10)
    hid_peer = swap(theirs(hid, 0), "seq", 1)
    proj, qf, kf, va, st = [], [], [], [], []
    for j in range(nh):
        outs = run_kernel(
            functools.partial(project_body, hp, hs),
            f"project_{j}",
            [shape((pc, tok), bf), shape((hp, 2 * hs, tok), bf), shape((hp, 2 * hs, tok), bf),
             shape((hp, AUG, tok), bf), shape((hp, AUG, 2 * hs), bf)],
            sc, hid, qkv_m[j], qkv_o[j], qkv_cols[j], maps[j], starts,
            flops=2 * model * pc * tok + 4 * pc * hs * tok, trans=4 * hp * hs * tok,
        )
        for to, a in zip((proj, qf, kf, va, st), outs):
            to.append(a)
    states = jnp.concatenate(st)
    around = [states] + [swap(states, "head", m) for m in peers]

    def by_own_pieces(a, m):
        a = a.reshape(nh, hp, AUG, 2 * hs)
        return jnp.stack([a[j ^ m] for j in range(nh)]).reshape(heads, AUG, 2 * hs)

    ends_in = [((run_last <= (other[m] + 1) * tok - 1)).astype(f32) for m in range(nh)]
    whole = sum(by_own_pieces(a, m).astype(f32) * ends_in[m] for m, a in enumerate(around)).astype(bf)
    before = chain_seq(whole, True, lambda k: (start_of[0] <= -(k - 1) * length - 1).astype(f32))

    nums = []
    pair_flops = 2 * hp * tok * tok * 3 // 4
    for j in range(nh):
        (num,) = run_kernel(
            functools.partial(local_mix_body, hp), f"local_mix_{j}", [shape((hp, AUG, tok), f32)],
            sc, qf[j], kf[j], va[j], starts, flops=pair_flops * (2 * hs + AUG),
        )
        nums.append(num)
    sin, mixd, mix, res, hidt2, hid2 = run_kernel(
        functools.partial(mix_out_body, hp, hs, nh),
        "mix_out",
        [shape((heads, AUG, 2 * hs), bf), shape((heads, hs + 8, tok), f32), shape((model, tok), bf),
         shape((model, tok), f32), shape((model, tok), bf), shape((tok, model), bf)],
        sc, *nums, *qf, *around[1:], before, *out_m, *out_o, starts, x, cols,
        flops=2 * model * model * tok + 2 * heads * AUG * 2 * hs * tok,
    )
    (gy,) = run_kernel(turn_body, "turn_grad", [shape((tok, model), bf)], sc, gyt)
    act_m, ug_m, act_o, ug_o, ubs = [], [], [], [], []
    sums = ()
    for j in range(nh):
        outs = run_kernel(
            functools.partial(feed_body, j == 0),
            f"feed_{j}",
            [shape((tok, model), f32), shape((model, tok), f32)] + [shape((tok, hidden // 2), bf)] * 4
            + [shape((8, hidden), f32)],
            sc, hid2, gy, blk_m[j], blk_o[j], up_rows[j], *sums,
            flops=8 * model * hidden * tok, trans=hidden * tok,
        )
        sums = tuple(outs[:2])
        for to, a in zip((act_m, ug_m, act_o, ug_o, ubs), outs[2:]):
            to.append(a)
    mlp_out, sg = sums
    (bo,) = run_kernel(block_out_body, "block_out", [shape((model, tok), bf)], sc, res, mlp_out, cols)

    def to_runs(a):
        a = pieces_to_owners(a.reshape(nh, width, tok), "head")
        return a.transpose(1, 0, 2).reshape(width, length).T[None]

    rg, ag, vec2, na, sgt = run_kernel(
        functools.partial(second_back_body, hp, hs, nh),
        "second_back",
        [shape((model, tok), f32), shape((model, tok), bf), shape((model, 128), f32),
         shape((heads, AUG, tok), bf), shape((heads, AUG, 2 * hs), bf)],
        sc, sg, res, gyt, cols, mixd, starts, *out_m, *out_o, *qf,
        flops=2 * model * model * tok + 2 * heads * AUG * 2 * hs * tok,
    )
    g_around = [sgt] + [swap(sgt, "head", m) for m in peers]
    begins_in = [(firsts[other[m]] < 0).astype(f32) for m in range(nh)]
    g_whole = sum(by_own_pieces(a, m).astype(f32) * begins_in[m] for m, a in enumerate(g_around)).astype(bf)
    after = chain_seq(g_whole, False, lambda k: (start_of[0] <= -(k - 1) * length - 1).astype(f32))

    local_back = []
    for j in range(nh):
        local_back.append(
            run_kernel(
                functools.partial(local_back_body, hp, hs, j), f"local_back_{j}",
                [shape((hp, hs, tok), bf), shape((hp, 2 * hs, tok), f32), shape((hp, hs, tok), f32)],
                sc, qf[j], kf[j], va[j], na, sin, starts, flops=pair_flops * (6 * hs + 3 * AUG),
            )
        )
    fg = None
    pg, map_grads, pbs = [None] * nh, [None] * nh, [None] * nh
    for j in [*range(nh - 1, 0, -1), 0]:
        pg[j], fg, map_grads[j], pbs[j] = run_kernel(
            functools.partial(project_back_body, hp, hs, nh, j, fg is None),
            f"project_back_{j}",
            [shape((pc, tok), bf), shape((model, tok), f32), shape((2 * hp * hs, hs), f32), shape((pc, 128), f32)],
            sc, *g_around[1:], after, kf[j], va[j], *local_back[j], proj[j], maps[j], qkv_m[j], qkv_o[j], starts,
            *(() if fg is None else (fg,)),
            flops=2 * model * pc * tok + 12 * pc * hs * tok,
        )
    tg, vec1 = run_kernel(
        first_back_body, "first_back", [shape((model, tok), bf), shape((model, 128), f32)], sc, fg, x, rg, cols
    )
    tokens_grad = to_runs(tg)
    block_out = to_runs(bo)

    def over_head(parts):
        total = parts[0].astype(f32)
        for m in peers:
            total += swap(parts[m], "head", m).astype(f32)
        for k in range(1, ns // 2):
            n = ns
            total += lax.ppermute(total, "seq", [(i, (i + 2 * k) % n) for i in range(n)])
        return total.astype(bf)

    def over_dp(a):
        rows = a.shape[0] // nz
        got = pieces_to_owners(a.reshape(nz, rows, -1), "dp")
        total = got.astype(f32).sum(0).astype(bf)
        return pieces_to_owners(jnp.broadcast_to(total[None], (nz,) + total.shape), "dp").reshape(a.shape)

    hidt2_peer, gyt_peer = swap(hidt2, "seq", 1), swap(gyt, "seq", 1)
    feed_parts = []
    for j in range(nh):
        (part,) = run_kernel(
            feed_grads_body, f"feed_grads_{j}", [shape((model, hidden), bf)], sc,
            hidt2, gyt, ug_m[j], act_m[j], hidt2_peer, gyt_peer, swap(ug_o[j], "seq", 1), swap(act_o[j], "seq", 1),
            flops=4 * model * hidden * tok,
        )
        feed_parts.append(part)
    mix_peer, ag_peer = swap(mix, "seq", 1), swap(theirs(ag, 0), "seq", 1)
    rows = hp * hs
    out_parts, qkv_parts = [], [None] * nh
    for j in range(nh):
        (part,) = run_kernel(
            rows_grads_body, f"out_grads_{j}", [shape((rows, half), bf)], sc,
            mix[j * rows : (j + 1) * rows], ag, mix_peer[j * rows : (j + 1) * rows], ag_peer,
            flops=2 * model * rows * tok,
        )
        out_parts.append(part)
    for j in [*range(nh - 1, 0, -1), 0]:
        (qkv_parts[j],) = run_kernel(
            rows_grads_body, f"qkv_grads_{j}", [shape((pc, half), bf)], sc, pg[j], hid, swap(pg[j], "seq", 1), hid_peer,
            flops=2 * model * pc * tok,
        )

    def both_halves(a, axis):
        other_half = swap(a, "seq", 1)
        return jnp.where(
            s2 == 0,
            jnp.concatenate([a, other_half], axis=axis),
            jnp.concatenate([other_half, a], axis=axis),
        ).astype(f32)

    feed_sum = over_dp(over_head(feed_parts))
    out_sum = over_dp(over_head(out_parts))
    qkv_sum = over_dp(over_head(qkv_parts))
    upweight_grad = both_halves(feed_sum[:, : hidden // 2], 1)
    downweight_grad = both_halves(feed_sum[:, hidden // 2 :], 1).T
    outweight_grad = both_halves(out_sum, 1)
    qkvweight_grad = both_halves(qkv_sum, 1).T

    vectors = jnp.concatenate([vec1[:, 0:2], vec2[:, 0:4]], axis=1).T
    vectors = vectors.reshape(6, nh, width).transpose(1, 0, 2).reshape(nh, -1)
    vectors = vectors[order]
    packs = []
    for j in range(nh):
        one = jnp.concatenate([map_grads[j].reshape(-1), pbs[j][:, 0], ubs[j][0], vectors[j]])
        packs.append(jnp.pad(one, (0, -one.shape[0] % 1024)).reshape(-1, 128))
    total = packs[0]
    for m in peers:
        total += swap(packs[m], "head", m)
    for k in range(1, ns):
        total_k = lax.ppermute(total, "seq", [(i, i ^ 1) for i in range(ns)]) if k == 1 else None
        if k == 1:
            total = total + total_k
    base = total
    for k in range(1, ns // 2):
        total = total + lax.ppermute(base, "seq", [(i, (i + 2 * k) % ns) for i in range(ns)])
    base = total
    for k in range(1, nz):
        total = total + lax.ppermute(base, "dp", [(i, (i + k) % nz) for i in range(nz)])
    total = total.reshape(-1)
    nm = hp * hs * hs
    query_grad = total[:nm].reshape(hp, hs, hs)
    key_grad = total[nm : 2 * nm].reshape(hp, hs, hs)
    at = 2 * nm
    qkvbias_grad = total[at : at + pc]
    upbias_grad = total[at + pc : at + pc + hidden]
    vec = total[at + pc + hidden : at + pc + hidden + 6 * width].reshape(6, width)
    return (block_out, tokens_grad, vec[0], vec[1], qkvweight_grad, qkvbias_grad, query_grad, key_grad,
            outweight_grad, vec[4], vec[2], vec[3], upweight_grad, upbias_grad, downweight_grad, vec[5])


def solution(mesh):
    wide = P("dp", "seq", "head")
    return jax.shard_map(
        local,
        mesh=mesh,
        in_specs=(wide, P(), P(), P(None, "head"), P("head"), P("head", None, None), P("head", None, None),
                  P("head", None), P("head"), P(), P(), P(None, "head"), P("head"), P("head", None), P("head"),
                  P("dp", "seq"), wide),
        out_specs=(wide, wide, P("head"), P("head"), P(None, "head"), P("head"), P("head", None, None),
                   P("head", None, None), P("head", None), P("head"), P("head"), P("head"), P(None, "head"), P("head"),
                   P("head", None), P("head")),
        check_vma=False,
    )
```

```python
import functools

import jax
import jax.numpy as jnp
from jax import lax
from jax.experimental import pallas as pl
from jax.experimental.pallas import tpu as pltpu
from jax.sharding import PartitionSpec as P

eps = 1e-05
gelu_scale = 0.7978845608028654
bf = jnp.bfloat16
f32 = jnp.float32
AUG = 80
TILE = 16


def nn(a, b):
    return lax.dot_general(a, b, (((1,), (0,)), ((), ())), preferred_element_type=f32)


def nt(a, b):
    return lax.dot_general(a, b, (((1,), (1,)), ((), ())), preferred_element_type=f32)


def tn(a, b):
    return lax.dot_general(a, b, (((0,), (0,)), ((), ())), preferred_element_type=f32)


def shape(dims, dtype):
    return jax.ShapeDtypeStruct(tuple(dims), dtype)


def whole(a):
    dims = tuple(a.shape)
    return pl.BlockSpec(dims, lambda *_: (0,) * len(dims))


def lead(count, *dims):
    return pl.BlockSpec((count,) + dims, lambda p, sc: (p,) + (0,) * len(dims))


def run_kernel(body, name, grid, scalars, ins, outs, flops=0, trans=0, scratch=()):
    moved = sum(a.size * jnp.dtype(a.dtype).itemsize for a, _ in ins + outs)
    return pl.pallas_call(
        body,
        out_shape=[o for o, _ in outs],
        grid_spec=pltpu.PrefetchScalarGridSpec(
            num_scalar_prefetch=1,
            grid=grid,
            in_specs=[spec or whole(a) for a, spec in ins],
            out_specs=[spec or whole(o) for o, spec in outs],
            scratch_shapes=list(scratch),
        ),
        compiler_params=pltpu.CompilerParams(vmem_limit_bytes=50 * 2**20),
        cost_estimate=pl.CostEstimate(flops=flops, bytes_accessed=moved, transcendentals=trans),
        name=name,
    )(scalars, *[a for a, _ in ins])


def norm_columns(values):
    center = values - jnp.mean(values, axis=0, keepdims=True)
    inv_std = lax.rsqrt(jnp.mean(center * center, axis=0, keepdims=True) + eps)
    return center * inv_std, inv_std


def norm_columns_back(grad, normed, inv_std, gain):
    scaled = grad * gain
    return inv_std * (
        scaled
        - jnp.mean(scaled, axis=0, keepdims=True)
        - normed * jnp.mean(scaled * normed, axis=0, keepdims=True)
    )


def column(rows, at, width):
    only = jnp.where(lax.broadcasted_iota(jnp.int32, rows.shape, 0) == at, rows.astype(f32), 0.0).astype(bf)
    upright = tn(only, jnp.ones((TILE, 128), bf))
    return jnp.concatenate([upright] * (width // 128), axis=1)


def row_sums(values):
    ones = jnp.ones((8, values.shape[1]), bf)
    if values.dtype == bf:
        return nt(ones, values)
    high = values.astype(bf)
    return nt(ones, high) + nt(ones, (values - high.astype(f32)).astype(bf))


def gelu_pair(up_pre):
    square = up_pre * up_pre
    tanh_value = jnp.tanh(gelu_scale * (up_pre + 0.044715 * square * up_pre))
    half_one = 0.5 * (1.0 + tanh_value)
    slope = half_one + 0.5 * up_pre * (1.0 - tanh_value * tanh_value) * gelu_scale * (
        1.0 + 3.0 * 0.044715 * square
    )
    return up_pre * half_one, slope


def soft_columns(logits):
    top = jnp.exp(logits - jnp.max(logits, axis=0, keepdims=True))
    return top / jnp.sum(top, axis=0, keepdims=True)


def ahead_mask(starts, rows, first_column, columns):
    j = lax.broadcasted_iota(jnp.int32, (rows, columns), 0)
    i = lax.broadcasted_iota(jnp.int32, (rows, columns), 1) + first_column
    return (j <= i) & (j >= starts[0:1, first_column : first_column + columns])


def causal_pieces(tokens):
    step = tokens // 2
    return ((0, step, step), (step, step, tokens))


HBM = pl.BlockSpec(memory_space=pl.ANY)


def load_all(refs, places, sems):
    copies = [pltpu.make_async_copy(ref, place, sems.at[k]) for k, (ref, place) in enumerate(zip(refs, places))]
    for copy in copies:
        copy.start()
    return copies


def part_places(refs, scratch, core):
    return [scratch.at[2 * (k // 2) + (core if k % 2 == 0 else 1 - core)] for k in range(len(refs))]


def pack_body(sc, qkv_ref, qm_ref, km_ref, rows_ref, out_ref, up_ref, down_ref, *outs):
    pc, model = qkv_ref.shape
    hs = qm_ref.shape[1]
    for core, (first_ref, wo_ref, wd_ref, wu_ref) in ((sc[0], outs[0:4]), (1 - sc[0], outs[4:8])):
        cut = pc // 2
        first_ref[0:cut, :] = qkv_ref[pl.ds(pl.multiple_of(core * cut, TILE), cut), :]
        first_ref[cut : cut + hs // 2, :] = jnp.zeros((hs // 2, model), bf)
        for i in range(qm_ref.shape[0] // hs):
            for k in range(2):
                rows = slice(i * hs + k * hs // 2, i * hs + (k + 1) * hs // 2)
                at = k * (model // 2) + 128 * i
                own = jnp.where(core == 0, qm_ref[rows, :].astype(f32), km_ref[rows, :].astype(f32))
                first_ref[cut : cut + hs // 2, at : at + hs] = own.astype(bf)
        first_ref[cut + hs // 2 :, :] = rows_ref[...]
        cut = out_ref.shape[0] // 2
        wo_ref[...] = out_ref[pl.ds(pl.multiple_of(core * cut, TILE), cut), :]
        half = down_ref.shape[0] // 2
        wd_ref[...] = down_ref[pl.ds(pl.multiple_of(core * half, TILE), half), :]
        at = pl.ds(pl.multiple_of(core * half, 128), half)
        wu_ref[:, 0 : model // 2] = up_ref[0 : model // 2, at]
        wu_ref[:, model // 2 :] = up_ref[model // 2 :, at]


def first_norm_body(sc, x_ref, gain_ref, hid_ref):
    normed, _ = norm_columns(x_ref[...].astype(f32))
    width = x_ref.shape[1]
    gains = gain_ref[...]
    hid_ref[...] = (normed * column(gains, 0, width) + column(gains, 1, width)).astype(bf)


def turn_body(sc, a_ref, o_ref):
    o_ref[...] = a_ref[...].T


def map_of(first_ref, at, i, hs, cut):
    model = first_ref.shape[2]
    rows = slice(cut, cut + hs // 2)
    return jnp.concatenate(
        [first_ref[at, rows, k * (model // 2) + 128 * i : k * (model // 2) + 128 * i + hs] for k in range(2)], axis=0
    )


def project_body(hp, hs, nh, sc, hid_ref, starts_ref, *refs):
    first_refs, (proj_ref, qf_ref, kf_ref, va_ref, st_ref, w_ref, sems) = refs[0 : 2 * nh], refs[2 * nh :]
    p = pl.program_id(0)
    wait_for_piece(first_refs, w_ref, sems, sc)
    pc, tokens = proj_ref.shape[1:]
    cut = pc // 2
    bias = column(w_ref[2 * p, cut + hs // 2 :, 0:pc], 0, tokens)
    for k in range(2):
        rows = slice(k * cut, (k + 1) * cut)
        proj_ref[0, rows, :] = (nn(w_ref[2 * p + k, 0:cut, :], hid_ref[...]) + bias[rows, :]).astype(bf)
    included = (starts_ref[0:1, :] == sc[1]).astype(f32)
    extra = lax.broadcasted_iota(jnp.int32, (AUG - hs, tokens), 0)
    extra = jnp.where(extra < 2, 1.0, 0.0).astype(bf)
    for i in range(hp):
        row = 3 * hs * i
        for part, out in ((0, qf_ref), (1, kf_ref)):
            own_map = map_of(w_ref, 2 * p + part, i, hs, cut)
            logits = tn(own_map, proj_ref[0, row + part * hs : row + (part + 1) * hs, :])
            out[i, 0:hs, :] = soft_columns(logits).astype(bf)
            out[i, hs : 2 * hs, :] = soft_columns(-logits).astype(bf)
        va_ref[i, 0:hs, :] = proj_ref[0, row + 2 * hs : row + 3 * hs, :]
        va_ref[i, hs:AUG, :] = extra
        kept = (va_ref[i].astype(f32) * included).astype(bf)
        st_ref[i] = nt(kept, kf_ref[i]).astype(bf)


def wait_for_piece(first_refs, w_ref, sems, sc):
    p = pl.program_id(0)
    places = part_places(first_refs, w_ref, sc[0])
    copies = [pltpu.make_async_copy(ref, place, sems.at[k]) for k, (ref, place) in enumerate(zip(first_refs, places))]

    @pl.when(p == 0)
    def _():
        for copy in copies:
            copy.start()

    for k, copy in enumerate(copies):

        @pl.when(p == k // 2)
        def _(copy=copy):
            copy.wait()


def local_mix_body(hp, sc, qf_ref, kf_ref, va_ref, starts_ref, num_ref):
    tokens = qf_ref.shape[2]
    starts = starts_ref[...]
    for first, width, rows in causal_pieces(tokens):
        mask = ahead_mask(starts, rows, first, width)
        for i in range(hp):
            scores = tn(kf_ref[i, :, 0:rows], qf_ref[i, :, first : first + width])
            scores = jnp.where(mask, scores, 0.0).astype(bf)
            num_ref[i, :, first : first + width] = nn(va_ref[i, :, 0:rows], scores)


def weighted_state(sc, slot, refs, i, hp):
    total = jnp.where(sc[slot + len(refs) - 1] > 0, refs[-1][i].astype(f32), 0.0)
    for m, ref in enumerate(refs[:-1], 1):
        total += jnp.where(sc[slot + m - 1] > 0, ref[((i // hp) ^ m) * hp + i % hp].astype(f32), 0.0)
    return total


def load_out_weight(sc, wo_refs, w_ref, sems):
    rows = wo_refs[0].shape[0]
    places = [
        w_ref.at[pl.ds(pl.multiple_of(rows * (2 * (k // 2) + (sc[0] if k % 2 == 0 else 1 - sc[0])), TILE), rows), :]
        for k in range(len(wo_refs))
    ]
    return load_all(wo_refs, places, sems)


def mix_out_body(hp, hs, nh, sc, num_ref, qf_ref, starts_ref, x_ref, gain_ref, *refs):
    state_refs, row_refs, wo_refs = refs[0:nh], refs[nh : 2 * nh], refs[2 * nh : 4 * nh]
    sin_ref, mixd_ref, mix_ref, res_ref, hidt_ref, hid_ref, w_ref, sems = refs[4 * nh :]
    copies = load_out_weight(sc, wo_refs, w_ref, sems)
    uses = starts_ref[0:1, :] < 0
    model, tokens = x_ref.shape
    for i in range(num_ref.shape[0]):
        state = weighted_state(sc, 2, state_refs, i, hp).astype(bf)
        sin_ref[i] = state
        num = num_ref[i] + jnp.where(uses, nn(state, qf_ref[i]), 0.0)
        mixture = num[0:hs, :] / num[hs : hs + 1, :]
        mixd_ref[i, 0:hs, :] = mixture
        mixd_ref[i, hs : hs + 8, :] = num[hs : hs + 8, :]
        mix_ref[i * hs : (i + 1) * hs, :] = mixture.astype(bf)
    for copy in copies:
        copy.wait()
    res_ref[...] = x_ref[...].astype(f32) + tn(w_ref[...], mix_ref[...])
    width = model // nh
    h = sc[2 + 2 * nh]
    for j in range(nh):
        rows = pl.ds(pl.multiple_of((h ^ j) * width, TILE), width)
        res_ref[rows, :] += column(row_refs[j][:, 0:width], 2, tokens)
    normed, _ = norm_columns(res_ref[...].astype(bf).astype(f32))
    gains = gain_ref[...]
    hidden = (normed * column(gains, 2, tokens) + column(gains, 3, tokens)).astype(bf)
    hidt_ref[...] = hidden
    hid_ref[...] = hidden.T


def feed_body(count, first, sc, hid_ref, gy_ref, *refs):
    row_refs, down_refs, up_refs = refs[0:count], refs[count : 3 * count], refs[3 * count : 5 * count]
    refs = refs[5 * count :]
    if not first:
        out_in, sg_in = refs[0:2]
        refs = refs[2:]
    out_ref, sg_ref, mine_ref, theirs_ref, ub_ref, down_ref, up_ref, bias_ref, sems = refs
    tokens, model = hid_ref.shape
    mh = model // 2
    half = mine_ref.shape[2] // 2
    downs = load_all(down_refs, [down_ref.at[k] for k in range(2 * count)], sems.at[0])
    ups = load_all(up_refs, [up_ref.at[k] for k in range(2 * count)], sems.at[1])
    for k in range(2 * count):
        core = sc[0] if k % 2 == 0 else 1 - sc[0]
        bias_ref[k] = row_refs[k // 2][:, pl.ds(pl.multiple_of(core * half, 128), half)].astype(f32)
    for k in range(2 * count):
        ups[k].wait()
        downs[k].wait()
        bias = bias_ref[k, 1:2, :]
        up_pre = nn(hid_ref[:, 0:mh], up_ref[k, :, 0:mh]) + nn(hid_ref[:, mh:], up_ref[k, :, mh:]) + bias
        value, slope = gelu_pair(up_pre)
        act = value.astype(bf)
        up_grad = (nt(gy_ref[...], down_ref[k]) * slope).astype(bf)
        into = mine_ref if k % 2 == 0 else theirs_ref
        into[k // 2, :, 0:half] = act
        into[k // 2, :, half:] = up_grad
        ub_ref[k // 2, 8 * (k % 2) : 8 * (k % 2) + 8, :] = nn(jnp.ones((8, tokens), bf), up_grad)
        out, left, right = nn(act, down_ref[k]), nt(up_ref[k, :, 0:mh], up_grad), nt(up_ref[k, :, mh:], up_grad)
        if k == 0:
            if not first:
                out, left, right = out + out_in[...], left + sg_in[0:mh, :], right + sg_in[mh:, :]
            out_ref[...] = out
            sg_ref[0:mh, :] = left
            sg_ref[mh:, :] = right
        else:
            out_ref[...] += out
            sg_ref[0:mh, :] += left
            sg_ref[mh:, :] += right


def block_out_body(nh, sc, res_ref, out_ref, *refs):
    row_refs, o_ref, total_ref = refs[0:nh], refs[nh], refs[nh + 1]
    model, tokens = res_ref.shape
    width = model // nh
    total_ref[...] = res_ref[...] + out_ref[...].T
    h = sc[2 + 2 * nh]
    for j in range(nh):
        bias = column(row_refs[j][:, 0 : 2 * width], 2, tokens)[width:, :]
        rows = pl.ds(pl.multiple_of((h ^ j) * width, TILE), width)
        o_ref[h ^ j] = (total_ref[rows, :] + bias).astype(bf)


def second_back_body(hs, nh, sc, sg_ref, res_ref, gyt_ref, gain_ref, mixd_ref, starts_ref, qf_ref, *refs):
    wo_refs, (rg_ref, ag_ref, vec_ref, na_ref, sgt_ref, w_ref, sems) = refs[0 : 2 * nh], refs[2 * nh :]
    copies = load_out_weight(sc, wo_refs, w_ref, sems)
    model, tokens = sg_ref.shape
    width = model // nh
    normed, inv_std = norm_columns(res_ref[...].astype(bf).astype(f32))
    sg = sg_ref[...]
    res_grad = gyt_ref[...].astype(f32) + norm_columns_back(sg, normed, inv_std, column(gain_ref[...], 2, tokens))
    rg_ref[...] = res_grad
    ag_ref[...] = res_grad.astype(bf)
    uses = (starts_ref[0:1, :] < 0).astype(f32)
    for copy in copies:
        copy.wait()
    mg = nn(w_ref[...], ag_ref[...])
    row = lax.broadcasted_iota(jnp.int32, (AUG - hs, tokens), 0)
    for i in range(qf_ref.shape[0]):
        num = mg[i * hs : (i + 1) * hs, :] / mixd_ref[i, hs : hs + 1, :]
        den = -jnp.sum(num * mixd_ref[i, 0:hs, :], axis=0, keepdims=True)
        high = den.astype(bf).astype(f32)
        extra = jnp.where(row == 0, high, jnp.where(row == 1, den - high, 0.0))
        na_ref[i, 0:hs, :] = num.astype(bf)
        na_ref[i, hs:AUG, :] = extra.astype(bf)
        kept = (na_ref[i].astype(f32) * uses).astype(bf)
        sgt_ref[i] = nt(kept, qf_ref[i]).astype(bf)
    for at, value in enumerate((sg * normed, sg, ag_ref[...], gyt_ref[...])):
        sums = row_sums(value)
        for p in range(nh):
            vec_ref[p, at : at + 1, :] = sums[0:1, p * width : (p + 1) * width]


def halves_back(feat, grad, hs):
    parts = []
    for k in range(2):
        soft = feat[k * hs : (k + 1) * hs, :].astype(f32)
        own = grad[k * hs : (k + 1) * hs, :]
        weight = jnp.sum(soft * own, axis=0, keepdims=True) / jnp.sum(soft, axis=0, keepdims=True)
        parts.append(soft * (own - weight))
    return (parts[0] - parts[1]).astype(bf)


def local_back_body(hp, hs, sc, qf_ref, kf_ref, va_ref, na_ref, sin_ref, starts_ref, ql_ref, kfg_ref, vg_ref):
    tokens = qf_ref.shape[2]
    starts = starts_ref[...]
    step = tokens // 2
    uses = starts[0:1, :] < 0
    masks = [ahead_mask(starts, rows, first, width) for first, width, rows in causal_pieces(tokens)]
    for i in range(hp):
        na = na_ref[i]
        through = tn(sin_ref[i], na)
        for which, (first, width, rows) in enumerate(causal_pieces(tokens)):
            at = slice(first, first + width)
            mask = masks[which]
            scores = jnp.where(mask, tn(kf_ref[i, :, 0:rows], qf_ref[i, :, at]), 0.0).astype(bf)
            sgrad = jnp.where(mask, tn(va_ref[i, :, 0:rows], na[:, at]), 0.0).astype(bf)
            qfg = nn(kf_ref[i, :, 0:rows], sgrad) + jnp.where(uses[:, at], through[:, at], 0.0)
            ql_ref[i, :, at] = halves_back(qf_ref[i, :, at], qfg, hs)
            kfg = nt(qf_ref[i, :, at], sgrad)
            vg = nt(na[:, at], scores)[0:hs, :]
            if which == 0:
                kfg_ref[i, :, 0:rows] = kfg
                vg_ref[i, :, 0:rows] = vg
            else:
                kfg_ref[i, :, 0:step] += kfg[:, 0:step]
                vg_ref[i, :, 0:step] += vg[:, 0:step]
                kfg_ref[i, :, step:] = kfg[:, step:]
                vg_ref[i, :, step:] = vg[:, step:]


def join_extra(state, hs):
    row = lax.broadcasted_iota(jnp.int32, state.shape, 0)
    both = state[hs : hs + 1, :] + state[hs + 1 : hs + 2, :]
    return jnp.where(row < hs, state, jnp.where(row == hs, both, 0.0))


def project_back_body(hp, hs, nh, sc, *refs):
    state_refs, first_refs, refs = refs[0:nh], refs[nh : 3 * nh], refs[3 * nh :]
    kf_ref, va_ref, ql_ref, kfg_ref, vg_ref, proj_ref, starts_ref, pg_ref, fg_ref, mg_ref, pb_ref, first_ref, sems = refs
    p = pl.program_id(0)
    wait_for_piece(first_refs, first_ref, sems, sc)
    included = starts_ref[0:1, :] == sc[1]
    cut = pg_ref.shape[1] // 2
    for i in range(hp):
        total = jnp.where(sc[1 + 2 * nh] > 0, state_refs[-1][i].astype(f32), 0.0)
        for m in range(1, nh):
            total += jnp.where(sc[1 + nh + m] > 0, state_refs[m - 1][i].astype(f32), 0.0)
        state = join_extra(total, hs).astype(bf)
        kfg = kfg_ref[i] + jnp.where(included, tn(state, va_ref[i]), 0.0)
        vg = vg_ref[i] + jnp.where(included, nn(state, kf_ref[i])[0:hs, :], 0.0)
        klg = halves_back(kf_ref[i], kfg, hs)
        qlg = ql_ref[i]
        row = 3 * hs * i
        pg_ref[0, row : row + hs, :] = nn(map_of(first_ref, 2 * p, i, hs, cut), qlg).astype(bf)
        pg_ref[0, row + hs : row + 2 * hs, :] = nn(map_of(first_ref, 2 * p + 1, i, hs, cut), klg).astype(bf)
        pg_ref[0, row + 2 * hs : row + 3 * hs, :] = vg.astype(bf)
        q_grad = nt(proj_ref[0, row : row + hs, :], qlg)
        k_grad = nt(proj_ref[0, row + hs : row + 2 * hs, :], klg)
        mg_ref[0, :, 128 * i : 128 * (i + 1)] = jnp.concatenate([q_grad, k_grad], axis=1)
    pb_ref[0] = row_sums(pg_ref[0])
    grad = tn(first_ref[2 * p, 0:cut, :], pg_ref[0, 0:cut, :]) + tn(first_ref[2 * p + 1, 0:cut, :], pg_ref[0, cut:, :])

    @pl.when(pl.program_id(0) == 0)
    def _():
        fg_ref[...] = grad

    @pl.when(pl.program_id(0) > 0)
    def _():
        fg_ref[...] += grad


def first_back_body(nh, sc, fg_ref, x_ref, rg_ref, gain_ref, tg_ref, vec_ref):
    model, tokens = fg_ref.shape
    width = model // nh
    normed, inv_std = norm_columns(x_ref[...].astype(f32))
    fg = fg_ref[...]
    gain = column(gain_ref[...], 0, tokens)
    tg = (rg_ref[...] + norm_columns_back(fg, normed, inv_std, gain)).astype(bf)
    for p in range(nh):
        tg_ref[p] = tg[p * width : (p + 1) * width, :]
    for at, value in enumerate((fg * normed, fg)):
        sums = row_sums(value)
        for p in range(nh):
            vec_ref[p, at : at + 1, :] = sums[0:1, p * width : (p + 1) * width]


def up_grads_body(nh, sc, hidt_ref, hidt2_ref, early_ref, late_ref, early2_ref, late2_ref, *o_refs):
    for j in range(nh):
        own, peer, k = (early_ref, early2_ref, j) if j < nh - 1 else (late_ref, late2_ref, 0)
        o_refs[j][...] = (nn(hidt_ref[...], own[k]) + nn(hidt2_ref[...], peer[k])).astype(bf)


def down_grads_body(nh, sc, gyt_ref, gyt2_ref, early_ref, late_ref, early2_ref, late2_ref,
                    mix_ref, mix2_ref, ag_ref, ag2_ref, *o_refs):
    model = gyt_ref.shape[0]
    width = model // nh
    for j in range(nh):
        own, peer, k = (early_ref, early2_ref, j) if j < nh - 1 else (late_ref, late2_ref, 0)
        o_refs[j][0:model, :] = (nn(gyt_ref[...], own[k]) + nn(gyt2_ref[...], peer[k])).astype(bf)
        rows = slice(j * width, (j + 1) * width)
        o_refs[j][model:, :] = (nt(mix_ref[rows, :], ag_ref[...]) + nt(mix2_ref[rows, :], ag2_ref[...])).astype(bf)


def last_grads_body(nh, sc, pg_ref, pg2_ref, hid_ref, hid2_ref, mg_ref, pb_ref, early_ref, late_ref, vec1_ref, vec2_ref,
                    *refs):
    o_refs, rows_ref = refs[0:nh], refs[nh]
    pc, half = pg_ref.shape[1], hid_ref.shape[0]
    hs = mg_ref.shape[1]
    width = vec1_ref.shape[2]
    h = sc[2 + 2 * nh]
    for j in range(nh):
        o_ref = o_refs[j]
        o_ref[0:pc, :] = (nt(pg_ref[j], hid_ref[...]) + nt(pg2_ref[j], hid2_ref[...])).astype(bf)
        o_ref[pc : pc + hs, :] = mg_ref[j].astype(bf)
        ub_ref, k = (early_ref, j) if j < nh - 1 else (late_ref, 0)
        first = jnp.where(sc[0] == 0, ub_ref[k, 0:1, :], ub_ref[k, 8:9, :])
        second = jnp.where(sc[0] == 0, ub_ref[k, 8:9, :], ub_ref[k, 0:1, :])
        rows_ref[...] = jnp.zeros_like(rows_ref)
        rows_ref[0:1, :] = pb_ref[j, 0:1, 0:half]
        rows_ref[1:2, 0 : pc - half] = pb_ref[j, 0:1, half:]
        rows_ref[2:3, :] = first
        rows_ref[3:4, :] = second
        rows_ref[4:8, 0:width] = vec2_ref[h ^ j, 0:4, :]
        rows_ref[8:10, 0:width] = vec1_ref[h ^ j, 0:2, :]
        o_ref[pc + hs :, :] = rows_ref[...].astype(bf)


def side_by_side_body(sc, mine_ref, theirs_ref, o_ref):
    half = mine_ref.shape[1]
    o_ref[:, pl.ds(pl.multiple_of(sc[0] * half, 128), half)] = mine_ref[...].astype(f32)
    o_ref[:, pl.ds(pl.multiple_of((1 - sc[0]) * half, 128), half)] = theirs_ref[...].astype(f32)


def down_out_body(sc, mine_ref, theirs_ref, down_ref, out_ref):
    model = down_ref.shape[1]
    half = mine_ref.shape[1]
    for core, ref in ((sc[0], mine_ref), (1 - sc[0], theirs_ref)):
        at = pl.ds(pl.multiple_of(core * half, 128), half)
        down_ref[at, :] = ref[0:model, :].astype(f32).T
        out_ref[:, at] = ref[model:, :].astype(f32)


def last_out_body(hs, sc, mine_ref, theirs_ref, qkv_ref, qm_ref, km_ref, rows_ref):
    pc = qkv_ref.shape[0]
    half = mine_ref.shape[1]
    for core, ref in ((sc[0], mine_ref), (1 - sc[0], theirs_ref)):
        at = pl.ds(pl.multiple_of(core * half, 128), half)
        qkv_ref[:, at] = ref[0:pc, :].astype(f32)
    maps = mine_ref[pc : pc + hs, :].astype(f32) + theirs_ref[pc : pc + hs, :].astype(f32)
    for i in range(qm_ref.shape[0]):
        qm_ref[i] = maps[:, 128 * i : 128 * i + hs]
        km_ref[i] = maps[:, 128 * i + hs : 128 * i + 2 * hs]
    rows = slice(pc + hs, pc + hs + TILE)
    rows_ref[...] = mine_ref[rows, :].astype(f32) + theirs_ref[rows, :].astype(f32)


def swap(a, axis, k):
    n = lax.axis_size(axis)
    return lax.ppermute(a, axis, [(i, i ^ k) for i in range(n)])


def trade(a, axis):
    return lax.all_to_all(a, axis, 0, 0, tiled=True)


def after(a, *others):
    return lax.optimization_barrier((a,) + others)[0]


def chain_seq(part, forward, weight_of):
    n = lax.axis_size("seq")
    total = None
    for k in range(1, n):
        pairs = [(i, i + k) if forward else (i + k, i) for i in range(n - k)]
        if n == 2:
            return lax.ppermute(part, "seq", pairs)
        sent = part if forward else part * weight_of(k).astype(part.dtype)
        got = lax.ppermute(sent, "seq", pairs).astype(f32) * (weight_of(k) if forward else 1.0)
        total = got if total is None else total + got
    return total.astype(bf)


def local(tokens, attn_gain, attn_shift, qkv_weight, qkv_bias, query_map, key_map, out_weight, out_bias,
          mlp_gain, mlp_shift, up_weight, up_bias, down_weight, down_bias, positions, out_grad):
    nh, ns, nz = lax.axis_size("head"), lax.axis_size("seq"), lax.axis_size("dp")
    length, width = tokens.shape[1], tokens.shape[2]
    model = width * nh
    half = model // 2
    hp, hs = query_map.shape[0], query_map.shape[1]
    heads = hp * nh
    pc = qkv_weight.shape[1]
    hidden = up_weight.shape[1]
    hh = hidden // 2
    tok = length // nh
    h = lax.axis_index("head")
    s2 = lax.axis_index("seq") % 2
    peers = range(1, nh)

    run = positions[0]
    start_of = jnp.arange(length, dtype=jnp.int32) - run
    chunk_starts = lax.dynamic_slice_in_dim(start_of, h * tok, tok, 0) - h * tok
    starts = jnp.broadcast_to(chunk_starts[None, :], (8, tok))
    firsts = start_of[::tok]
    run_last = start_of[length - 1]
    other = [h ^ m for m in range(nh)]
    fwd = [(other[m] < h) & (firsts[h] <= (other[m] + 1) * tok - 1) for m in peers]
    bwd = [(other[m] > h) & (firsts[other[m]] <= (h + 1) * tok - 1) for m in peers]
    sc = jnp.stack(
        [s2, chunk_starts[tok - 1]]
        + [a.astype(jnp.int32) for a in fwd]
        + [(firsts[h] < 0).astype(jnp.int32)]
        + [a.astype(jnp.int32) for a in bwd]
        + [(run_last <= (h + 1) * tok - 1).astype(jnp.int32), h]
    ).astype(jnp.int32)

    def to_chunks(a):
        a = a[0].T.reshape(width, nh, tok).transpose(1, 0, 2)
        return trade(a, "head").reshape(model, tok)

    def to_runs(a):
        return trade(a, "head").transpose(1, 0, 2).reshape(width, length).T[None]

    own_rows = jnp.stack(
        [jnp.pad(qkv_bias, (0, model - pc)), jnp.pad(up_bias, (0, model - hidden)),
         jnp.pad(jnp.concatenate([out_bias, down_bias]), (0, model - 2 * width))]
    )
    own_rows = jnp.pad(own_rows, ((0, TILE - 3), (0, 0)))
    gains = jnp.pad(jnp.stack([attn_gain, attn_shift, mlp_gain, mlp_shift]), ((0, TILE - 4), (0, 0)))
    fr = pc // 2 + hs // 2 + TILE
    parts = [shape((fr, model), bf), shape((width // 2, model), bf), shape((hh, model), bf), shape((hh, model), bf)]
    packed = run_kernel(
        pack_body, "pack_weights", (1,), sc,
        [(a, None) for a in (qkv_weight.T, query_map.reshape(-1, hs), key_map.reshape(-1, hs), own_rows, out_weight,
                             up_weight, down_weight)],
        [(a, None) for a in parts * 2],
    )
    x = to_chunks(tokens)

    def halves(own, other, arrived):
        return [[own, other]] + [[a, swap(a, "seq", 1)] for a in arrived]

    first_got = [swap(packed[0], "head", m) for m in peers]
    first = halves(packed[0], packed[4], first_got)
    wo_own = after(packed[1], *first_got)
    wo_got = [swap(wo_own, "head", m) for m in peers]
    wo = halves(packed[1], packed[5], wo_got)
    all_first = [a for pair in first for a in pair]
    all_wo = [a for pair in wo for a in pair]
    row_specs = [(pair[0], pl.BlockSpec((TILE, model), lambda *_: (fr // TILE - 1, 0))) for pair in first]
    in_hbm = lambda arrays: [(a, HBM) for a in arrays]
    first_scratch = [pltpu.VMEM((2 * nh, fr, model), bf), pltpu.SemaphoreType.DMA((2 * nh,))]
    wo_scratch = [pltpu.VMEM((model, model), bf), pltpu.SemaphoreType.DMA((2 * nh,))]

    (hid,) = run_kernel(first_norm_body, "first_norm", (1,), sc, [(x, None), (gains, None)], [(shape((model, tok), bf), None)])
    va_spec, state_spec, feat_spec = lead(hp, AUG, tok), lead(hp, AUG, 2 * hs), lead(hp, 2 * hs, tok)
    feat = (shape((heads, 2 * hs, tok), bf), feat_spec)
    proj, qf, kf, va, states = run_kernel(
        functools.partial(project_body, hp, hs, nh), "project", (nh,), sc,
        [(hid, None), (starts, None)] + in_hbm(all_first),
        [(shape((nh, pc, tok), bf), lead(1, pc, tok)), feat, feat,
         (shape((heads, AUG, tok), bf), va_spec), (shape((heads, AUG, 2 * hs), bf), state_spec)],
        flops=nh * (2 * model * pc * tok + 4 * pc * hs * tok), trans=4 * heads * hs * tok, scratch=first_scratch,
    )
    pair_flops = 2 * heads * tok * tok * 3 // 4
    (num,) = run_kernel(
        functools.partial(local_mix_body, hp), "local_mix", (nh,), sc,
        [(qf, feat_spec), (kf, feat_spec), (va, va_spec), (starts, None)],
        [(shape((heads, AUG, tok), f32), va_spec)], flops=pair_flops * (2 * hs + AUG),
    )
    around = [after(swap(states, "head", m), num) for m in peers]

    def to_own_pieces(a, m):
        a = a.reshape(nh, hp, AUG, 2 * hs)
        return jnp.stack([a[j ^ m] for j in range(nh)]).reshape(heads, AUG, 2 * hs)

    ends_in = [(run_last <= (other[m] + 1) * tok - 1).astype(f32) for m in range(nh)]
    whole_run = sum(to_own_pieces(a, m).astype(f32) * ends_in[m] for m, a in enumerate([states] + around)).astype(bf)
    before = chain_seq(whole_run, True, lambda k: (start_of[0] <= -(k - 1) * length - 1).astype(f32))

    down_own, up_own = after(packed[2], *wo_got), after(packed[3], *wo_got)
    down_got, up_got = {1: swap(down_own, "head", 1)}, {2: swap(up_own, "head", 2)}
    down_late, up_late = after(down_own, states), after(up_own, states)
    down_got[2] = swap(down_late, "head", 2)
    up_got[1] = swap(up_late, "head", 1)
    down_got[3] = swap(after(down_got[1], num), "head", 2)
    up_got[3] = swap(after(up_got[2], num), "head", 1)
    down = halves(packed[2], packed[6], [down_got[m] for m in peers])
    up = halves(packed[3], packed[7], [up_got[m] for m in peers])
    gyt = to_chunks(out_grad)

    sin, mixd, mix, res, hidt2, hid2 = run_kernel(
        functools.partial(mix_out_body, hp, hs, nh), "mix_out", (1,), sc,
        [(a, None) for a in (num, qf, starts, x, gains, *around, before)] + row_specs + in_hbm(all_wo),
        [(shape((heads, AUG, 2 * hs), bf), None), (shape((heads, hs + 8, tok), f32), None), (shape((model, tok), bf), None),
         (shape((model, tok), f32), None), (shape((model, tok), bf), None), (shape((tok, model), bf), None)],
        flops=2 * model * model * tok + 2 * heads * AUG * 2 * hs * tok, scratch=wo_scratch,
    )
    hidt2_peer, gyt_peer, mix_peer = swap(hidt2, "seq", 1), swap(gyt, "seq", 1), swap(mix, "seq", 1)
    hid_peer = swap(lax.dynamic_slice_in_dim(hid, (1 - s2) * half, half, 0), "seq", 1)

    (gy,) = run_kernel(turn_body, "turn_grad", (1,), sc, [(gyt, None)], [(shape((tok, model), bf), None)])

    def feed(which, sums):
        count = len(which)
        return run_kernel(
            functools.partial(feed_body, count, not sums), f"feed_{which[0]}", (1,), sc,
            [(hid2, None), (gy, None)] + [row_specs[j] for j in which]
            + in_hbm([a for j in which for a in down[j]]) + in_hbm([a for j in which for a in up[j]])
            + [(a, None) for a in sums],
            [(shape((tok, model), f32), None), (shape((model, tok), f32), None), (shape((count, tok, hidden), bf), None),
             (shape((count, tok, hidden), bf), None), (shape((count, TILE, hh), f32), None)],
            flops=count * 8 * model * hidden * tok, trans=count * hidden * tok,
            scratch=[pltpu.VMEM((2 * count, hh, model), bf), pltpu.VMEM((2 * count, hh, model), bf),
                     pltpu.VMEM((2 * count, TILE, hh), f32), pltpu.SemaphoreType.DMA((2, 2 * count))],
        )

    part_out, part_sg, early, early_theirs, early_ub = feed(list(range(nh - 1)), ())
    early_peer = swap(early_theirs, "seq", 1)
    mlp_out, sg, late, late_theirs, late_ub = feed([nh - 1], (part_out, part_sg))
    late_peer = swap(late_theirs, "seq", 1)
    run_block = (shape((nh, width, tok), bf), None)
    (bo,) = run_kernel(
        functools.partial(block_out_body, nh), "block_out", (1,), sc,
        [(res, None), (mlp_out, None)] + row_specs, [run_block], scratch=[pltpu.VMEM((model, tok), f32)],
    )

    vec_block = (shape((nh, 8, width), f32), None)
    rg, ag, vec2, na, sgt = run_kernel(
        functools.partial(second_back_body, hs, nh), "second_back", (1,), sc,
        [(a, None) for a in (sg, res, gyt, gains, mixd, starts, qf)] + in_hbm(all_wo),
        [(shape((model, tok), f32), None), (shape((model, tok), bf), None), vec_block,
         (shape((heads, AUG, tok), bf), None), (shape((heads, AUG, 2 * hs), bf), None)],
        flops=2 * model * model * tok + 2 * heads * AUG * 2 * hs * tok, scratch=wo_scratch,
    )
    g_sent = [swap(sgt, "head", m) for m in peers]
    ag_peer = swap(lax.dynamic_slice_in_dim(ag, (1 - s2) * half, half, 0), "seq", 1)
    def over_head(own, got):
        total = sum(a.astype(f32) for a in got) + own.astype(f32)
        base = total
        for k in range(1, ns // 2):
            total += lax.ppermute(base, "seq", [(i, (i + 2 * k) % ns) for i in range(ns)])
        return total.astype(bf)

    def over_dp(total):
        total = (total.astype(f32) + swap(total, "dp", 1).astype(f32)).astype(bf)
        across = lax.ppermute(total, "dp", [(1, 2), (2, 1)])
        total = (total.astype(f32) + across.astype(f32)).astype(bf)
        out = lax.ppermute(total, "dp", [(1, 0), (2, 3)])
        z = lax.axis_index("dp")
        return jnp.where((z == 1) | (z == 2), total, out)

    def over_dp_traded(total):
        rows = total.shape[0] // nz
        own = trade(total.reshape(nz, rows, -1), "dp").astype(f32).sum(0).astype(bf)
        return trade(jnp.broadcast_to(own[None], (nz,) + own.shape), "dp").reshape(total.shape)

    def both_halves(a):
        return a, swap(a, "seq", 1)

    def columns_of(a, at):
        return (a, pl.BlockSpec((a.shape[0], tok, hh), lambda p, sc: (0, 0, at)))

    half_spec = pl.BlockSpec((half, tok), lambda p, sc: (sc[0], 0))
    up_parts = run_kernel(
        functools.partial(up_grads_body, nh), "up_grads", (1,), sc,
        [(hidt2, None), (hidt2_peer, None)] + [columns_of(a, 1) for a in (early, late, early_peer, late_peer)],
        [(shape((model, hh), bf), None)] * nh, flops=nh * 2 * model * hidden * tok,
    )
    up_got = [swap(up_parts[m], "head", m) for m in peers]
    down_parts = run_kernel(
        functools.partial(down_grads_body, nh), "down_grads", (1,), sc,
        [(gyt, None), (gyt_peer, None)] + [columns_of(a, 0) for a in (early, late, early_peer, late_peer)]
        + [(mix, None), (mix_peer, None), (ag, half_spec), (ag_peer, None)],
        [(shape((model + width, hh), bf), None)] * nh, flops=nh * 2 * model * (hidden + width) * tok,
    )

    down_got_sum = [swap(down_parts[m], "head", m) for m in peers]

    g_around = [after(a, up_parts[0], down_parts[0]) for a in g_sent]
    begins_in = [(firsts[other[m]] < 0).astype(f32) for m in range(nh)]
    g_whole = sum(to_own_pieces(a, m).astype(f32) * begins_in[m] for m, a in enumerate([sgt] + g_around)).astype(bf)
    after_run = chain_seq(g_whole, False, lambda k: (start_of[0] <= -(k - 1) * length - 1).astype(f32))
    na_late = after(na, g_whole)
    ql, kfg, vg = run_kernel(
        functools.partial(local_back_body, hp, hs), "local_back", (nh,), sc,
        [(qf, feat_spec), (kf, feat_spec), (va, va_spec), (na_late, va_spec), (sin, state_spec), (starts, None)],
        [(shape((heads, hs, tok), bf), lead(hp, hs, tok)), (shape((heads, 2 * hs, tok), f32), feat_spec),
         (shape((heads, hs, tok), f32), lead(hp, hs, tok))],
        flops=pair_flops * (6 * hs + 3 * AUG),
    )

    def peer_states(a, m):
        return (a, pl.BlockSpec((hp, AUG, 2 * hs), lambda p, sc: (p ^ m, 0, 0)))

    pg, fg, map_grads, pb = run_kernel(
        functools.partial(project_back_body, hp, hs, nh), "project_back", (nh,), sc,
        [peer_states(a, m) for a, m in zip(g_around + [after_run], [*peers, 0])] + in_hbm(all_first)
        + [(kf, feat_spec), (va, va_spec), (ql, lead(hp, hs, tok)), (kfg, feat_spec), (vg, lead(hp, hs, tok)),
           (proj, lead(1, pc, tok)), (starts, None)],
        [(shape((nh, pc, tok), bf), lead(1, pc, tok)), (shape((model, tok), f32), None),
         (shape((nh, hs, 128 * hp), f32), lead(1, hs, 128 * hp)), (shape((nh, 8, pc), f32), lead(1, 8, pc))],
        flops=nh * (2 * model * pc * tok + 12 * pc * hs * tok), scratch=first_scratch,
    )
    pg_peer = swap(pg, "seq", 1)
    up_mid = over_head(after(up_parts[0], pg), up_got)
    tg, vec1 = run_kernel(
        functools.partial(first_back_body, nh), "first_back", (1,), sc,
        [(after(fg, up_mid), None), (x, None), (rg, None), (gains, None)], [run_block, vec_block],
    )
    tokens_grad = to_runs(tg)
    block_out = to_runs(bo)
    last_rows = -(-(pc + hs + TILE) // (nz * TILE)) * nz * TILE
    last_parts = run_kernel(
        functools.partial(last_grads_body, nh), "last_grads", (1,), sc,
        [(pg, None), (pg_peer, None), (hid, half_spec), (hid_peer, None)]
        + [(a, None) for a in (map_grads, pb, early_ub, late_ub, vec1, vec2)],
        [(shape((last_rows, half), bf), None)] * nh, flops=nh * 2 * model * pc * tok,
        scratch=[pltpu.VMEM((last_rows - pc - hs, half), f32)],
    )

    up_sum = both_halves(over_dp(up_mid))
    down_sum = both_halves(over_dp(over_head(after(down_parts[0], *last_parts), down_got_sum)))
    last_mid = over_head(last_parts[0], [swap(last_parts[m], "head", m) for m in peers])
    last_sum = both_halves(over_dp_traded(last_mid))
    (upweight_grad,) = run_kernel(
        side_by_side_body, "up_result", (1,), sc, [(a, None) for a in up_sum], [(shape((model, hidden), f32), None)]
    )
    downweight_grad, outweight_grad = run_kernel(
        down_out_body, "down_result", (1,), sc, [(a, None) for a in down_sum],
        [(shape((hidden, model), f32), None), (shape((width, model), f32), None)],
    )
    qkv_grad, query_grad, key_grad, rows = run_kernel(
        functools.partial(last_out_body, hs), "last_result", (1,), sc, [(a, None) for a in last_sum],
        [(shape((pc, model), f32), None), (shape((hp, hs, hs), f32), None), (shape((hp, hs, hs), f32), None),
         (shape((TILE, half), f32), None)],
    )
    qkvbias_grad = jnp.concatenate([rows[0], rows[1, 0 : pc - half]])
    upbias_grad = jnp.concatenate([rows[2], rows[3]])
    vec = rows[4:10, 0:width]
    return (block_out, tokens_grad, vec[4], vec[5], qkv_grad.T, qkvbias_grad, query_grad, key_grad,
            outweight_grad, vec[2], vec[0], vec[1], upweight_grad, upbias_grad, downweight_grad, vec[3])


def solution(mesh):
    wide = P("dp", "seq", "head")
    return jax.shard_map(
        local,
        mesh=mesh,
        in_specs=(wide, P(), P(), P(None, "head"), P("head"), P("head", None, None), P("head", None, None),
                  P("head", None), P("head"), P(), P(), P(None, "head"), P("head"), P("head", None), P("head"),
                  P("dp", "seq"), wide),
        out_specs=(wide, wide, P("head"), P("head"), P(None, "head"), P("head"), P("head", None, None),
                   P("head", None, None), P("head", None), P("head"), P("head"), P("head"), P(None, "head"), P("head"),
                   P("head", None), P("head")),
        check_vma=False,
    )
```

```python
import functools

import jax
import jax.numpy as jnp
from jax import lax
from jax.experimental import pallas as pl
from jax.experimental.pallas import tpu as pltpu
from jax.sharding import PartitionSpec as P

eps = 1e-05
gelu_scale = 0.7978845608028654
bf = jnp.bfloat16
f32 = jnp.float32
AUG = 80
TILE = 16


def nn(a, b):
    return lax.dot_general(a, b, (((1,), (0,)), ((), ())), preferred_element_type=f32)


def nt(a, b):
    return lax.dot_general(a, b, (((1,), (1,)), ((), ())), preferred_element_type=f32)


def tn(a, b):
    return lax.dot_general(a, b, (((0,), (0,)), ((), ())), preferred_element_type=f32)


def shape(dims, dtype):
    return jax.ShapeDtypeStruct(tuple(dims), dtype)


def whole(a):
    dims = tuple(a.shape)
    return pl.BlockSpec(dims, lambda *_: (0,) * len(dims))


def lead(count, *dims):
    return pl.BlockSpec((count,) + dims, lambda p, sc: (p,) + (0,) * len(dims))


def run_kernel(body, name, grid, scalars, ins, outs, scratch=(), aliases=None):
    return pl.pallas_call(
        body,
        out_shape=[o for o, _ in outs],
        grid_spec=pltpu.PrefetchScalarGridSpec(
            num_scalar_prefetch=1,
            grid=grid,
            in_specs=[spec or whole(a) for a, spec in ins],
            out_specs=[spec or whole(o) for o, spec in outs],
            scratch_shapes=list(scratch),
        ),
        compiler_params=pltpu.CompilerParams(vmem_limit_bytes=50 * 2**20),
        cost_estimate=pl.CostEstimate(flops=0, bytes_accessed=0, transcendentals=0),
        input_output_aliases=aliases or {},
        name=name,
    )(scalars, *[a for a, _ in ins])


def norm_columns(values):
    center = values - jnp.mean(values, axis=0, keepdims=True)
    inv_std = lax.rsqrt(jnp.mean(center * center, axis=0, keepdims=True) + eps)
    return center * inv_std, inv_std


def norm_columns_back(grad, normed, inv_std, gain):
    scaled = grad * gain
    return inv_std * (
        scaled
        - jnp.mean(scaled, axis=0, keepdims=True)
        - normed * jnp.mean(scaled * normed, axis=0, keepdims=True)
    )


def column(rows, at, width):
    only = jnp.where(lax.broadcasted_iota(jnp.int32, rows.shape, 0) == at, rows.astype(f32), 0.0).astype(bf)
    upright = tn(only, jnp.ones((TILE, 128), bf))
    return jnp.concatenate([upright] * (width // 128), axis=1)


def row_sums(values):
    ones = jnp.ones((8, values.shape[1]), bf)
    if values.dtype == bf:
        return nt(ones, values)
    high = values.astype(bf)
    return nt(ones, high) + nt(ones, (values - high.astype(f32)).astype(bf))


def gelu_pair(up_pre):
    square = up_pre * up_pre
    tanh_value = jnp.tanh(gelu_scale * (up_pre + 0.044715 * square * up_pre))
    half_one = 0.5 * (1.0 + tanh_value)
    slope = half_one + 0.5 * up_pre * (1.0 - tanh_value * tanh_value) * gelu_scale * (
        1.0 + 3.0 * 0.044715 * square
    )
    return up_pre * half_one, slope


def soft_columns(logits):
    top = jnp.exp(logits - jnp.max(logits, axis=0, keepdims=True))
    return top / jnp.sum(top, axis=0, keepdims=True)


def ahead_mask(starts, rows, first_column, columns):
    j = lax.broadcasted_iota(jnp.int32, (rows, columns), 0)
    i = lax.broadcasted_iota(jnp.int32, (rows, columns), 1) + first_column
    return (j <= i) & (j >= starts[0:1, first_column : first_column + columns])


def causal_pieces(tokens):
    step = tokens // 2
    return ((0, step, step), (step, step, tokens))


HBM = pl.BlockSpec(memory_space=pl.ANY)


def load_all(refs, places, sems):
    copies = [pltpu.make_async_copy(ref, place, sems.at[k]) for k, (ref, place) in enumerate(zip(refs, places))]
    for copy in copies:
        copy.start()
    return copies


def part_places(refs, scratch, core):
    return [scratch.at[2 * (k // 2) + (core if k % 2 == 0 else 1 - core)] for k in range(len(refs))]


def pack_body(sc, qkv_ref, qm_ref, km_ref, qb_ref, ub_ref, ob_ref, db_ref, out_ref, up_ref, down_ref,
              first_ref, other_ref, wa_ref, wb_ref, rows_ref):
    pc, model = qkv_ref.shape
    hs = qm_ref.shape[1]
    width = ob_ref.shape[1]
    rows_ref[...] = jnp.zeros_like(rows_ref)
    rows_ref[0:1, 0:pc] = qb_ref[...].astype(f32)
    rows_ref[1:2, 0 : ub_ref.shape[1]] = ub_ref[...].astype(f32)
    rows_ref[2:3, 0:width] = ob_ref[...].astype(f32)
    rows_ref[3:4, 0:width] = db_ref[...].astype(f32)
    for core, ref in ((sc[0], first_ref), (1 - sc[0], other_ref)):
        cut = pc // 2
        ref[0:cut, :] = qkv_ref[pl.ds(pl.multiple_of(core * cut, TILE), cut), :]
        ref[cut : cut + hs // 2, :] = jnp.zeros((hs // 2, model), bf)
        for i in range(qm_ref.shape[0] // hs):
            for k in range(2):
                rows = slice(i * hs + k * hs // 2, i * hs + (k + 1) * hs // 2)
                at = k * (model // 2) + 128 * i
                own = jnp.where(core == 0, qm_ref[rows, :].astype(f32), km_ref[rows, :].astype(f32))
                ref[cut : cut + hs // 2, at : at + hs] = own.astype(bf)
        cut += hs // 2
        ref[cut : cut + TILE, :] = rows_ref[...].astype(bf)
        half = out_ref.shape[0] // 2
        ref[cut + TILE :, :] = out_ref[pl.ds(pl.multiple_of(core * half, TILE), half), :]
    half = down_ref.shape[0] // 2
    at = pl.ds(pl.multiple_of(sc[0] * half, TILE), half)
    soon = wa_ref.shape[0]
    lanes = pl.ds(pl.multiple_of(sc[0] * half, 128), half)
    wa_ref[:, 0:half] = up_ref[0:soon, lanes]
    wa_ref[:, half:] = down_ref[pl.ds(pl.multiple_of(sc[0] * half, TILE), soon), 0:half]
    wb_ref[:, 0:half] = up_ref[soon:, lanes]
    wb_ref[0 : half - soon, half:] = down_ref[pl.ds(pl.multiple_of(sc[0] * half + soon, TILE), half - soon), 0:half]
    wb_ref[half - soon :, half:] = down_ref[at, half:]


def first_norm_body(sc, x_ref, gain_ref, hid_ref):
    normed, _ = norm_columns(x_ref[...].astype(f32))
    width = x_ref.shape[1]
    gains = gain_ref[...]
    hid_ref[...] = (normed * column(gains, 0, width) + column(gains, 1, width)).astype(bf)


def turn_body(sc, a_ref, b_ref, o_ref):
    tokens = a_ref.shape[1]
    o_ref[0:tokens, :] = a_ref[...].T
    o_ref[tokens:, :] = b_ref[...].T


def map_of(first_ref, at, i, hs, cut):
    model = first_ref.shape[2]
    rows = slice(cut, cut + hs // 2)
    return jnp.concatenate(
        [first_ref[at, rows, k * (model // 2) + 128 * i : k * (model // 2) + 128 * i + hs] for k in range(2)], axis=0
    )


def project_body(hp, hs, count, sc, hid_ref, starts_ref, *refs):
    first_refs = refs[0 : 2 * count]
    proj_ref, qf_ref, kf_ref, va_ref, st_ref, w_ref, sems = refs[-7:]
    p = pl.program_id(0)
    wait_for_piece(first_refs, w_ref, sems, sc)
    pc, tokens = proj_ref.shape[1:]
    cut = pc // 2
    bias = column(w_ref[2 * p, cut + hs // 2 : cut + hs // 2 + TILE, 0:pc], 0, tokens)
    for k in range(2):
        rows = slice(k * cut, (k + 1) * cut)
        proj_ref[0, rows, :] = (nn(w_ref[2 * p + k, 0:cut, :], hid_ref[...]) + bias[rows, :]).astype(bf)
    included = (starts_ref[0:1, :] == sc[1]).astype(f32)
    extra = lax.broadcasted_iota(jnp.int32, (AUG - hs, tokens), 0)
    extra = jnp.where(extra < 2, 1.0, 0.0).astype(bf)
    for i in range(hp):
        row = 3 * hs * i
        for part, out in ((0, qf_ref), (1, kf_ref)):
            own_map = map_of(w_ref, 2 * p + part, i, hs, cut)
            logits = tn(own_map, proj_ref[0, row + part * hs : row + (part + 1) * hs, :])
            out[i, 0:hs, :] = soft_columns(logits).astype(bf)
            out[i, hs : 2 * hs, :] = soft_columns(-logits).astype(bf)
        va_ref[i, 0:hs, :] = proj_ref[0, row + 2 * hs : row + 3 * hs, :]
        va_ref[i, hs:AUG, :] = extra
        kept = (va_ref[i].astype(f32) * included).astype(bf)
        st_ref[i] = nt(kept, kf_ref[i]).astype(bf)


def wait_for_piece(first_refs, w_ref, sems, sc):
    p = pl.program_id(0)
    places = part_places(first_refs, w_ref, sc[0])
    rows = w_ref.shape[1]
    copies = [
        pltpu.make_async_copy(ref.at[pl.ds(0, rows), :], place, sems.at[k])
        for k, (ref, place) in enumerate(zip(first_refs, places))
    ]

    @pl.when(p == 0)
    def _():
        for copy in copies:
            copy.start()

    for k, copy in enumerate(copies):

        @pl.when(p == k // 2)
        def _(copy=copy):
            copy.wait()


def local_mix_body(hp, sc, qf_ref, kf_ref, va_ref, starts_ref, num_ref):
    tokens = qf_ref.shape[2]
    starts = starts_ref[...]
    for first, width, rows in causal_pieces(tokens):
        mask = ahead_mask(starts, rows, first, width)
        for i in range(hp):
            scores = tn(kf_ref[i, :, 0:rows], qf_ref[i, :, first : first + width])
            scores = jnp.where(mask, scores, 0.0).astype(bf)
            num_ref[i, :, first : first + width] = nn(va_ref[i, :, 0:rows], scores)


def weighted_state(sc, slot, refs, i, hp):
    total = jnp.where(sc[slot + len(refs) - 1] > 0, refs[-1][i].astype(f32), 0.0)
    for m, ref in enumerate(refs[:-1], 1):
        total += jnp.where(sc[slot + m - 1] > 0, ref[((i // hp) ^ m) * hp + i % hp].astype(f32), 0.0)
    return total


def load_out_weight(sc, first_refs, w_ref, sems):
    rows = w_ref.shape[0] // len(first_refs)
    at = first_refs[0].shape[0] - rows
    places = [
        w_ref.at[pl.ds(pl.multiple_of(rows * (2 * (k // 2) + (sc[0] if k % 2 == 0 else 1 - sc[0])), TILE), rows), :]
        for k in range(len(first_refs))
    ]
    return load_all([ref.at[pl.ds(at, rows), :] for ref in first_refs], places, sems)


def mix_out_body(hp, hs, nh, sc, num_ref, qf_ref, starts_ref, x_ref, gain_ref, *refs):
    state_refs, row_refs, wo_refs = refs[0:nh], refs[nh : 2 * nh], refs[2 * nh : 4 * nh]
    sin_ref, mixd_ref, mix_ref, res_ref, hidt_ref, hid_ref, w_ref, sems = refs[4 * nh :]
    copies = load_out_weight(sc, wo_refs, w_ref, sems)
    uses = starts_ref[0:1, :] < 0
    model, tokens = x_ref.shape
    for i in range(num_ref.shape[0]):
        state = weighted_state(sc, 2, state_refs, i, hp).astype(bf)
        sin_ref[i] = state
        num = num_ref[i] + jnp.where(uses, nn(state, qf_ref[i]), 0.0)
        mixture = num[0:hs, :] / num[hs : hs + 1, :]
        mixd_ref[i, 0:hs, :] = mixture
        mixd_ref[i, hs : hs + 8, :] = num[hs : hs + 8, :]
        mix_ref[i * hs : (i + 1) * hs, :] = mixture.astype(bf)
    for copy in copies:
        copy.wait()
    res_ref[...] = x_ref[...].astype(f32) + tn(w_ref[...], mix_ref[...])
    width = model // nh
    h = sc[2 + 2 * nh]
    for j in range(nh):
        rows = pl.ds(pl.multiple_of((h ^ j) * width, TILE), width)
        res_ref[rows, :] += column(row_refs[j][:, 0:width], 2, tokens)
    normed, _ = norm_columns(res_ref[...].astype(bf).astype(f32))
    gains = gain_ref[...]
    hidden = (normed * column(gains, 2, tokens) + column(gains, 3, tokens)).astype(bf)
    hidt_ref[...] = hidden
    hid_ref[...] = hidden.T


def feed_body(count, first, sc, *refs):
    hid_ins, hidt_ins, gyt_ins, gy_in = refs[0:2], refs[2:4], refs[4:6], refs[6]
    row_refs = refs[7 : 7 + count]
    w_ins = refs[7 + count : 7 + 3 * count]
    refs = refs[7 + 3 * count :]
    if first:
        out_ref, sg_ref = refs[0:2]
        refs = refs[2:]
    else:
        out_in, sg_in, out_own, out_peer, sg_own, sg_peer = refs[0:6]
        refs = refs[6:]
    w_refs, ub_ref, refs = refs[0:count], refs[count], refs[count + 1 :]
    hid_ref, hidt_ref, gyt_ref, gy_ref, down_ref, up_ref, act_ref, ug_ref, sems = refs
    tokens, model = hid_ins[0].shape
    half = act_ref.shape[1]
    runs = [slice(0, tokens), slice(tokens, 2 * tokens)]
    left, right = pl.ds(0, half), pl.ds(half, half)
    soon = w_ins[0].shape[0]
    rest = half - soon
    tops, lows = w_ins[0::2], w_ins[1::2]
    parts = [
        ([a.at[:, left], b.at[:, left], a.at[:, right], b.at[pl.ds(0, rest), right], b.at[pl.ds(rest, half), right]],
         [up_ref.at[k, pl.ds(0, soon), :], up_ref.at[k, pl.ds(soon, model - soon), :], down_ref.at[k, pl.ds(0, soon), left],
          down_ref.at[k, pl.ds(soon, rest), left], down_ref.at[k, :, right]])
        for k, (a, b) in enumerate(zip(tops, lows))
    ]
    load = [
        load_all([hid_ins[0], *parts[0][0][0:2], gy_in.at[pl.ds(0, tokens), :], *parts[0][0][2:]],
                 [hid_ref.at[pl.ds(0, tokens), :], *parts[0][1][0:2], gy_ref.at[pl.ds(0, tokens), :], *parts[0][1][2:]],
                 sems.at[0]),
        load_all([hid_ins[1], gy_in.at[pl.ds(tokens, tokens), :]],
                 [hid_ref.at[pl.ds(tokens, tokens), :], gy_ref.at[pl.ds(tokens, tokens), :]], sems.at[1]),
        load_all([*hidt_ins, *gyt_ins],
                 [a.at[:, pl.ds(k * tokens, tokens)] for a in (hidt_ref, gyt_ref) for k in range(2)], sems.at[2]),
    ]
    if count > 1:
        load.append(load_all([a for p in parts[1:] for a in p[0]], [a for p in parts[1:] for a in p[1]], sems.at[3]))
    at_half = pl.ds(pl.multiple_of(sc[0] * half, 128), half)
    for k in range(count):
        bias = row_refs[k][:, at_half].astype(f32)[1:2, :]
        if k == 1:
            for copy in load[3]:
                copy.wait()
        for which, rows in enumerate(runs):
            if k == 0:
                for copy in load[which]:
                    copy.wait()
            value, slope = gelu_pair(nn(hid_ref[rows, :], up_ref[k]) + bias)
            act_ref[rows, :] = value.astype(bf)
            ug_ref[rows, :] = (nt(gy_ref[rows, :], down_ref[k]) * slope).astype(bf)
        if k == 0:
            for copy in load[2]:
                copy.wait()
        ub_ref[k] = nn(jnp.ones((8, 2 * tokens), bf), ug_ref[...])
        w_refs[k][0:model, :] = nn(hidt_ref[...], ug_ref[...]).astype(bf)
        w_refs[k][model:, :] = nn(gyt_ref[...], act_ref[...]).astype(bf)
        if first and k == 0:
            out_ref[...] = nn(act_ref[...], down_ref[k])
            sg_ref[...] = nt(up_ref[k], ug_ref[...])
        elif first:
            out_ref[...] += nn(act_ref[...], down_ref[k])
            sg_ref[...] += nt(up_ref[k], ug_ref[...])
        else:
            sg_own[...] = sg_in[:, runs[0]] + nt(up_ref[k], ug_ref[runs[0], :])
            sg_peer[...] = (sg_in[:, runs[1]] + nt(up_ref[k], ug_ref[runs[1], :])).astype(bf)
            out_own[...] = out_in[runs[0], :] + nn(act_ref[runs[0], :], down_ref[k])
            out_peer[...] = (out_in[runs[1], :] + nn(act_ref[runs[1], :], down_ref[k])).astype(bf)


def block_out_body(nh, sc, res_ref, out_ref, out2_ref, tg_ref, *refs):
    row_refs, o_ref, total_ref = refs[0:nh], refs[nh], refs[nh + 1]
    model, tokens = res_ref.shape
    width = model // nh
    total_ref[...] = res_ref[...] + (out_ref[...] + out2_ref[...].astype(f32)).T
    h = sc[2 + 2 * nh]
    for j in range(nh):
        rows = pl.ds(pl.multiple_of((h ^ j) * width, TILE), width)
        o_ref[j, 1] = tg_ref[j]
        o_ref[h ^ j, 0] = (total_ref[rows, :] + column(row_refs[j][:, 0:width], 3, tokens)).astype(bf)


def lay_out_body(nh, sc, in_ref, *o_refs):
    tokens = in_ref.shape[3]
    for k in range(2):
        for q in range(nh):
            o_refs[k][:, q * tokens : (q + 1) * tokens] = in_ref[q, k]


def second_back_body(hs, nh, sc, sg_ref, sg2_ref, res_ref, gyt_ref, gain_ref, mixd_ref, starts_ref, qf_ref, *refs):
    wo_refs, (rg_ref, ag_ref, vec_ref, na_ref, sgt_ref, w_ref, sems) = refs[0 : 2 * nh], refs[2 * nh :]
    copies = load_out_weight(sc, wo_refs, w_ref, sems)
    model, tokens = sg_ref.shape
    width = model // nh
    normed, inv_std = norm_columns(res_ref[...].astype(bf).astype(f32))
    sg = sg_ref[...] + sg2_ref[...].astype(f32)
    res_grad = gyt_ref[...].astype(f32) + norm_columns_back(sg, normed, inv_std, column(gain_ref[...], 2, tokens))
    rg_ref[...] = res_grad
    ag_ref[...] = res_grad.astype(bf)
    uses = (starts_ref[0:1, :] < 0).astype(f32)
    for copy in copies:
        copy.wait()
    mg = nn(w_ref[...], ag_ref[...])
    row = lax.broadcasted_iota(jnp.int32, (AUG - hs, tokens), 0)
    for i in range(qf_ref.shape[0]):
        num = mg[i * hs : (i + 1) * hs, :] / mixd_ref[i, hs : hs + 1, :]
        den = -jnp.sum(num * mixd_ref[i, 0:hs, :], axis=0, keepdims=True)
        high = den.astype(bf).astype(f32)
        extra = jnp.where(row == 0, high, jnp.where(row == 1, den - high, 0.0))
        na_ref[i, 0:hs, :] = num.astype(bf)
        na_ref[i, hs:AUG, :] = extra.astype(bf)
        kept = (na_ref[i].astype(f32) * uses).astype(bf)
        sgt_ref[i] = nt(kept, qf_ref[i]).astype(bf)
    for at, value in enumerate((sg * normed, sg, ag_ref[...], gyt_ref[...])):
        sums = row_sums(value)
        for p in range(nh):
            vec_ref[p, at : at + 1, :] = sums[0:1, p * width : (p + 1) * width]


def halves_back(feat, grad, hs):
    parts = []
    for k in range(2):
        soft = feat[k * hs : (k + 1) * hs, :].astype(f32)
        own = grad[k * hs : (k + 1) * hs, :]
        weight = jnp.sum(soft * own, axis=0, keepdims=True) / jnp.sum(soft, axis=0, keepdims=True)
        parts.append(soft * (own - weight))
    return (parts[0] - parts[1]).astype(bf)


def local_back_body(hp, hs, sc, qf_ref, kf_ref, va_ref, na_ref, sin_ref, starts_ref, ql_ref, kfg_ref, vg_ref):
    tokens = qf_ref.shape[2]
    starts = starts_ref[...]
    step = tokens // 2
    uses = starts[0:1, :] < 0
    masks = [ahead_mask(starts, rows, first, width) for first, width, rows in causal_pieces(tokens)]
    for i in range(hp):
        na = na_ref[i]
        through = tn(sin_ref[i], na)
        for which, (first, width, rows) in enumerate(causal_pieces(tokens)):
            at = slice(first, first + width)
            mask = masks[which]
            scores = jnp.where(mask, tn(kf_ref[i, :, 0:rows], qf_ref[i, :, at]), 0.0).astype(bf)
            sgrad = jnp.where(mask, tn(va_ref[i, :, 0:rows], na[:, at]), 0.0).astype(bf)
            qfg = nn(kf_ref[i, :, 0:rows], sgrad) + jnp.where(uses[:, at], through[:, at], 0.0)
            ql_ref[i, :, at] = halves_back(qf_ref[i, :, at], qfg, hs)
            kfg = nt(qf_ref[i, :, at], sgrad)
            vg = nt(na[:, at], scores)[0:hs, :]
            if which == 0:
                kfg_ref[i, :, 0:rows] = kfg
                vg_ref[i, :, 0:rows] = vg
            else:
                kfg_ref[i, :, 0:step] += kfg[:, 0:step]
                vg_ref[i, :, 0:step] += vg[:, 0:step]
                kfg_ref[i, :, step:] = kfg[:, step:]
                vg_ref[i, :, step:] = vg[:, step:]


def join_extra(state, hs):
    row = lax.broadcasted_iota(jnp.int32, state.shape, 0)
    both = state[hs : hs + 1, :] + state[hs + 1 : hs + 2, :]
    return jnp.where(row < hs, state, jnp.where(row == hs, both, 0.0))


def project_back_body(hp, hs, nh, sc, *refs):
    state_refs, first_refs, refs = refs[0:nh], refs[nh : 3 * nh], refs[3 * nh :]
    kf_ref, va_ref, ql_ref, kfg_ref, vg_ref, proj_ref, starts_ref, *pg_refs, fg_ref, mg_ref, pb_ref, pg_ref, first_ref, sems = refs
    p = pl.program_id(0)
    wait_for_piece(first_refs, first_ref, sems, sc)
    included = starts_ref[0:1, :] == sc[1]
    cut = pg_ref.shape[1] // 2
    for i in range(hp):
        total = jnp.where(sc[1 + 2 * nh] > 0, state_refs[-1][i].astype(f32), 0.0)
        for m in range(1, nh):
            total += jnp.where(sc[1 + nh + m] > 0, state_refs[m - 1][i].astype(f32), 0.0)
        state = join_extra(total, hs).astype(bf)
        kfg = kfg_ref[i] + jnp.where(included, tn(state, va_ref[i]), 0.0)
        vg = vg_ref[i] + jnp.where(included, nn(state, kf_ref[i])[0:hs, :], 0.0)
        klg = halves_back(kf_ref[i], kfg, hs)
        qlg = ql_ref[i]
        row = 3 * hs * i
        pg_ref[0, row : row + hs, :] = nn(map_of(first_ref, 2 * p, i, hs, cut), qlg).astype(bf)
        pg_ref[0, row + hs : row + 2 * hs, :] = nn(map_of(first_ref, 2 * p + 1, i, hs, cut), klg).astype(bf)
        pg_ref[0, row + 2 * hs : row + 3 * hs, :] = vg.astype(bf)
        q_grad = nt(proj_ref[0, row : row + hs, :], qlg)
        k_grad = nt(proj_ref[0, row + hs : row + 2 * hs, :], klg)
        mg_ref[0, :, 128 * i : 128 * (i + 1)] = jnp.concatenate([q_grad, k_grad], axis=1)
    for j, ref in enumerate(pg_refs):

        @pl.when(p == j)
        def _(ref=ref):
            ref[...] = pg_ref[0]

    pb_ref[0] = row_sums(pg_ref[0])
    grad = tn(first_ref[2 * p, 0:cut, :], pg_ref[0, 0:cut, :]) + tn(first_ref[2 * p + 1, 0:cut, :], pg_ref[0, cut:, :])

    @pl.when(pl.program_id(0) == 0)
    def _():
        fg_ref[...] = grad

    @pl.when(pl.program_id(0) > 0)
    def _():
        fg_ref[...] += grad


def first_back_body(nh, sc, fg_ref, x_ref, rg_ref, gain_ref, tg_ref, vec_ref):
    model, tokens = fg_ref.shape
    width = model // nh
    normed, inv_std = norm_columns(x_ref[...].astype(f32))
    fg = fg_ref[...]
    gain = column(gain_ref[...], 0, tokens)
    tg = (rg_ref[...] + norm_columns_back(fg, normed, inv_std, gain)).astype(bf)
    for p in range(nh):
        tg_ref[p] = tg[p * width : (p + 1) * width, :]
    for at, value in enumerate((fg * normed, fg)):
        sums = row_sums(value)
        for p in range(nh):
            vec_ref[p, at : at + 1, :] = sums[0:1, p * width : (p + 1) * width]


def out_grads_body(nh, sc, mix_ref, mix2_ref, ag_ref, ag2_ref, o_ref):
    width = o_ref.shape[1]
    h = sc[2 + 2 * nh]
    for j in range(nh):
        rows = slice(j * width, (j + 1) * width)
        o_ref[h ^ j] = (nt(mix_ref[rows, :], ag_ref[...]) + nt(mix2_ref[rows, :], ag2_ref[...])).astype(bf)


def feed_sum_body(nh, nz, sc, *refs):
    w_refs, out_ref, keep_ref, send_ref, total_ref = refs[0:nh], *refs[nh:]
    rows = w_refs[0].shape[0]
    total_ref[0:rows, :] = sum(ref[...].astype(f32) for ref in w_refs).astype(bf)
    total_ref[rows:, :] = sum(out_ref[k].astype(f32) for k in range(nh)).astype(bf)
    z = sc[3 + 2 * nh]
    part = total_ref.shape[0] // nz
    for k in range(nz):
        o_ref = keep_ref if k % 2 == 0 else send_ref
        rows = slice((k // 2) * part, (k // 2 + 1) * part)
        o_ref[rows, :] = total_ref[pl.ds(pl.multiple_of((z ^ k) * part, TILE), part), :]


def pair_sum_body(sc, own_ref, got_ref, keep_ref, send_ref):
    part = keep_ref.shape[0]
    keep_ref[...] = (own_ref[0:part, :].astype(f32) + got_ref[0:part, :].astype(f32)).astype(bf)
    send_ref[...] = (own_ref[part:, :].astype(f32) + got_ref[part:, :].astype(f32)).astype(bf)


def last_grads_body(nh, sc, *refs):
    pg_refs, pg2_refs, refs = refs[0:nh], refs[nh : 2 * nh], refs[2 * nh :]
    hid_ref, hid2_ref, mg_ref, pb_ref, early_ref, late_ref, vec1_ref, vec2_ref, *o_refs, rows_ref = refs
    pc, half = pg_refs[0].shape[0], hid_ref.shape[0]
    hs = mg_ref.shape[1]
    width = vec1_ref.shape[2]
    h = sc[2 + 2 * nh]
    for j in range(nh):
        o_ref = o_refs[j]
        o_ref[0:pc, :] = (nt(pg_refs[j][...], hid_ref[...]) + nt(pg2_refs[j][...], hid2_ref[...])).astype(bf)
        o_ref[pc : pc + hs, :] = mg_ref[j].astype(bf)
        ub_ref, k = (early_ref, j) if j < nh - 1 else (late_ref, 0)
        rows_ref[...] = jnp.zeros_like(rows_ref)
        rows_ref[0:1, :] = pb_ref[j, 0:1, 0:half]
        rows_ref[1:2, 0 : pc - half] = pb_ref[j, 0:1, half:]
        rows_ref[2:3, :] = jnp.where(sc[0] == 0, ub_ref[k, 0:1, :], 0.0)
        rows_ref[3:4, :] = jnp.where(sc[0] == 0, 0.0, ub_ref[k, 0:1, :])
        rows_ref[4:8, 0:width] = vec2_ref[h ^ j, 0:4, :]
        rows_ref[8:10, 0:width] = vec1_ref[h ^ j, 0:2, :]
        o_ref[pc + hs :, :] = rows_ref[...].astype(bf)


def feed_out_body(nh, nz, sc, *refs):
    up_ref, down_ref, out_ref, total_ref = refs[2 * nz :]
    z = sc[3 + 2 * nh]
    part = refs[0].shape[0]
    for k in range(2 * nz):
        total_ref[k // nz, pl.ds(pl.multiple_of((z ^ (k % nz)) * part, TILE), part), :] = refs[k][...]
    model = down_ref.shape[1]
    half = total_ref.shape[2]
    for k, core in enumerate((sc[0], 1 - sc[0])):
        at = pl.ds(pl.multiple_of(core * half, 128), half)
        up_ref[:, at] = total_ref[k, 0:model, :].astype(f32)
        down_ref[at, :] = total_ref[k, model : 2 * model, :].astype(f32).T
        out_ref[:, at] = total_ref[k, 2 * model :, :].astype(f32)


def last_out_body(hs, sc, mine_ref, theirs_ref, qkv_ref, qm_ref, km_ref, qb_ref, ub_ref, vec_ref):
    pc = qkv_ref.shape[0]
    half = mine_ref.shape[1]
    for core, ref in ((sc[0], mine_ref), (1 - sc[0], theirs_ref)):
        at = pl.ds(pl.multiple_of(core * half, 128), half)
        qkv_ref[:, at] = ref[0:pc, :].astype(f32)
    maps = mine_ref[pc : pc + hs, :].astype(f32) + theirs_ref[pc : pc + hs, :].astype(f32)
    for i in range(qm_ref.shape[0]):
        qm_ref[i] = maps[:, 128 * i : 128 * i + hs]
        km_ref[i] = maps[:, 128 * i + hs : 128 * i + 2 * hs]
    rows = slice(pc + hs, pc + hs + TILE)
    rows = mine_ref[rows, :].astype(f32) + theirs_ref[rows, :].astype(f32)
    qb_ref[:, 0:half] = rows[0:1, :]
    qb_ref[:, half:] = rows[1:2, 0 : pc - half]
    ub_ref[:, 0:half] = rows[2:3, :]
    ub_ref[:, half:] = rows[3:4, :]
    vec_ref[...] = rows


def swap(a, axis, k):
    n = lax.axis_size(axis)
    return lax.ppermute(a, axis, [(i, i ^ k) for i in range(n)])


def trade(a, axis):
    return lax.all_to_all(a, axis, 0, 0, tiled=True)


def after(a, *others):
    return lax.optimization_barrier((a,) + others)[0]


def chain_seq(part, forward, weight_of):
    n = lax.axis_size("seq")
    total = None
    for k in range(1, n):
        pairs = [(i, i + k) if forward else (i + k, i) for i in range(n - k)]
        if n == 2:
            return lax.ppermute(part, "seq", pairs)
        sent = part if forward else part * weight_of(k).astype(part.dtype)
        got = lax.ppermute(sent, "seq", pairs).astype(f32) * (weight_of(k) if forward else 1.0)
        total = got if total is None else total + got
    return total.astype(bf)


def local(tokens, attn_gain, attn_shift, qkv_weight, qkv_bias, query_map, key_map, out_weight, out_bias,
          mlp_gain, mlp_shift, up_weight, up_bias, down_weight, down_bias, positions, out_grad):
    nh, ns, nz = lax.axis_size("head"), lax.axis_size("seq"), lax.axis_size("dp")
    length, width = tokens.shape[1], tokens.shape[2]
    model = width * nh
    half = model // 2
    hp, hs = query_map.shape[0], query_map.shape[1]
    heads = hp * nh
    pc = qkv_weight.shape[1]
    hidden = up_weight.shape[1]
    hh = hidden // 2
    tok = length // nh
    h = lax.axis_index("head")
    s2 = lax.axis_index("seq") % 2
    peers = range(1, nh)

    run = positions[0]
    start_of = jnp.arange(length, dtype=jnp.int32) - run
    chunk_starts = lax.dynamic_slice_in_dim(start_of, h * tok, tok, 0) - h * tok
    starts = jnp.broadcast_to(chunk_starts[None, :], (8, tok))
    firsts = start_of[::tok]
    run_last = start_of[length - 1]
    other = [h ^ m for m in range(nh)]
    fwd = [(other[m] < h) & (firsts[h] <= (other[m] + 1) * tok - 1) for m in peers]
    bwd = [(other[m] > h) & (firsts[other[m]] <= (h + 1) * tok - 1) for m in peers]
    sc = jnp.stack(
        [s2, chunk_starts[tok - 1]]
        + [a.astype(jnp.int32) for a in fwd]
        + [(firsts[h] < 0).astype(jnp.int32)]
        + [a.astype(jnp.int32) for a in bwd]
        + [(run_last <= (h + 1) * tok - 1).astype(jnp.int32), h, lax.axis_index("dp")]
    ).astype(jnp.int32)

    def beyond_chip(total):
        base = total
        for k in range(1, ns // 2):
            total += lax.ppermute(base, "seq", [(i, (i + 2 * k) % ns) for i in range(ns)])
        return total

    both = jnp.concatenate([a[0].T.reshape(width, nh, tok).transpose(1, 0, 2) for a in (tokens, out_grad)])
    both = both.reshape(2, nh, width, tok).transpose(1, 0, 2, 3)
    both = trade(both, "head")

    core_of = jnp.full((1,), s2, jnp.int32)
    gains = jnp.pad(jnp.stack([attn_gain, attn_shift, mlp_gain, mlp_shift]), ((0, TILE - 4), (0, 0)))
    fl = pc // 2 + hs // 2 + TILE
    fr = fl + width // 2
    soon = hh - TILE
    own, other_half, wa_own, wb_own = run_kernel(
        pack_body, "pack_weights", (1,), core_of,
        [(a, None) for a in (qkv_weight.T, query_map.reshape(-1, hs), key_map.reshape(-1, hs), qkv_bias[None], up_bias[None],
                             out_bias[None], down_bias[None], out_weight, up_weight, down_weight)],
        [(shape((fr, model), bf), None), (shape((fr, model), bf), None), (shape((soon, 2 * hh), bf), None), (shape((2 * hh - soon, 2 * hh), bf), None)],
        scratch=[pltpu.VMEM((TILE, model), f32)],
    )
    x, gyt = [both[:, k].reshape(model, tok) for k in range(2)]
    own = after(own, sc)
    first_got = [swap(own, "head", m) for m in peers]
    x, gyt = after(x, *first_got[:-1]), after(gyt, *first_got[:-1])
    gyt_peer = swap(gyt, "seq", 1)
    (hid,) = run_kernel(
        first_norm_body, "first_norm", (1,), core_of, [(x, None), (gains, None)], [(shape((model, tok), bf), None)]
    )
    hid_peer = swap(lax.dynamic_slice_in_dim(hid, (1 - s2) * half, half, 0), "seq", 1)
    (gy,) = run_kernel(
        turn_body, "turn_grad", (1,), core_of, [(gyt, None), (gyt_peer, None)], [(shape((2 * tok, model), bf), None)]
    )
    firsts_of = [[own, other_half]] + [[a, swap(after(a, hid), "seq", 1)] for a in first_got[:-1]]
    row_specs = [(pair[0], pl.BlockSpec((TILE, model), lambda *_: (fl // TILE - 1, 0))) for pair in firsts_of + [first_got[-1:]]]
    in_hbm = lambda arrays: [(a, HBM) for a in arrays]
    first_scratch = [pltpu.VMEM((2 * nh, fl, model), bf), pltpu.SemaphoreType.DMA((2 * nh,))]
    wo_scratch = [pltpu.VMEM((model, model), bf), pltpu.SemaphoreType.DMA((2 * nh,))]

    va_spec, state_spec, feat_spec = lead(hp, AUG, tok), lead(hp, AUG, 2 * hs), lead(hp, 2 * hs, tok)
    hid_now = after(hid, gyt_peer, hid_peer)

    def project(first_piece, count, so_far):
        def at(spec):
            return pl.BlockSpec(spec.block_shape, lambda p, sc: (p + first_piece,) + (0,) * (len(spec.block_shape) - 1))

        outs = [(shape((nh, pc, tok), bf), at(lead(1, pc, tok))), (shape((heads, 2 * hs, tok), bf), at(feat_spec)),
                (shape((heads, 2 * hs, tok), bf), at(feat_spec)), (shape((heads, AUG, tok), bf), at(va_spec)),
                (shape((heads, AUG, 2 * hs), bf), at(state_spec))]
        arrays = [a for pair in firsts_of[first_piece : first_piece + count] for a in pair]
        return run_kernel(
            functools.partial(project_body, hp, hs, count), f"project_{first_piece}", (count,), sc,
            [(hid_now, None), (starts, None)] + in_hbm(arrays) + in_hbm(so_far), outs,
            scratch=[pltpu.VMEM((2 * count, fl, model), bf), pltpu.SemaphoreType.DMA((2 * count,))],
            aliases={3 + 2 * count + k: k for k in range(len(so_far))},
        )

    so_far = project(0, nh - 1, ())
    far = after(first_got[-1], so_far[-1])
    firsts_of.append([far, after(swap(far, "seq", 1), so_far[-1])])
    all_first = [a for pair in firsts_of for a in pair]
    proj, qf, kf, va, states = project(nh - 1, 1, so_far)
    wa_own = after(wa_own, *first_got[:-1])
    wa_x, wa_y = swap(wa_own, "head", 1), swap(wa_own, "head", 2)
    (num,) = run_kernel(
        functools.partial(local_mix_body, hp), "local_mix", (nh,), sc,
        [(qf, feat_spec), (kf, feat_spec), (after(va, gy, wa_x, wa_y), va_spec), (starts, None)],
        [(shape((heads, AUG, tok), f32), va_spec)],
    )
    around = [after(swap(states, "head", m), num) for m in peers]

    def to_own_pieces(a, m):
        a = a.reshape(nh, hp, AUG, 2 * hs)
        return jnp.stack([a[j ^ m] for j in range(nh)]).reshape(heads, AUG, 2 * hs)

    ends_in = [(run_last <= (other[m] + 1) * tok - 1).astype(f32) for m in range(nh)]
    whole_run = sum(to_own_pieces(a, m).astype(f32) * ends_in[m] for m, a in enumerate([states] + around)).astype(bf)
    before = chain_seq(whole_run, True, lambda k: (start_of[0] <= -(k - 1) * length - 1).astype(f32))

    wb_own = after(wb_own, *around)
    wb_x, wb_y = swap(wb_own, "head", 1), swap(wb_own, "head", 2)
    w_all = [[wa_own, wb_own], [wa_x, wb_x], [wa_y, wb_y], [swap(wa_x, "head", 2), swap(wb_y, "head", 1)]]

    sin, mixd, mix, res, hidt2, hid2 = run_kernel(
        functools.partial(mix_out_body, hp, hs, nh), "mix_out", (1,), sc,
        [(a, None) for a in (num, after(qf, wb_x, wb_y), starts, x, gains, *around, before)] + row_specs + in_hbm(all_first),
        [(shape((heads, AUG, 2 * hs), bf), None), (shape((heads, hs + 8, tok), f32), None), (shape((model, tok), bf), None),
         (shape((model, tok), f32), None), (shape((model, tok), bf), None), (shape((tok, model), bf), None)],
        scratch=wo_scratch,
    )
    hidt2_peer, hid2_peer = [swap(a, "seq", 1) for a in (hidt2, hid2)]

    all_rows = 2 * model + width

    def feed(which, sums):
        count = len(which)
        if sums:
            outs = [shape((tok, model), f32), shape((tok, model), bf), shape((model, tok), f32), shape((model, tok), bf)]
        else:
            outs = [shape((2 * tok, model), f32), shape((model, 2 * tok), f32)]
        return run_kernel(
            functools.partial(feed_body, count, not sums), f"feed_{which[0]}", (1,), sc,
            in_hbm([hid2, hid2_peer, hidt2, hidt2_peer, gyt, gyt_peer, gy]) + [row_specs[j] for j in which]
            + in_hbm([a for j in which for a in w_all[j]]) + [(a, None) for a in sums],
            [(a, None) for a in outs] + [(shape((2 * model, hh), bf), None)] * count + [(shape((count, 8, hh), f32), None)],
            scratch=[pltpu.VMEM((2 * tok, model), bf), pltpu.VMEM((model, 2 * tok), bf), pltpu.VMEM((model, 2 * tok), bf),
                     pltpu.VMEM((2 * tok, model), bf), pltpu.VMEM((count, hh, model), bf), pltpu.VMEM((count, model, hh), bf),
                     pltpu.VMEM((2 * tok, hh), bf), pltpu.VMEM((2 * tok, hh), bf),
                     pltpu.SemaphoreType.DMA((4, 5 * nh))],
        )

    part_out, part_sg, *early = feed(list(range(nh - 1)), ())
    w_parts, early_ub = early[:-1], early[-1]
    w_got = [swap(w_parts[m], "head", m) for m in range(1, nh - 1)]
    mix_peer = swap(after(mix, early_ub), "seq", 1)
    out_own, out_send, sg_own, sg_send, w_last, late_ub = feed([nh - 1], (part_out, part_sg))
    sg_recv = swap(sg_send, "seq", 1)

    vec_block = (shape((nh, 8, width), f32), None)
    rg, ag, vec2, na, sgt = run_kernel(
        functools.partial(second_back_body, hs, nh), "second_back", (1,), sc,
        [(a, None) for a in (sg_own, sg_recv, res, gyt, gains, mixd, starts, qf)] + in_hbm(all_first),
        [(shape((model, tok), f32), None), (shape((model, tok), bf), None), vec_block,
         (shape((heads, AUG, tok), bf), None), (shape((heads, AUG, 2 * hs), bf), None)],
        scratch=wo_scratch,
    )
    g_sent = [swap(sgt, "head", m) for m in peers]
    half_spec = pl.BlockSpec((half, tok), lambda p, sc: (sc[0], 0))
    ag_peer = swap(lax.dynamic_slice_in_dim(ag, (1 - s2) * half, half, 0), "seq", 1)
    (out_part,) = run_kernel(
        functools.partial(out_grads_body, nh), "out_grads", (1,), sc,
        [(after(mix, *w_got), None), (mix_peer, None), (ag, half_spec), (ag_peer, None)], [(shape((nh, width, half), bf), None)],
    )

    na_late = after(na, out_part)
    ql, kfg, vg = run_kernel(
        functools.partial(local_back_body, hp, hs), "local_back", (nh,), sc,
        [(qf, feat_spec), (kf, feat_spec), (va, va_spec), (na_late, va_spec), (sin, state_spec), (starts, None)],
        [(shape((heads, hs, tok), bf), lead(hp, hs, tok)), (shape((heads, 2 * hs, tok), f32), feat_spec),
         (shape((heads, hs, tok), f32), lead(hp, hs, tok))],
    )
    g_around = [after(a, ql) for a in g_sent]
    w_got.append(swap(after(w_last, *g_around), "head", nh - 1))
    out_got = trade(out_part, "head")
    begins_in = [(firsts[other[m]] < 0).astype(f32) for m in range(nh)]
    g_whole = sum(to_own_pieces(a, m).astype(f32) * begins_in[m] for m, a in enumerate([sgt] + g_around)).astype(bf)
    after_run = chain_seq(g_whole, False, lambda k: (start_of[0] <= -(k - 1) * length - 1).astype(f32))
    def peer_states(a, m):
        return (a, pl.BlockSpec((hp, AUG, 2 * hs), lambda p, sc: (p ^ m, 0, 0)))

    *pg, fg, map_grads, pb = run_kernel(
        functools.partial(project_back_body, hp, hs, nh), "project_back", (nh,), sc,
        [peer_states(a, m) for a, m in zip(g_around + [after_run], [*peers, 0])] + in_hbm(all_first)
        + [(kf, feat_spec), (va, va_spec), (ql, lead(hp, hs, tok)), (after(kfg, out_got), feat_spec), (vg, lead(hp, hs, tok)),
           (proj, lead(1, pc, tok)), (starts, None)],
        [(shape((pc, tok), bf), None)] * nh
        + [(shape((model, tok), f32), None),
           (shape((nh, hs, 128 * hp), f32), lead(1, hs, 128 * hp)), (shape((nh, 8, pc), f32), lead(1, 8, pc))],
        scratch=[pltpu.VMEM((1, pc, tok), bf)] + first_scratch,
    )
    pg_peer = [swap(a, "seq", 1) for a in pg]
    tg, vec1 = run_kernel(
        functools.partial(first_back_body, nh), "first_back", (1,), sc,
        [(fg, None), (x, None), (rg, None), (gains, None)], [(shape((nh, width, tok), bf), None), vec_block],
    )
    last_rows = -(-(pc + hs + TILE) // (nz * TILE)) * nz * TILE
    last_parts = run_kernel(
        functools.partial(last_grads_body, nh), "last_grads", (1,), sc,
        [(a, None) for a in (*pg, *pg_peer)] + [(hid, half_spec), (hid_peer, None)]
        + [(a, None) for a in (after(map_grads, w_got[-1]), pb, early_ub, late_ub, vec1, vec2)],
        [(shape((last_rows, half), bf), None)] * nh,
        scratch=[pltpu.VMEM((last_rows - pc - hs, half), f32)],
    )

    feed_rows = all_rows // nz
    feed_sums = run_kernel(
        functools.partial(feed_sum_body, nh, nz), "feed_sum", (1,), sc,
        [(a, None) for a in (after(w_parts[0], *last_parts), *w_got, out_got)],
        [(shape((2 * feed_rows, hh), bf), None)] * 2, scratch=[pltpu.VMEM((all_rows, hh), bf)],
    )
    feed_sums = [beyond_chip(a) for a in feed_sums]
    feed_got = swap(feed_sums[1], "dp", 1)
    out_recv = swap(after(out_send, *pg), "seq", 1)
    (chunks,) = run_kernel(
        functools.partial(block_out_body, nh), "block_out", (1,), sc,
        [(after(res, *feed_sums), None), (out_own, None), (out_recv, None), (tg, None)] + row_specs,
        [(shape((nh, 2, width, tok), bf), None)], scratch=[pltpu.VMEM((model, tok), f32)],
    )
    last_got = [after(swap(last_parts[m], "head", m), chunks, *feed_sums).astype(f32) for m in peers]
    total = beyond_chip(sum(last_got) + last_parts[0].astype(f32)).astype(bf)
    pair = (total.astype(f32) + after(swap(total, "dp", 1), feed_got).astype(f32)).astype(bf)
    across = lax.ppermute(pair, "dp", [(1, 2), (2, 1)])
    feed_keep, feed_send = run_kernel(
        pair_sum_body, "pair_sum", (1,), sc, [(feed_sums[0], None), (after(feed_got, pair), None)],
        [(shape((feed_rows, hh), bf), None)] * 2,
    )
    feed_far = swap(feed_send, "dp", 2)
    four = (pair.astype(f32) + across.astype(f32)).astype(bf)
    ends = lax.ppermute(four, "dp", [(1, 0), (2, 3)])
    chunks = trade(chunks, "head")
    feed_one = (feed_keep.astype(f32) + after(feed_far, chunks, four).astype(f32)).astype(bf)
    feed_two = swap(feed_one, "dp", 2)
    feed_total = [feed_one, swap(feed_one, "dp", 1), feed_two, swap(feed_two, "dp", 1)]
    z = lax.axis_index("dp")
    last_sum = jnp.where((z == 1) | (z == 2), four, ends)
    block_out, tokens_grad = run_kernel(
        functools.partial(lay_out_body, nh), "lay_out", (1,), sc, [(chunks, None)],
        [(shape((width, length), bf), None)] * 2,
    )
    upweight_grad, downweight_grad, outweight_grad = run_kernel(
        functools.partial(feed_out_body, nh, nz), "feed_result", (1,), sc, [(a, None) for a in feed_total] + [(swap(a, "seq", 1), None) for a in feed_total],
        [(shape((model, hidden), f32), None), (shape((hidden, model), f32), None), (shape((width, model), f32), None)],
        scratch=[pltpu.VMEM((2, all_rows, hh), bf)],
    )
    qkv_grad, query_grad, key_grad, qkvbias_grad, upbias_grad, rows = run_kernel(
        functools.partial(last_out_body, hs), "last_result", (1,), sc, [(last_sum, None), (swap(last_sum, "seq", 1), None)],
        [(shape((pc, model), f32), None), (shape((hp, hs, hs), f32), None), (shape((hp, hs, hs), f32), None),
         (shape((1, pc), f32), None), (shape((1, hidden), f32), None), (shape((TILE, half), f32), None)],
    )
    vec = rows[4:10, 0:width]
    return (block_out.T[None], tokens_grad.T[None], vec[4], vec[5], qkv_grad.T, qkvbias_grad[0], query_grad, key_grad,
            outweight_grad, vec[2], vec[0], vec[1], upweight_grad, upbias_grad[0], downweight_grad, vec[3])


def solution(mesh):
    wide = P("dp", "seq", "head")
    return jax.shard_map(
        local,
        mesh=mesh,
        in_specs=(wide, P(), P(), P(None, "head"), P("head"), P("head", None, None), P("head", None, None),
                  P("head", None), P("head"), P(), P(), P(None, "head"), P("head"), P("head", None), P("head"),
                  P("dp", "seq"), wide),
        out_specs=(wide, wide, P("head"), P("head"), P(None, "head"), P("head"), P("head", None, None),
                   P("head", None, None), P("head", None), P("head"), P("head"), P("head"), P(None, "head"), P("head"),
                   P("head", None), P("head")),
        check_vma=False,
    )
```

```python
import functools

import jax
import jax.numpy as jnp
from jax import lax
from jax.experimental import pallas as pl
from jax.experimental.pallas import tpu as pltpu
from jax.sharding import PartitionSpec as P

eps = 1e-05
gelu_scale = 0.7978845608028654
bf = jnp.bfloat16
f32 = jnp.float32
AUG = 80
TILE = 16


def nn(a, b):
    return lax.dot_general(a, b, (((1,), (0,)), ((), ())), preferred_element_type=f32)


def nt(a, b):
    return lax.dot_general(a, b, (((1,), (1,)), ((), ())), preferred_element_type=f32)


def tn(a, b):
    return lax.dot_general(a, b, (((0,), (0,)), ((), ())), preferred_element_type=f32)


def shape(dims, dtype):
    return jax.ShapeDtypeStruct(tuple(dims), dtype)


def whole(a):
    dims = tuple(a.shape)
    return pl.BlockSpec(dims, lambda *_: (0,) * len(dims))


def lead(count, *dims):
    return pl.BlockSpec((count,) + dims, lambda p, sc: (p,) + (0,) * len(dims))


def run_kernel(body, name, grid, scalars, ins, outs, scratch=(), aliases=None):
    return pl.pallas_call(
        body,
        out_shape=[o for o, _ in outs],
        grid_spec=pltpu.PrefetchScalarGridSpec(
            num_scalar_prefetch=1,
            grid=grid,
            in_specs=[spec or whole(a) for a, spec in ins],
            out_specs=[spec or whole(o) for o, spec in outs],
            scratch_shapes=list(scratch),
        ),
        compiler_params=pltpu.CompilerParams(vmem_limit_bytes=18 * 2**20),
        cost_estimate=pl.CostEstimate(flops=0, bytes_accessed=0, transcendentals=0),
        input_output_aliases=aliases or {},
        name=name,
    )(scalars, *[a for a, _ in ins])


def norm_columns(values):
    center = values - jnp.mean(values, axis=0, keepdims=True)
    inv_std = lax.rsqrt(jnp.mean(center * center, axis=0, keepdims=True) + eps)
    return center * inv_std, inv_std


def norm_columns_back(grad, normed, inv_std, gain):
    scaled = grad * gain
    return inv_std * (
        scaled
        - jnp.mean(scaled, axis=0, keepdims=True)
        - normed * jnp.mean(scaled * normed, axis=0, keepdims=True)
    )


def column(rows, at, width):
    only = jnp.where(lax.broadcasted_iota(jnp.int32, rows.shape, 0) == at, rows.astype(f32), 0.0).astype(bf)
    upright = tn(only, jnp.ones((TILE, 128), bf))
    return jnp.concatenate([upright] * (width // 128), axis=1)


def row_sums(values):
    ones = jnp.ones((8, values.shape[1]), bf)
    if values.dtype == bf:
        return nt(ones, values)
    high = values.astype(bf)
    return nt(ones, high) + nt(ones, (values - high.astype(f32)).astype(bf))


def gelu_pair(up_pre):
    square = up_pre * up_pre
    tanh_value = jnp.tanh(gelu_scale * (up_pre + 0.044715 * square * up_pre))
    half_one = 0.5 * (1.0 + tanh_value)
    slope = half_one + 0.5 * up_pre * (1.0 - tanh_value * tanh_value) * gelu_scale * (
        1.0 + 3.0 * 0.044715 * square
    )
    return up_pre * half_one, slope


def soft_columns(logits):
    top = jnp.exp(logits - jnp.max(logits, axis=0, keepdims=True))
    return top / jnp.sum(top, axis=0, keepdims=True)


def ahead_mask(starts, rows, first_column, columns):
    j = lax.broadcasted_iota(jnp.int32, (rows, columns), 0)
    i = lax.broadcasted_iota(jnp.int32, (rows, columns), 1) + first_column
    return (j <= i) & (j >= starts[0:1, first_column : first_column + columns])


def causal_pieces(tokens):
    step = tokens // 2
    return ((0, step, step), (step, step, tokens))


HBM = pl.BlockSpec(memory_space=pl.ANY)
IN_VMEM = pl.BlockSpec(memory_space=pltpu.VMEM)


def load_all(refs, places, sems):
    copies = [pltpu.make_async_copy(ref, place, sems.at[k]) for k, (ref, place) in enumerate(zip(refs, places))]
    for copy in copies:
        copy.start()
    return copies


def part_places(refs, scratch, core):
    return [scratch.at[2 * (k // 2) + (core if k % 2 == 0 else 1 - core)] for k in range(len(refs))]


def tables_body(nh, ids, pos_ref, row_ref, starts_ref, table_ref):
    length = pos_ref.shape[1]
    tok = length // nh
    h = ids[1]
    own = row_ref[:, pl.ds(pl.multiple_of(h * tok, 128), tok)]
    lane = lax.broadcasted_iota(jnp.int32, (8, tok), 1)
    starts_ref[...] = lane - own

    def start_of(t):
        return t - pos_ref[0, t]

    def flag(value):
        return jnp.where(value, 1, 0)

    run_last = start_of(length - 1)
    other = [h ^ m for m in range(nh)]
    values = [ids[0], start_of((h + 1) * tok - 1) - h * tok]
    values += [flag((q < h) & (start_of(h * tok) <= (q + 1) * tok - 1)) for q in other[1:]]
    values += [flag(start_of(h * tok) < 0)]
    values += [flag((q > h) & (start_of(q * tok) <= (h + 1) * tok - 1)) for q in other[1:]]
    values += [flag(run_last <= (h + 1) * tok - 1), h, ids[2]]
    values += [flag(run_last <= (q + 1) * tok - 1) for q in other]
    values += [flag(start_of(q * tok) < 0) for q in other]
    lane = lax.broadcasted_iota(jnp.int32, (8, 128), 1)
    table = jnp.zeros((8, 128), jnp.int32)
    for k, value in enumerate(values):
        table = jnp.where(lane == k, value, table)
    table_ref[...] = table


def state_sum_body(hp, nh, first, sc, *refs):
    for i in range(refs[nh].shape[0]):
        total = jnp.zeros(refs[0].shape[1:], f32)
        for m in range(nh):
            total += jnp.where(sc[first + m] > 0, refs[m][((i // hp) ^ m) * hp + i % hp].astype(f32), 0.0)
        refs[nh][i] = total.astype(bf)


def pack_body(sc, qkv_ref, qm_ref, km_ref, qb_ref, ub_ref, ob_ref, db_ref, out_ref, up_ref, down_ref,
              first_ref, other_ref, wa_ref, wb_ref, rows_ref):
    pc, model = qkv_ref.shape
    hs = qm_ref.shape[1]
    width = ob_ref.shape[1]
    rows_ref[...] = jnp.zeros_like(rows_ref)
    rows_ref[0:1, 0:pc] = qb_ref[...].astype(f32)
    rows_ref[1:2, 0 : ub_ref.shape[1]] = ub_ref[...].astype(f32)
    rows_ref[2:3, 0:width] = ob_ref[...].astype(f32)
    rows_ref[3:4, 0:width] = db_ref[...].astype(f32)
    for core, ref in ((sc[0], first_ref), (1 - sc[0], other_ref)):
        cut = pc // 2
        ref[0:cut, :] = qkv_ref[pl.ds(pl.multiple_of(core * cut, TILE), cut), :]
        ref[cut : cut + hs // 2, :] = jnp.zeros((hs // 2, model), bf)
        for i in range(qm_ref.shape[0] // hs):
            for k in range(2):
                rows = slice(i * hs + k * hs // 2, i * hs + (k + 1) * hs // 2)
                at = k * (model // 2) + 128 * i
                own = jnp.where(core == 0, qm_ref[rows, :].astype(f32), km_ref[rows, :].astype(f32))
                ref[cut : cut + hs // 2, at : at + hs] = own.astype(bf)
        cut += hs // 2
        ref[cut : cut + TILE, :] = rows_ref[...].astype(bf)
        half = out_ref.shape[0] // 2
        ref[cut + TILE :, :] = out_ref[pl.ds(pl.multiple_of(core * half, TILE), half), :]
    half = down_ref.shape[0] // 2
    at = pl.ds(pl.multiple_of(sc[0] * half, TILE), half)
    lanes = pl.ds(pl.multiple_of(sc[0] * half, 128), half)
    for k, w_ref in enumerate((wa_ref, wb_ref)):
        part = slice(k * half, (k + 1) * half)
        w_ref[:, 0:half] = up_ref[part, lanes]
        w_ref[:, half:] = down_ref[at, part]


def first_norm_body(sc, x_ref, gain_ref, hid_ref):
    normed, _ = norm_columns(x_ref[...].astype(f32))
    width = x_ref.shape[1]
    gains = gain_ref[...]
    hid_ref[...] = (normed * column(gains, 0, width) + column(gains, 1, width)).astype(bf)


def turn_body(sc, a_ref, b_ref, o_ref):
    tokens = a_ref.shape[1]
    o_ref[0:tokens, :] = a_ref[...].T
    o_ref[tokens:, :] = b_ref[...].T


def map_of(first_ref, at, i, hs, cut):
    model = first_ref.shape[2]
    rows = slice(cut, cut + hs // 2)
    return jnp.concatenate(
        [first_ref[at, rows, k * (model // 2) + 128 * i : k * (model // 2) + 128 * i + hs] for k in range(2)], axis=0
    )


def project_body(hp, hs, count, sc, hid_ref, starts_ref, *refs):
    first_refs = refs[0 : 2 * count]
    proj_ref, qf_ref, kf_ref, va_ref, st_ref, w_ref, sems = refs[-7:]
    p = pl.program_id(0)
    wait_for_piece(first_refs, w_ref, sems, sc)
    pc, tokens = proj_ref.shape[1:]
    cut = pc // 2
    bias = column(w_ref[2 * p, cut + hs // 2 : cut + hs // 2 + TILE, 0:pc], 0, tokens)
    for k in range(2):
        rows = slice(k * cut, (k + 1) * cut)
        proj_ref[0, rows, :] = (nn(w_ref[2 * p + k, 0:cut, :], hid_ref[...]) + bias[rows, :]).astype(bf)
    included = (starts_ref[0:1, :] == sc[1]).astype(f32)
    extra = lax.broadcasted_iota(jnp.int32, (AUG - hs, tokens), 0)
    extra = jnp.where(extra < 2, 1.0, 0.0).astype(bf)
    for i in range(hp):
        row = 3 * hs * i
        for part, out in ((0, qf_ref), (1, kf_ref)):
            own_map = map_of(w_ref, 2 * p + part, i, hs, cut)
            logits = tn(own_map, proj_ref[0, row + part * hs : row + (part + 1) * hs, :])
            out[i, 0:hs, :] = soft_columns(logits).astype(bf)
            out[i, hs : 2 * hs, :] = soft_columns(-logits).astype(bf)
        va_ref[i, 0:hs, :] = proj_ref[0, row + 2 * hs : row + 3 * hs, :]
        va_ref[i, hs:AUG, :] = extra
        kept = (va_ref[i].astype(f32) * included).astype(bf)
        st_ref[i] = nt(kept, kf_ref[i]).astype(bf)


def wait_for_piece(first_refs, w_ref, sems, sc):
    p = pl.program_id(0)
    places = part_places(first_refs, w_ref, sc[0])
    rows = w_ref.shape[1]
    copies = [
        pltpu.make_async_copy(ref.at[pl.ds(0, rows), :], place, sems.at[k])
        for k, (ref, place) in enumerate(zip(first_refs, places))
    ]

    @pl.when(p == 0)
    def _():
        for copy in copies:
            copy.start()

    for k, copy in enumerate(copies):

        @pl.when(p == k // 2)
        def _(copy=copy):
            copy.wait()


def local_mix_body(hp, sc, qf_ref, kf_ref, va_ref, starts_ref, num_ref):
    tokens = qf_ref.shape[2]
    starts = starts_ref[...]
    for first, width, rows in causal_pieces(tokens):
        mask = ahead_mask(starts, rows, first, width)
        for i in range(hp):
            scores = tn(kf_ref[i, :, 0:rows], qf_ref[i, :, first : first + width])
            scores = jnp.where(mask, scores, 0.0).astype(bf)
            num_ref[i, :, first : first + width] = nn(va_ref[i, :, 0:rows], scores)


def weighted_state(sc, slot, refs, i, hp):
    total = jnp.where(sc[slot + len(refs) - 1] > 0, refs[-1][i].astype(f32), 0.0)
    for m, ref in enumerate(refs[:-1], 1):
        total += jnp.where(sc[slot + m - 1] > 0, ref[((i // hp) ^ m) * hp + i % hp].astype(f32), 0.0)
    return total


def load_out_weight(sc, first_refs, w_ref, sems):
    rows = w_ref.shape[0] // len(first_refs)
    at = first_refs[0].shape[0] - rows
    places = [
        w_ref.at[pl.ds(pl.multiple_of(rows * (2 * (k // 2) + (sc[0] if k % 2 == 0 else 1 - sc[0])), TILE), rows), :]
        for k in range(len(first_refs))
    ]
    return load_all([ref.at[pl.ds(at, rows), :] for ref in first_refs], places, sems)


def mix_out_body(hp, hs, nh, sc, num_ref, qf_ref, starts_ref, x_ref, gain_ref, *refs):
    state_refs, row_refs, wo_refs = refs[0:nh], refs[nh : 2 * nh], refs[2 * nh : 4 * nh]
    sin_ref, mixd_ref, mix_ref, res_ref, top_ref, low_ref, w_ref, sems = refs[4 * nh :]
    copies = load_out_weight(sc, wo_refs, w_ref, sems)
    uses = starts_ref[0:1, :] < 0
    model, tokens = x_ref.shape
    for i in range(num_ref.shape[0]):
        state = weighted_state(sc, 2, state_refs, i, hp).astype(bf)
        sin_ref[i] = state
        num = num_ref[i] + jnp.where(uses, nn(state, qf_ref[i]), 0.0)
        mixture = num[0:hs, :] / num[hs : hs + 1, :]
        mixd_ref[i, 0:hs, :] = mixture
        mixd_ref[i, hs : hs + 8, :] = num[hs : hs + 8, :]
        mix_ref[i * hs : (i + 1) * hs, :] = mixture.astype(bf)
    for copy in copies:
        copy.wait()
    res_ref[...] = x_ref[...].astype(f32) + tn(w_ref[...], mix_ref[...])
    width = model // nh
    h = sc[2 + 2 * nh]
    for j in range(nh):
        rows = pl.ds(pl.multiple_of((h ^ j) * width, TILE), width)
        res_ref[rows, :] += column(row_refs[j][:, 0:width], 2, tokens)
    normed, _ = norm_columns(res_ref[...].astype(bf).astype(f32))
    gains = gain_ref[...]
    hidden = (normed * column(gains, 2, tokens) + column(gains, 3, tokens)).astype(bf)
    half = top_ref.shape[0]
    top_ref[...] = hidden[0:half, :]
    low_ref[...] = hidden[half:, :]


def feed_body(count, first, sc, *refs):
    hidt_ins, gyt_ins, gy_in = refs[0:4], refs[4:6], refs[6]
    row_refs = refs[7 : 7 + count]
    w_ins = refs[7 + count : 7 + 3 * count]
    refs = refs[7 + 3 * count :]
    if first:
        out_ref, sg_ref = refs[0:2]
        refs = refs[2:]
    else:
        out_in, sg_in, out_own, out_peer, sg_own, sg_peer = refs[0:6]
        refs = refs[6:]
    w_refs, ub_ref, refs = refs[0:count], refs[count], refs[count + 1 :]
    hid_ref, act_ref, ug_ref = refs
    mid, tokens = hidt_ins[0].shape
    model = 2 * mid
    half = act_ref.shape[1]
    runs = [slice(0, tokens), slice(tokens, 2 * tokens)]
    lo, hi = slice(0, half), slice(half, 2 * half)
    at_half = pl.ds(pl.multiple_of(sc[0] * half, 128), half)
    for k in range(count):
        bias = row_refs[k][:, at_half].astype(f32)[1:2, :]
        first_w, second_w = w_ins[2 * k], w_ins[2 * k + 1]
        for which, rows in enumerate(runs):
            if k == 0:
                for m in range(2):
                    hid_ref[rows, m * mid : (m + 1) * mid] = hidt_ins[2 * which + m][...].T
            up_pre = nn(hid_ref[rows, lo], first_w[:, lo]) + nn(hid_ref[rows, hi], second_w[:, lo]) + bias
            value, slope = gelu_pair(up_pre)
            act_ref[rows, :] = value.astype(bf)
            back = nt(gy_in[rows, lo], first_w[:, hi]) + nt(gy_in[rows, hi], second_w[:, hi])
            ug_ref[rows, :] = (back * slope).astype(bf)
        ub_ref[k] = nn(jnp.ones((8, 2 * tokens), bf), ug_ref[...])
        for m in range(2):
            grads = [nn(hidt_ins[2 * r + m][...], ug_ref[runs[r], :]) for r in range(2)]
            w_refs[k][m * mid : (m + 1) * mid, :] = (grads[0] + grads[1]).astype(bf)
        grads = [nn(gyt_ins[r][...], act_ref[runs[r], :]) for r in range(2)]
        w_refs[k][model : 2 * model, :] = (grads[0] + grads[1]).astype(bf)
        w_refs[k][2 * model :, :] = jnp.zeros((TILE, half), bf)
        for at, w in ((lo, first_w), (hi, second_w)):
            if first and k == 0:
                out_ref[:, at] = nn(act_ref[...], w[:, hi])
                sg_ref[at, :] = nt(w[:, lo], ug_ref[...])
            elif first:
                out_ref[:, at] += nn(act_ref[...], w[:, hi])
                sg_ref[at, :] += nt(w[:, lo], ug_ref[...])
            else:
                out = out_in[:, at] + nn(act_ref[...], w[:, hi])
                out_own[:, at] = out[runs[0], :]
                out_peer[:, at] = out[runs[1], :].astype(bf)
                sg = sg_in[at, :] + nt(w[:, lo], ug_ref[...])
                sg_own[at, :] = sg[:, runs[0]]
                sg_peer[at, :] = sg[:, runs[1]].astype(bf)


def block_out_body(nh, sc, res_ref, out_ref, out2_ref, tg_ref, *refs):
    row_refs, o_ref, total_ref = refs[0:nh], refs[nh], refs[nh + 1]
    model, tokens = res_ref.shape
    width = model // nh
    total_ref[...] = res_ref[...] + (out_ref[...] + out2_ref[...].astype(f32)).T
    h = sc[2 + 2 * nh]
    for j in range(nh):
        rows = pl.ds(pl.multiple_of((h ^ j) * width, TILE), width)
        o_ref[j, 1] = tg_ref[j]
        o_ref[h ^ j, 0] = (total_ref[rows, :] + column(row_refs[j][:, 0:width], 3, tokens)).astype(bf)


def lay_out_body(nh, sc, in_ref, *o_refs):
    tokens = in_ref.shape[3]
    for k in range(2):
        for q in range(nh):
            o_refs[k][:, q * tokens : (q + 1) * tokens] = in_ref[q, k]


def second_back_body(hs, nh, sc, sg_ref, sg2_ref, res_ref, gyt_ref, gain_ref, mixd_ref, starts_ref, qf_ref, *refs):
    wo_refs, (rg_ref, ag_ref, vec_ref, na_ref, sgt_ref, w_ref, sems) = refs[0 : 2 * nh], refs[2 * nh :]
    copies = load_out_weight(sc, wo_refs, w_ref, sems)
    model, tokens = sg_ref.shape
    width = model // nh
    normed, inv_std = norm_columns(res_ref[...].astype(bf).astype(f32))
    sg = sg_ref[...] + sg2_ref[...].astype(f32)
    res_grad = gyt_ref[...].astype(f32) + norm_columns_back(sg, normed, inv_std, column(gain_ref[...], 2, tokens))
    rg_ref[...] = res_grad
    ag_ref[...] = res_grad.astype(bf)
    uses = (starts_ref[0:1, :] < 0).astype(f32)
    for copy in copies:
        copy.wait()
    mg = nn(w_ref[...], ag_ref[...])
    row = lax.broadcasted_iota(jnp.int32, (AUG - hs, tokens), 0)
    for i in range(qf_ref.shape[0]):
        num = mg[i * hs : (i + 1) * hs, :] / mixd_ref[i, hs : hs + 1, :]
        den = -jnp.sum(num * mixd_ref[i, 0:hs, :], axis=0, keepdims=True)
        high = den.astype(bf).astype(f32)
        extra = jnp.where(row == 0, high, jnp.where(row == 1, den - high, 0.0))
        na_ref[i, 0:hs, :] = num.astype(bf)
        na_ref[i, hs:AUG, :] = extra.astype(bf)
        kept = (na_ref[i].astype(f32) * uses).astype(bf)
        sgt_ref[i] = nt(kept, qf_ref[i]).astype(bf)
    for at, value in enumerate((sg * normed, sg, ag_ref[...], gyt_ref[...])):
        sums = row_sums(value)
        for p in range(nh):
            vec_ref[p, at : at + 1, :] = sums[0:1, p * width : (p + 1) * width]


def halves_back(feat, grad, hs):
    parts = []
    for k in range(2):
        soft = feat[k * hs : (k + 1) * hs, :].astype(f32)
        own = grad[k * hs : (k + 1) * hs, :]
        weight = jnp.sum(soft * own, axis=0, keepdims=True) / jnp.sum(soft, axis=0, keepdims=True)
        parts.append(soft * (own - weight))
    return (parts[0] - parts[1]).astype(bf)


def local_back_body(hp, hs, sc, qf_ref, kf_ref, va_ref, na_ref, sin_ref, starts_ref, ql_ref, kfg_ref, vg_ref):
    tokens = qf_ref.shape[2]
    starts = starts_ref[...]
    step = tokens // 2
    uses = starts[0:1, :] < 0
    masks = [ahead_mask(starts, rows, first, width) for first, width, rows in causal_pieces(tokens)]
    for i in range(hp):
        na = na_ref[i]
        through = tn(sin_ref[i], na)
        for which, (first, width, rows) in enumerate(causal_pieces(tokens)):
            at = slice(first, first + width)
            mask = masks[which]
            scores = jnp.where(mask, tn(kf_ref[i, :, 0:rows], qf_ref[i, :, at]), 0.0).astype(bf)
            sgrad = jnp.where(mask, tn(va_ref[i, :, 0:rows], na[:, at]), 0.0).astype(bf)
            qfg = nn(kf_ref[i, :, 0:rows], sgrad) + jnp.where(uses[:, at], through[:, at], 0.0)
            ql_ref[i, :, at] = halves_back(qf_ref[i, :, at], qfg, hs)
            kfg = nt(qf_ref[i, :, at], sgrad)
            vg = nt(na[:, at], scores)[0:hs, :]
            if which == 0:
                kfg_ref[i, :, 0:rows] = kfg
                vg_ref[i, :, 0:rows] = vg
            else:
                kfg_ref[i, :, 0:step] += kfg[:, 0:step]
                vg_ref[i, :, 0:step] += vg[:, 0:step]
                kfg_ref[i, :, step:] = kfg[:, step:]
                vg_ref[i, :, step:] = vg[:, step:]


def join_extra(state, hs):
    row = lax.broadcasted_iota(jnp.int32, state.shape, 0)
    both = state[hs : hs + 1, :] + state[hs + 1 : hs + 2, :]
    return jnp.where(row < hs, state, jnp.where(row == hs, both, 0.0))


def project_back_body(hp, hs, nh, sc, *refs):
    state_refs, first_refs, refs = refs[0:nh], refs[nh : 3 * nh], refs[3 * nh :]
    kf_ref, va_ref, ql_ref, kfg_ref, vg_ref, proj_ref, starts_ref, *pg_refs, fg_ref, mg_ref, pb_ref, pg_ref, first_ref, sems = refs
    p = pl.program_id(0)
    wait_for_piece(first_refs, first_ref, sems, sc)
    included = starts_ref[0:1, :] == sc[1]
    cut = pg_ref.shape[1] // 2
    for i in range(hp):
        total = jnp.where(sc[1 + 2 * nh] > 0, state_refs[-1][i].astype(f32), 0.0)
        for m in range(1, nh):
            total += jnp.where(sc[1 + nh + m] > 0, state_refs[m - 1][i].astype(f32), 0.0)
        state = join_extra(total, hs).astype(bf)
        kfg = kfg_ref[i] + jnp.where(included, tn(state, va_ref[i]), 0.0)
        vg = vg_ref[i] + jnp.where(included, nn(state, kf_ref[i])[0:hs, :], 0.0)
        klg = halves_back(kf_ref[i], kfg, hs)
        qlg = ql_ref[i]
        row = 3 * hs * i
        pg_ref[0, row : row + hs, :] = nn(map_of(first_ref, 2 * p, i, hs, cut), qlg).astype(bf)
        pg_ref[0, row + hs : row + 2 * hs, :] = nn(map_of(first_ref, 2 * p + 1, i, hs, cut), klg).astype(bf)
        pg_ref[0, row + 2 * hs : row + 3 * hs, :] = vg.astype(bf)
        q_grad = nt(proj_ref[0, row : row + hs, :], qlg)
        k_grad = nt(proj_ref[0, row + hs : row + 2 * hs, :], klg)
        mg_ref[0, :, 128 * i : 128 * (i + 1)] = jnp.concatenate([q_grad, k_grad], axis=1)
    for j, ref in enumerate(pg_refs):

        @pl.when(p == j)
        def _(ref=ref):
            ref[...] = pg_ref[0]

    pb_ref[0] = row_sums(pg_ref[0])
    grad = tn(first_ref[2 * p, 0:cut, :], pg_ref[0, 0:cut, :]) + tn(first_ref[2 * p + 1, 0:cut, :], pg_ref[0, cut:, :])

    @pl.when(pl.program_id(0) == 0)
    def _():
        fg_ref[...] = grad

    @pl.when(pl.program_id(0) > 0)
    def _():
        fg_ref[...] += grad


def first_back_body(nh, sc, fg_ref, x_ref, rg_ref, gain_ref, tg_ref, vec_ref):
    model, tokens = fg_ref.shape
    width = model // nh
    normed, inv_std = norm_columns(x_ref[...].astype(f32))
    fg = fg_ref[...]
    gain = column(gain_ref[...], 0, tokens)
    tg = (rg_ref[...] + norm_columns_back(fg, normed, inv_std, gain)).astype(bf)
    for p in range(nh):
        tg_ref[p] = tg[p * width : (p + 1) * width, :]
    for at, value in enumerate((fg * normed, fg)):
        sums = row_sums(value)
        for p in range(nh):
            vec_ref[p, at : at + 1, :] = sums[0:1, p * width : (p + 1) * width]


def split_quarters(nh, nz, sc, total_ref, keep_ref, send_ref):
    part = total_ref.shape[0] // nz
    for k in range(nz):
        o_ref = keep_ref if k % 2 == 0 else send_ref
        at = pl.ds(pl.multiple_of((sc[3 + 2 * nh] ^ k) * part, TILE), part)
        o_ref[(k // 2) * part : (k // 2 + 1) * part, :] = total_ref[at, :]


def feed_sum_body(nh, nz, sc, *refs):
    keep_ref, send_ref, total_ref = refs[nh:]
    rows = total_ref.shape[0]
    total_ref[...] = sum(ref[0:rows, :].astype(f32) for ref in refs[0:nh]).astype(bf)
    split_quarters(nh, nz, sc, total_ref, keep_ref, send_ref)


def last_sum_body(nh, nz, sc, *refs):
    keep_ref, send_ref, total_ref = refs[nh:]
    total_ref[...] = sum(ref[...].astype(f32) for ref in refs[0:nh]).astype(bf)
    split_quarters(nh, nz, sc, total_ref, keep_ref, send_ref)


def pair_sum_body(sc, own_ref, got_ref, keep_ref, send_ref):
    part = keep_ref.shape[0]
    keep_ref[...] = (own_ref[0:part, :].astype(f32) + got_ref[0:part, :].astype(f32)).astype(bf)
    send_ref[...] = (own_ref[part:, :].astype(f32) + got_ref[part:, :].astype(f32)).astype(bf)


def last_grads_body(nh, sc, *refs):
    pg_refs, pg2_refs, refs = refs[0:nh], refs[nh : 2 * nh], refs[2 * nh :]
    hid_ref, hid2_ref, mg_ref, pb_ref, early_ref, late_ref, vec1_ref, vec2_ref = refs[0:8]
    mix_ref, mix2_ref, ag_ref, ag2_ref, *o_refs, rows_ref = refs[8:]
    pc, half = pg_refs[0].shape[0], hid_ref.shape[0]
    hs = mg_ref.shape[1]
    width = vec1_ref.shape[2]
    h = sc[2 + 2 * nh]
    for j in range(nh):
        o_ref = o_refs[j]
        o_ref[0:pc, :] = (nt(pg_refs[j][...], hid_ref[...]) + nt(pg2_refs[j][...], hid2_ref[...])).astype(bf)
        o_ref[pc : pc + hs, :] = mg_ref[j].astype(bf)
        ub_ref, k = (early_ref, j) if j < nh - 1 else (late_ref, 0)
        rows_ref[...] = jnp.zeros_like(rows_ref)
        rows_ref[0:1, :] = pb_ref[j, 0:1, 0:half]
        rows_ref[1:2, 0 : pc - half] = pb_ref[j, 0:1, half:]
        rows_ref[2:3, :] = jnp.where(sc[0] == 0, ub_ref[k, 0:1, :], 0.0)
        rows_ref[3:4, :] = jnp.where(sc[0] == 0, 0.0, ub_ref[k, 0:1, :])
        rows_ref[4:8, 0:width] = vec2_ref[h ^ j, 0:4, :]
        rows_ref[8:10, 0:width] = vec1_ref[h ^ j, 0:2, :]
        at = pc + hs + TILE
        o_ref[pc + hs : at, :] = rows_ref[...].astype(bf)
        rows = slice(j * width, (j + 1) * width)
        o_ref[at : at + width, :] = (nt(mix_ref[rows, :], ag_ref[...]) + nt(mix2_ref[rows, :], ag2_ref[...])).astype(bf)
        o_ref[at + width :, :] = jnp.zeros((o_ref.shape[0] - at - width, half), bf)


def join_quarters(nh, nz, sc, refs, total_ref):
    part = refs[0].shape[0]
    for k in range(2 * nz):
        at = pl.ds(pl.multiple_of((sc[3 + 2 * nh] ^ (k % nz)) * part, TILE), part)
        total_ref[k // nz, at, :] = refs[k][...]


def feed_out_body(nh, nz, sc, *refs):
    up_ref, down_ref, total_ref = refs[2 * nz :]
    join_quarters(nh, nz, sc, refs, total_ref)
    model = down_ref.shape[1]
    half = total_ref.shape[2]
    for k, core in enumerate((sc[0], 1 - sc[0])):
        at = pl.ds(pl.multiple_of(core * half, 128), half)
        up_ref[:, at] = total_ref[k, 0:model, :].astype(f32)
        down_ref[at, :] = total_ref[k, model : 2 * model, :].astype(f32).T


def last_out_body(hs, nh, nz, sc, *refs):
    qkv_ref, out_ref, qm_ref, km_ref, qb_ref, ub_ref, vec_ref, total_ref = refs[2 * nz :]
    join_quarters(nh, nz, sc, refs, total_ref)
    pc = qkv_ref.shape[0]
    half = total_ref.shape[2]
    for k, core in enumerate((sc[0], 1 - sc[0])):
        at = pl.ds(pl.multiple_of(core * half, 128), half)
        qkv_ref[:, at] = total_ref[k, 0:pc, :].astype(f32)
        first = pc + hs + TILE
        out_ref[:, at] = total_ref[k, first : first + out_ref.shape[0], :].astype(f32)
    maps = total_ref[0, pc : pc + hs, :].astype(f32) + total_ref[1, pc : pc + hs, :].astype(f32)
    for i in range(qm_ref.shape[0]):
        qm_ref[i] = maps[:, 128 * i : 128 * i + hs]
        km_ref[i] = maps[:, 128 * i + hs : 128 * i + 2 * hs]
    rows = slice(pc + hs, pc + hs + TILE)
    rows = total_ref[0, rows, :].astype(f32) + total_ref[1, rows, :].astype(f32)
    qb_ref[:, 0:half] = rows[0:1, :]
    qb_ref[:, half:] = rows[1:2, 0 : pc - half]
    ub_ref[:, 0:half] = rows[2:3, :]
    ub_ref[:, half:] = rows[3:4, :]
    vec_ref[...] = rows


def swap(a, axis, k):
    n = lax.axis_size(axis)
    return lax.ppermute(a, axis, [(i, i ^ k) for i in range(n)])


def trade(a, axis):
    return lax.all_to_all(a, axis, 0, 0, tiled=True)


def after(a, *others):
    return lax.optimization_barrier((a,) + others)[0]


def chain_seq(part, forward, weight_of):
    n = lax.axis_size("seq")
    total = None
    for k in range(1, n):
        pairs = [(i, i + k) if forward else (i + k, i) for i in range(n - k)]
        if n == 2:
            return lax.ppermute(part, "seq", pairs)
        sent = part if forward else part * weight_of(k).astype(part.dtype)
        got = lax.ppermute(sent, "seq", pairs).astype(f32) * (weight_of(k) if forward else 1.0)
        total = got if total is None else total + got
    return total.astype(bf)


def local(tokens, attn_gain, attn_shift, qkv_weight, qkv_bias, query_map, key_map, out_weight, out_bias,
          mlp_gain, mlp_shift, up_weight, up_bias, down_weight, down_bias, positions, out_grad):
    nh, ns, nz = lax.axis_size("head"), lax.axis_size("seq"), lax.axis_size("dp")
    length, width = tokens.shape[1], tokens.shape[2]
    model = width * nh
    half = model // 2
    hp, hs = query_map.shape[0], query_map.shape[1]
    heads = hp * nh
    pc = qkv_weight.shape[1]
    hidden = up_weight.shape[1]
    hh = hidden // 2
    tok = length // nh
    h = lax.axis_index("head")
    s2 = lax.axis_index("seq") % 2
    peers = range(1, nh)

    ids = jnp.stack([s2, h, lax.axis_index("dp")]).astype(jnp.int32)
    starts, table = pl.pallas_call(
        functools.partial(tables_body, nh),
        out_shape=[shape((8, tok), jnp.int32), shape((8, 128), jnp.int32)],
        in_specs=[pl.BlockSpec(memory_space=pltpu.SMEM), pl.BlockSpec(memory_space=pltpu.SMEM),
                  pl.BlockSpec(memory_space=pltpu.VMEM)],
        name="tables",
    )(ids, positions, positions)
    sc = table[0, 0 : 4 + 4 * nh]
    run_start = -positions[0, 0]

    def beyond_chip(total):
        base = total
        for k in range(1, ns // 2):
            total += lax.ppermute(base, "seq", [(i, (i + 2 * k) % ns) for i in range(ns)])
        return total

    both = jnp.concatenate([a[0].T.reshape(width, nh, tok).transpose(1, 0, 2) for a in (tokens, out_grad)])
    both = both.reshape(2, nh, width, tok).transpose(1, 0, 2, 3)
    both = trade(both, "head")

    core_of = jnp.full((1,), s2, jnp.int32)
    gains = jnp.pad(jnp.stack([attn_gain, attn_shift, mlp_gain, mlp_shift]), ((0, TILE - 4), (0, 0)))
    fl = pc // 2 + hs // 2 + TILE
    fr = fl + width // 2
    own, other_half, wa_own, wb_own = run_kernel(
        pack_body, "pack_weights", (1,), core_of,
        [(a, None) for a in (qkv_weight.T, query_map.reshape(-1, hs), key_map.reshape(-1, hs), qkv_bias[None], up_bias[None],
                             out_bias[None], down_bias[None], out_weight, up_weight, down_weight)],
        [(shape((fr, model), bf), None), (shape((fr, model), bf), None), (shape((hh, 2 * hh), bf), None), (shape((hh, 2 * hh), bf), None)],
        scratch=[pltpu.VMEM((TILE, model), f32)],
    )
    x, gyt = [both[:, k].reshape(model, tok) for k in range(2)]
    own = after(own, sc)
    first_got = [swap(own, "head", m) for m in peers]
    x, gyt = after(x, *first_got[:-1]), after(gyt, *first_got[:-1])
    gyt_peer = swap(gyt, "seq", 1)
    (hid,) = run_kernel(
        first_norm_body, "first_norm", (1,), core_of, [(x, None), (gains, None)], [(shape((model, tok), bf), None)]
    )
    hid_peer = swap(lax.dynamic_slice_in_dim(hid, (1 - s2) * half, half, 0), "seq", 1)
    (gy,) = run_kernel(
        turn_body, "turn_grad", (1,), core_of, [(gyt, None), (gyt_peer, None)], [(shape((2 * tok, model), bf), None)]
    )
    firsts_of = [[own, other_half]] + [[a, swap(after(a, hid), "seq", 1)] for a in first_got[:-1]]
    row_specs = [(pair[0], pl.BlockSpec((TILE, model), lambda *_: (fl // TILE - 1, 0))) for pair in firsts_of + [first_got[-1:]]]
    in_hbm = lambda arrays: [(a, HBM) for a in arrays]
    first_scratch = [pltpu.VMEM((2 * nh, fl, model), bf), pltpu.SemaphoreType.DMA((2 * nh,))]
    wo_scratch = [pltpu.VMEM((model, model), bf), pltpu.SemaphoreType.DMA((2 * nh,))]

    va_spec, state_spec, feat_spec = lead(hp, AUG, tok), lead(hp, AUG, 2 * hs), lead(hp, 2 * hs, tok)
    hid_now = after(hid, gyt_peer, hid_peer)

    def project(first_piece, count, so_far):
        def at(spec):
            return pl.BlockSpec(spec.block_shape, lambda p, sc: (p + first_piece,) + (0,) * (len(spec.block_shape) - 1))

        outs = [(shape((nh, pc, tok), bf), at(lead(1, pc, tok))), (shape((heads, 2 * hs, tok), bf), at(feat_spec)),
                (shape((heads, 2 * hs, tok), bf), at(feat_spec)), (shape((heads, AUG, tok), bf), at(va_spec)),
                (shape((heads, AUG, 2 * hs), bf), at(state_spec))]
        arrays = [a for pair in firsts_of[first_piece : first_piece + count] for a in pair]
        return run_kernel(
            functools.partial(project_body, hp, hs, count), f"project_{first_piece}", (count,), sc,
            [(hid_now, None), (starts, None)] + in_hbm(arrays) + in_hbm(so_far), outs,
            scratch=[pltpu.VMEM((2 * count, fl, model), bf), pltpu.SemaphoreType.DMA((2 * count,))],
            aliases={3 + 2 * count + k: k for k in range(len(so_far))},
        )

    so_far = project(0, nh - 1, ())
    far = after(first_got[-1], so_far[-1])
    firsts_of.append([far, after(swap(far, "seq", 1), so_far[-1])])
    all_first = [a for pair in firsts_of for a in pair]
    proj, qf, kf, va, states = project(nh - 1, 1, so_far)
    wa_own = after(wa_own, *first_got[:-1])
    wa_x, wa_y = swap(wa_own, "head", 1), swap(wa_own, "head", 2)
    (num,) = run_kernel(
        functools.partial(local_mix_body, hp), "local_mix", (nh,), sc,
        [(qf, feat_spec), (kf, feat_spec), (after(va, gy, wa_x, wa_y), va_spec), (starts, None)],
        [(shape((heads, AUG, tok), f32), va_spec)],
    )
    around = [after(swap(states, "head", m), num) for m in peers]

    def states_together(first, arrays):
        (total,) = run_kernel(
            functools.partial(state_sum_body, hp, nh, first), f"state_sum_{first}", (1,), sc, [(a, None) for a in arrays],
            [(shape((heads, AUG, 2 * hs), bf), None)],
        )
        return total

    whole_run = states_together(4 + 2 * nh, [states] + around)
    before = chain_seq(whole_run, True, lambda k: (run_start <= -(k - 1) * length - 1).astype(f32))

    wb_own = after(wb_own, before)
    wb_x, wb_y = swap(wb_own, "head", 1), swap(wb_own, "head", 2)

    sin, mixd, mix, res, *hidt2 = run_kernel(
        functools.partial(mix_out_body, hp, hs, nh), "mix_out", (1,), sc,
        [(a, None) for a in (num, qf, starts, x, gains, *around, before)] + row_specs + in_hbm(all_first),
        [(shape((heads, AUG, 2 * hs), bf), None), (shape((heads, hs + 8, tok), f32), None), (shape((model, tok), bf), None),
         (shape((model, tok), f32), None), (shape((half, tok), bf), None), (shape((half, tok), bf), None)],
        scratch=wo_scratch,
    )
    hidt2_peer = [swap(a, "seq", 1) for a in hidt2]
    w_far = [swap(after(wa_x, mix), "head", 2), swap(after(wb_y, mix), "head", 1)]
    w_all = [[wa_own, wb_own], [wa_x, wb_x], [wa_y, wb_y], w_far]

    all_rows = 2 * model

    def feed(which, sums):
        count = len(which)
        if sums:
            outs = [shape((tok, model), f32), shape((tok, model), bf), shape((model, tok), f32), shape((model, tok), bf)]
        else:
            outs = [shape((2 * tok, model), f32), shape((model, 2 * tok), f32)]
        return run_kernel(
            functools.partial(feed_body, count, not sums), f"feed_{which[0]}", (1,), sc,
            [(a, IN_VMEM) for a in (*hidt2, *hidt2_peer, gyt, gyt_peer, gy)] + [row_specs[j] for j in which]
            + [(a, IN_VMEM) for j in which for a in w_all[j]] + [(a, IN_VMEM) for a in sums],
            [(a, None if sums else IN_VMEM) for a in outs] + [(shape((2 * model + TILE, hh), bf), None)] * count + [(shape((count, 8, hh), f32), None)],
            scratch=[pltpu.VMEM((2 * tok, model), bf), pltpu.VMEM((2 * tok, hh), bf), pltpu.VMEM((2 * tok, hh), bf)],
        )

    part_out, part_sg, *early = feed(list(range(nh - 1)), ())
    w_parts, early_ub = early[:-1], early[-1]
    w_got = [swap(w_parts[m], "head", m) for m in range(1, nh - 1)]
    mix_peer = swap(after(mix, early_ub), "seq", 1)
    out_own, out_send, sg_own, sg_send, w_last, late_ub = feed([nh - 1], (part_out, part_sg))
    sg_recv = swap(sg_send, "seq", 1)

    vec_block = (shape((nh, 8, width), f32), None)
    rg, ag, vec2, na, sgt = run_kernel(
        functools.partial(second_back_body, hs, nh), "second_back", (1,), sc,
        [(a, None) for a in (sg_own, sg_recv, res, gyt, gains, mixd, starts, qf)] + in_hbm(all_first),
        [(shape((model, tok), f32), None), (shape((model, tok), bf), None), vec_block,
         (shape((heads, AUG, tok), bf), None), (shape((heads, AUG, 2 * hs), bf), None)],
        scratch=wo_scratch,
    )
    sgt = after(sgt, *w_got)
    g_sent = [swap(sgt, "head", m) for m in peers]
    half_spec = pl.BlockSpec((half, tok), lambda p, sc: (sc[0], 0))
    ag_peer = swap(lax.dynamic_slice_in_dim(ag, (1 - s2) * half, half, 0), "seq", 1)

    na_late = na
    ql, kfg, vg = run_kernel(
        functools.partial(local_back_body, hp, hs), "local_back", (nh,), sc,
        [(qf, feat_spec), (kf, feat_spec), (va, va_spec), (na_late, va_spec), (sin, state_spec), (starts, None)],
        [(shape((heads, hs, tok), bf), lead(hp, hs, tok)), (shape((heads, 2 * hs, tok), f32), feat_spec),
         (shape((heads, hs, tok), f32), lead(hp, hs, tok))],
    )
    g_around = [after(a, ql) for a in g_sent]
    w_got.append(swap(after(w_last, *g_around), "head", nh - 1))
    g_whole = states_together(4 + 3 * nh, [sgt] + g_around)
    after_run = chain_seq(g_whole, False, lambda k: (run_start <= -(k - 1) * length - 1).astype(f32))
    def peer_states(a, m):
        return (a, pl.BlockSpec((hp, AUG, 2 * hs), lambda p, sc: (p ^ m, 0, 0)))

    *pg, fg, map_grads, pb = run_kernel(
        functools.partial(project_back_body, hp, hs, nh), "project_back", (nh,), sc,
        [peer_states(a, m) for a, m in zip(g_around + [after_run], [*peers, 0])] + in_hbm(all_first)
        + [(kf, feat_spec), (va, va_spec), (ql, lead(hp, hs, tok)), (after(kfg, ag_peer, mix_peer), feat_spec), (vg, lead(hp, hs, tok)),
           (proj, lead(1, pc, tok)), (starts, None)],
        [(shape((pc, tok), bf), None)] * nh
        + [(shape((model, tok), f32), None),
           (shape((nh, hs, 128 * hp), f32), lead(1, hs, 128 * hp)), (shape((nh, 8, pc), f32), lead(1, 8, pc))],
        scratch=[pltpu.VMEM((1, pc, tok), bf)] + first_scratch,
    )
    pg_peer = [swap(a, "seq", 1) for a in pg]
    tg, vec1 = run_kernel(
        functools.partial(first_back_body, nh), "first_back", (1,), sc,
        [(fg, None), (x, None), (rg, None), (gains, None)], [(shape((nh, width, tok), bf), None), vec_block],
    )
    last_rows = -(-(pc + hs + TILE + width) // (nz * TILE)) * nz * TILE
    last_parts = run_kernel(
        functools.partial(last_grads_body, nh), "last_grads", (1,), sc,
        [(a, None) for a in (*pg, *pg_peer)] + [(hid, half_spec), (hid_peer, None)]
        + [(a, None) for a in (after(map_grads, w_got[-1]), pb, early_ub, late_ub, vec1, vec2, mix, mix_peer)]
        + [(ag, half_spec), (ag_peer, None)],
        [(shape((last_rows, half), bf), None)] * nh,
        scratch=[pltpu.VMEM((TILE, half), f32)],
    )

    feed_rows, part_rows = all_rows // nz, last_rows // nz

    def halves_of(body, name, arrays, rows):
        return run_kernel(
            functools.partial(body, nh, nz), name, (1,), sc, [(a, None) for a in arrays],
            [(shape((2 * rows, hh), bf), None)] * 2, scratch=[pltpu.VMEM((nz * rows, hh), bf)],
        )

    def quarter(name, keep, got, rows):
        return run_kernel(
            pair_sum_body, name, (1,), sc, [(keep, None), (got, None)], [(shape((rows, hh), bf), None)] * 2
        )

    def spread(one):
        two = swap(one, "dp", 2)
        return [one, swap(one, "dp", 1), two, swap(two, "dp", 1)]

    feed_keep, feed_send = halves_of(
        feed_sum_body, "feed_sum", (after(w_parts[0], *last_parts), *w_got), feed_rows
    )
    feed_keep, feed_send = beyond_chip(feed_keep), beyond_chip(feed_send)
    out_recv = swap(after(out_send, *pg), "seq", 1)
    (chunks,) = run_kernel(
        functools.partial(block_out_body, nh), "block_out", (1,), sc,
        [(after(res, feed_keep), None), (out_own, None), (out_recv, None), (tg, None)] + row_specs,
        [(shape((nh, 2, width, tok), bf), None)], scratch=[pltpu.VMEM((model, tok), f32)],
    )
    feed_near, feed_next = quarter("feed_pair", feed_keep, swap(feed_send, "dp", 1), feed_rows)
    feed_far = swap(feed_next, "dp", 2)
    last_got = [after(swap(last_parts[m], "head", m), chunks, feed_near) for m in peers]
    last_keep, last_send = halves_of(last_sum_body, "last_sum", (last_parts[0], *last_got), part_rows)
    last_keep, last_send = beyond_chip(last_keep), beyond_chip(last_send)
    last_pair = swap(last_send, "dp", 1)
    feed_one = (feed_near.astype(f32) + after(feed_far, last_keep).astype(f32)).astype(bf)
    last_near, last_next = quarter("last_pair", last_keep, after(last_pair, feed_one), part_rows)
    last_one = (last_near.astype(f32) + swap(last_next, "dp", 2).astype(f32)).astype(bf)
    feed_total, last_total = spread(feed_one), spread(last_one)
    chunks = trade(chunks, "head")
    block_out, tokens_grad = run_kernel(
        functools.partial(lay_out_body, nh), "lay_out", (1,), sc, [(chunks, None)],
        [(shape((width, length), bf), None)] * 2,
    )
    upweight_grad, downweight_grad = run_kernel(
        functools.partial(feed_out_body, nh, nz), "feed_result", (1,), sc, [(a, None) for a in feed_total] + [(swap(a, "seq", 1), None) for a in feed_total],
        [(shape((model, hidden), f32), None), (shape((hidden, model), f32), None)],
        scratch=[pltpu.VMEM((2, all_rows, hh), bf)],
    )
    qkv_grad, outweight_grad, query_grad, key_grad, qkvbias_grad, upbias_grad, rows = run_kernel(
        functools.partial(last_out_body, hs, nh, nz), "last_result", (1,), sc, [(a, None) for a in last_total] + [(swap(a, "seq", 1), None) for a in last_total],
        [(shape((pc, model), f32), None), (shape((width, model), f32), None), (shape((hp, hs, hs), f32), None),
         (shape((hp, hs, hs), f32), None),
         (shape((1, pc), f32), None), (shape((1, hidden), f32), None), (shape((TILE, half), f32), None)],
        scratch=[pltpu.VMEM((2, last_rows, half), bf)],
    )
    vec = rows[4:10, 0:width]
    return (block_out.T[None], tokens_grad.T[None], vec[4], vec[5], qkv_grad.T, qkvbias_grad[0], query_grad, key_grad,
            outweight_grad, vec[2], vec[0], vec[1], upweight_grad, upbias_grad[0], downweight_grad, vec[3])


def solution(mesh):
    wide = P("dp", "seq", "head")
    return jax.shard_map(
        local,
        mesh=mesh,
        in_specs=(wide, P(), P(), P(None, "head"), P("head"), P("head", None, None), P("head", None, None),
                  P("head", None), P("head"), P(), P(), P(None, "head"), P("head"), P("head", None), P("head"),
                  P("dp", "seq"), wide),
        out_specs=(wide, wide, P("head"), P("head"), P(None, "head"), P("head"), P("head", None, None),
                   P("head", None, None), P("head", None), P("head"), P("head"), P("head"), P(None, "head"), P("head"),
                   P("head", None), P("head")),
        check_vma=False,
    )
```

```python
import functools

import jax
import jax.numpy as jnp
from jax import lax
from jax.experimental import pallas as pl
from jax.experimental.pallas import tpu as pltpu
from jax.sharding import PartitionSpec as P

eps = 1e-05
gelu_scale = 0.7978845608028654
bf = jnp.bfloat16
f32 = jnp.float32
AUG = 80
TILE = 16


def nn(a, b):
    return lax.dot_general(a, b, (((1,), (0,)), ((), ())), preferred_element_type=f32)


def nt(a, b):
    return lax.dot_general(a, b, (((1,), (1,)), ((), ())), preferred_element_type=f32)


def tn(a, b):
    return lax.dot_general(a, b, (((0,), (0,)), ((), ())), preferred_element_type=f32)


def shape(dims, dtype):
    return jax.ShapeDtypeStruct(tuple(dims), dtype)


def whole(a):
    dims = tuple(a.shape)
    return pl.BlockSpec(dims, lambda *_: (0,) * len(dims))


def lead(count, *dims):
    return pl.BlockSpec((count,) + dims, lambda p, sc: (p,) + (0,) * len(dims))


def run_kernel(body, name, grid, scalars, ins, outs, scratch=(), aliases=None):
    return pl.pallas_call(
        body,
        out_shape=[o for o, _ in outs],
        grid_spec=pltpu.PrefetchScalarGridSpec(
            num_scalar_prefetch=1,
            grid=grid,
            in_specs=[spec or whole(a) for a, spec in ins],
            out_specs=[spec or whole(o) for o, spec in outs],
            scratch_shapes=list(scratch),
        ),
        compiler_params=pltpu.CompilerParams(vmem_limit_bytes=18 * 2**20),
        cost_estimate=pl.CostEstimate(flops=0, bytes_accessed=0, transcendentals=0),
        input_output_aliases=aliases or {},
        name=name,
    )(scalars, *[a for a, _ in ins])


def norm_columns(values):
    center = values - jnp.mean(values, axis=0, keepdims=True)
    inv_std = lax.rsqrt(jnp.mean(center * center, axis=0, keepdims=True) + eps)
    return center * inv_std, inv_std


def norm_columns_back(grad, normed, inv_std, gain):
    scaled = grad * gain
    return inv_std * (
        scaled
        - jnp.mean(scaled, axis=0, keepdims=True)
        - normed * jnp.mean(scaled * normed, axis=0, keepdims=True)
    )


def column(rows, at, width):
    only = jnp.where(lax.broadcasted_iota(jnp.int32, rows.shape, 0) == at, rows.astype(f32), 0.0).astype(bf)
    upright = tn(only, jnp.ones((TILE, 128), bf))
    return jnp.concatenate([upright] * (width // 128), axis=1)


def row_sums(values):
    ones = jnp.ones((8, values.shape[1]), bf)
    if values.dtype == bf:
        return nt(ones, values)
    high = values.astype(bf)
    return nt(ones, high) + nt(ones, (values - high.astype(f32)).astype(bf))


def gelu_pair(up_pre):
    square = up_pre * up_pre
    tanh_value = jnp.tanh(gelu_scale * (up_pre + 0.044715 * square * up_pre))
    half_one = 0.5 * (1.0 + tanh_value)
    slope = half_one + 0.5 * up_pre * (1.0 - tanh_value * tanh_value) * gelu_scale * (
        1.0 + 3.0 * 0.044715 * square
    )
    return up_pre * half_one, slope


def soft_columns(logits):
    top = jnp.exp(logits - jnp.max(logits, axis=0, keepdims=True))
    return top / jnp.sum(top, axis=0, keepdims=True)


def ahead_mask(starts, rows, first_column, columns):
    j = lax.broadcasted_iota(jnp.int32, (rows, columns), 0)
    i = lax.broadcasted_iota(jnp.int32, (rows, columns), 1) + first_column
    return (j <= i) & (j >= starts[0:1, first_column : first_column + columns])


def causal_pieces(tokens):
    step = tokens // 2
    return ((0, step, step), (step, step, tokens))


HBM = pl.BlockSpec(memory_space=pl.ANY)
IN_VMEM = pl.BlockSpec(memory_space=pltpu.VMEM)


def load_all(refs, places, sems):
    copies = [pltpu.make_async_copy(ref, place, sems.at[k]) for k, (ref, place) in enumerate(zip(refs, places))]
    for copy in copies:
        copy.start()
    return copies


def part_places(refs, scratch, core):
    return [scratch.at[2 * (k // 2) + (core if k % 2 == 0 else 1 - core)] for k in range(len(refs))]


def tables_body(nh, ids, pos_ref, row_ref, starts_ref, table_ref):
    length = pos_ref.shape[1]
    tok = length // nh
    h = ids[1]
    own = row_ref[:, pl.ds(pl.multiple_of(h * tok, 128), tok)]
    lane = lax.broadcasted_iota(jnp.int32, (8, tok), 1)
    starts_ref[...] = lane - own

    def start_of(t):
        return t - pos_ref[0, t]

    def flag(value):
        return jnp.where(value, 1, 0)

    run_last = start_of(length - 1)
    other = [h ^ m for m in range(nh)]
    values = [ids[0], start_of((h + 1) * tok - 1) - h * tok]
    values += [flag((q < h) & (start_of(h * tok) <= (q + 1) * tok - 1)) for q in other[1:]]
    values += [flag(start_of(h * tok) < 0)]
    values += [flag((q > h) & (start_of(q * tok) <= (h + 1) * tok - 1)) for q in other[1:]]
    values += [flag(run_last <= (h + 1) * tok - 1), h, ids[2]]
    values += [flag(run_last <= (q + 1) * tok - 1) for q in other]
    values += [flag(start_of(q * tok) < 0) for q in other]
    lane = lax.broadcasted_iota(jnp.int32, (8, 128), 1)
    table = jnp.zeros((8, 128), jnp.int32)
    for k, value in enumerate(values):
        table = jnp.where(lane == k, value, table)
    table_ref[...] = table


def state_sum_body(hp, nh, first, sc, *refs):
    for i in range(refs[nh].shape[0]):
        total = jnp.zeros(refs[0].shape[1:], f32)
        for m in range(nh):
            total += jnp.where(sc[first + m] > 0, refs[m][((i // hp) ^ m) * hp + i % hp].astype(f32), 0.0)
        refs[nh][i] = total.astype(bf)


def pack_body(sc, qkv_ref, qm_ref, km_ref, qb_ref, ub_ref, ob_ref, db_ref, out_ref, up_ref, down_ref,
              first_ref, other_ref, wa_ref, wb_ref, rows_ref):
    pc, model = qkv_ref.shape
    hs = qm_ref.shape[1]
    width = ob_ref.shape[1]
    rows_ref[...] = jnp.zeros_like(rows_ref)
    rows_ref[0:1, 0:pc] = qb_ref[...].astype(f32)
    rows_ref[1:2, 0 : ub_ref.shape[1]] = ub_ref[...].astype(f32)
    rows_ref[2:3, 0:width] = ob_ref[...].astype(f32)
    rows_ref[3:4, 0:width] = db_ref[...].astype(f32)
    for core, ref in ((sc[0], first_ref), (1 - sc[0], other_ref)):
        cut = pc // 2
        ref[0:cut, :] = qkv_ref[pl.ds(pl.multiple_of(core * cut, TILE), cut), :]
        ref[cut : cut + hs // 2, :] = jnp.zeros((hs // 2, model), bf)
        for i in range(qm_ref.shape[0] // hs):
            for k in range(2):
                rows = slice(i * hs + k * hs // 2, i * hs + (k + 1) * hs // 2)
                at = k * (model // 2) + 128 * i
                own = jnp.where(core == 0, qm_ref[rows, :].astype(f32), km_ref[rows, :].astype(f32))
                ref[cut : cut + hs // 2, at : at + hs] = own.astype(bf)
        cut += hs // 2
        ref[cut : cut + TILE, :] = rows_ref[...].astype(bf)
        half = out_ref.shape[0] // 2
        ref[cut + TILE :, :] = out_ref[pl.ds(pl.multiple_of(core * half, TILE), half), :]
    half = down_ref.shape[0] // 2
    at = pl.ds(pl.multiple_of(sc[0] * half, TILE), half)
    lanes = pl.ds(pl.multiple_of(sc[0] * half, 128), half)
    for k, w_ref in enumerate((wa_ref, wb_ref)):
        part = slice(k * half, (k + 1) * half)
        w_ref[:, 0:half] = up_ref[part, lanes]
        w_ref[:, half:] = down_ref[at, part]


def chunks_body(nh, sc, a_ref, b_ref, o_ref):
    tokens = o_ref.shape[3]
    for q in range(nh):
        for k, ref in enumerate((a_ref, b_ref)):
            o_ref[q, k] = ref[:, q * tokens : (q + 1) * tokens]


def first_norm_body(sc, x_ref, gain_ref, hid_ref):
    normed, _ = norm_columns(x_ref[...].astype(f32))
    width = x_ref.shape[1]
    gains = gain_ref[...]
    hid_ref[...] = (normed * column(gains, 0, width) + column(gains, 1, width)).astype(bf)


def turn_body(sc, a_ref, b_ref, o_ref):
    tokens = a_ref.shape[1]
    o_ref[0:tokens, :] = a_ref[...].T
    o_ref[tokens:, :] = b_ref[...].T


def map_of(first_ref, at, i, hs, cut):
    model = first_ref.shape[2]
    rows = slice(cut, cut + hs // 2)
    return jnp.concatenate(
        [first_ref[at, rows, k * (model // 2) + 128 * i : k * (model // 2) + 128 * i + hs] for k in range(2)], axis=0
    )


def project_body(hp, hs, count, sc, hid_ref, starts_ref, *refs):
    first_refs = refs[0 : 2 * count]
    proj_ref, qf_ref, kf_ref, va_ref, st_ref, w_ref, sems = refs[-7:]
    p = pl.program_id(0)
    wait_for_piece(first_refs, w_ref, sems, sc)
    pc, tokens = proj_ref.shape[1:]
    cut = pc // 2
    bias = column(w_ref[2 * p, cut + hs // 2 : cut + hs // 2 + TILE, 0:pc], 0, tokens)
    for k in range(2):
        rows = slice(k * cut, (k + 1) * cut)
        proj_ref[0, rows, :] = (nn(w_ref[2 * p + k, 0:cut, :], hid_ref[...]) + bias[rows, :]).astype(bf)
    included = (starts_ref[0:1, :] == sc[1]).astype(f32)
    extra = lax.broadcasted_iota(jnp.int32, (AUG - hs, tokens), 0)
    extra = jnp.where(extra < 2, 1.0, 0.0).astype(bf)
    for i in range(hp):
        row = 3 * hs * i
        for part, out in ((0, qf_ref), (1, kf_ref)):
            own_map = map_of(w_ref, 2 * p + part, i, hs, cut)
            logits = tn(own_map, proj_ref[0, row + part * hs : row + (part + 1) * hs, :])
            out[i, 0:hs, :] = soft_columns(logits).astype(bf)
            out[i, hs : 2 * hs, :] = soft_columns(-logits).astype(bf)
        va_ref[i, 0:hs, :] = proj_ref[0, row + 2 * hs : row + 3 * hs, :]
        va_ref[i, hs:AUG, :] = extra
        kept = (va_ref[i].astype(f32) * included).astype(bf)
        st_ref[i] = nt(kept, kf_ref[i]).astype(bf)


def wait_for_piece(first_refs, w_ref, sems, sc):
    p = pl.program_id(0)
    places = part_places(first_refs, w_ref, sc[0])
    rows = w_ref.shape[1]
    copies = [
        pltpu.make_async_copy(ref.at[pl.ds(0, rows), :], place, sems.at[k])
        for k, (ref, place) in enumerate(zip(first_refs, places))
    ]

    @pl.when(p == 0)
    def _():
        for copy in copies:
            copy.start()

    for k, copy in enumerate(copies):

        @pl.when(p == k // 2)
        def _(copy=copy):
            copy.wait()


def local_mix_body(hp, sc, qf_ref, kf_ref, va_ref, starts_ref, num_ref):
    tokens = qf_ref.shape[2]
    starts = starts_ref[...]
    for first, width, rows in causal_pieces(tokens):
        mask = ahead_mask(starts, rows, first, width)
        for i in range(hp):
            scores = tn(kf_ref[i, :, 0:rows], qf_ref[i, :, first : first + width])
            scores = jnp.where(mask, scores, 0.0).astype(bf)
            num_ref[i, :, first : first + width] = nn(va_ref[i, :, 0:rows], scores)


def weighted_state(sc, slot, refs, i, hp):
    total = jnp.where(sc[slot + len(refs) - 1] > 0, refs[-1][i].astype(f32), 0.0)
    for m, ref in enumerate(refs[:-1], 1):
        total += jnp.where(sc[slot + m - 1] > 0, ref[((i // hp) ^ m) * hp + i % hp].astype(f32), 0.0)
    return total


def load_out_weight(sc, first_refs, w_ref, sems):
    rows = w_ref.shape[0] // len(first_refs)
    at = first_refs[0].shape[0] - rows
    places = [
        w_ref.at[pl.ds(pl.multiple_of(rows * (2 * (k // 2) + (sc[0] if k % 2 == 0 else 1 - sc[0])), TILE), rows), :]
        for k in range(len(first_refs))
    ]
    return load_all([ref.at[pl.ds(at, rows), :] for ref in first_refs], places, sems)


def mix_out_body(hp, hs, nh, sc, num_ref, qf_ref, starts_ref, x_ref, gain_ref, *refs):
    state_refs, row_refs, wo_refs = refs[0:nh], refs[nh : 2 * nh], refs[2 * nh : 4 * nh]
    sin_ref, mixd_ref, mix_ref, res_ref, top_ref, low_ref, w_ref, sems = refs[4 * nh :]
    copies = load_out_weight(sc, wo_refs, w_ref, sems)
    uses = starts_ref[0:1, :] < 0
    model, tokens = x_ref.shape
    for i in range(num_ref.shape[0]):
        state = weighted_state(sc, 2, state_refs, i, hp).astype(bf)
        sin_ref[i] = state
        num = num_ref[i] + jnp.where(uses, nn(state, qf_ref[i]), 0.0)
        mixture = num[0:hs, :] / num[hs : hs + 1, :]
        mixd_ref[i, 0:hs, :] = mixture
        mixd_ref[i, hs : hs + 8, :] = num[hs : hs + 8, :]
        mix_ref[i * hs : (i + 1) * hs, :] = mixture.astype(bf)
    for copy in copies:
        copy.wait()
    res_ref[...] = x_ref[...].astype(f32) + tn(w_ref[...], mix_ref[...])
    width = model // nh
    h = sc[2 + 2 * nh]
    for j in range(nh):
        rows = pl.ds(pl.multiple_of((h ^ j) * width, TILE), width)
        res_ref[rows, :] += column(row_refs[j][:, 0:width], 2, tokens)
    normed, _ = norm_columns(res_ref[...].astype(bf).astype(f32))
    gains = gain_ref[...]
    hidden = (normed * column(gains, 2, tokens) + column(gains, 3, tokens)).astype(bf)
    half = top_ref.shape[0]
    top_ref[...] = hidden[0:half, :]
    low_ref[...] = hidden[half:, :]


def feed_body(count, first, last, sc, *refs):
    hidt_ins, gyt_ins, gy_in = refs[0:4], refs[4:6], refs[6]
    row_refs = refs[7 : 7 + count]
    w_ins = refs[7 + count : 7 + 3 * count]
    refs = refs[7 + 3 * count :]
    if first:
        out_ref, sg_ref = refs[0:2]
        refs = refs[2:]
    elif not last:
        out_in, sg_in, out_ref, sg_ref = refs[0:4]
        refs = refs[4:]
    else:
        out_in, sg_in, out_own, out_peer, sg_own, sg_peer = refs[0:6]
        refs = refs[6:]
    w_refs, ub_ref, refs = refs[0:count], refs[count], refs[count + 1 :]
    hid_ref, act_ref, ug_ref = refs
    mid, tokens = hidt_ins[0].shape
    model = 2 * mid
    half = act_ref.shape[1]
    runs = [slice(0, tokens), slice(tokens, 2 * tokens)]
    lo, hi = slice(0, half), slice(half, 2 * half)
    at_half = pl.ds(pl.multiple_of(sc[0] * half, 128), half)
    for k in range(count):
        bias = row_refs[k][:, at_half].astype(f32)[1:2, :]
        first_w, second_w = w_ins[2 * k], w_ins[2 * k + 1]
        for which, rows in enumerate(runs):
            if k == 0:
                for m in range(2):
                    hid_ref[rows, m * mid : (m + 1) * mid] = hidt_ins[2 * which + m][...].T
            up_pre = nn(hid_ref[rows, lo], first_w[:, lo]) + nn(hid_ref[rows, hi], second_w[:, lo]) + bias
            value, slope = gelu_pair(up_pre)
            act_ref[rows, :] = value.astype(bf)
            back = nt(gy_in[rows, lo], first_w[:, hi]) + nt(gy_in[rows, hi], second_w[:, hi])
            ug_ref[rows, :] = (back * slope).astype(bf)
        ub_ref[k] = nn(jnp.ones((8, 2 * tokens), bf), ug_ref[...])
        for m in range(2):
            grads = [nn(hidt_ins[2 * r + m][...], ug_ref[runs[r], :]) for r in range(2)]
            w_refs[k][m * mid : (m + 1) * mid, :] = (grads[0] + grads[1]).astype(bf)
        grads = [nn(gyt_ins[r][...], act_ref[runs[r], :]) for r in range(2)]
        w_refs[k][model : 2 * model, :] = (grads[0] + grads[1]).astype(bf)
        w_refs[k][2 * model :, :] = jnp.zeros((TILE, half), bf)
        for at, w in ((lo, first_w), (hi, second_w)):
            if first and k == 0:
                out_ref[:, at] = nn(act_ref[...], w[:, hi])
                sg_ref[at, :] = nt(w[:, lo], ug_ref[...])
            elif not last and k == 0:
                out_ref[:, at] = out_in[:, at] + nn(act_ref[...], w[:, hi])
                sg_ref[at, :] = sg_in[at, :] + nt(w[:, lo], ug_ref[...])
            elif not last:
                out_ref[:, at] += nn(act_ref[...], w[:, hi])
                sg_ref[at, :] += nt(w[:, lo], ug_ref[...])
            else:
                out = out_in[:, at] + nn(act_ref[...], w[:, hi])
                out_own[:, at] = out[runs[0], :]
                out_peer[:, at] = out[runs[1], :].astype(bf)
                sg = sg_in[at, :] + nt(w[:, lo], ug_ref[...])
                sg_own[at, :] = sg[:, runs[0]]
                sg_peer[at, :] = sg[:, runs[1]].astype(bf)


def block_out_body(nh, sc, res_ref, out_ref, out2_ref, tg_ref, *refs):
    row_refs, o_ref, total_ref = refs[0:nh], refs[nh], refs[nh + 1]
    model, tokens = res_ref.shape
    width = model // nh
    total_ref[...] = res_ref[...] + (out_ref[...] + out2_ref[...].astype(f32)).T
    h = sc[2 + 2 * nh]
    for j in range(nh):
        rows = pl.ds(pl.multiple_of((h ^ j) * width, TILE), width)
        o_ref[j, 1] = tg_ref[j]
        o_ref[h ^ j, 0] = (total_ref[rows, :] + column(row_refs[j][:, 0:width], 3, tokens)).astype(bf)


def lay_out_body(nh, sc, in_ref, *o_refs):
    tokens = in_ref.shape[3]
    for k in range(2):
        for q in range(nh):
            o_refs[k][:, q * tokens : (q + 1) * tokens] = in_ref[q, k]


def second_back_body(hs, nh, sc, sg_ref, sg2_ref, res_ref, gyt_ref, gain_ref, mixd_ref, starts_ref, qf_ref, *refs):
    wo_refs, (rg_ref, ag_ref, vec_ref, na_ref, sgt_ref, w_ref, sems) = refs[0 : 2 * nh], refs[2 * nh :]
    copies = load_out_weight(sc, wo_refs, w_ref, sems)
    model, tokens = sg_ref.shape
    width = model // nh
    normed, inv_std = norm_columns(res_ref[...].astype(bf).astype(f32))
    sg = sg_ref[...] + sg2_ref[...].astype(f32)
    res_grad = gyt_ref[...].astype(f32) + norm_columns_back(sg, normed, inv_std, column(gain_ref[...], 2, tokens))
    rg_ref[...] = res_grad
    ag_ref[...] = res_grad.astype(bf)
    uses = (starts_ref[0:1, :] < 0).astype(f32)
    for copy in copies:
        copy.wait()
    mg = nn(w_ref[...], ag_ref[...])
    row = lax.broadcasted_iota(jnp.int32, (AUG - hs, tokens), 0)
    for i in range(qf_ref.shape[0]):
        num = mg[i * hs : (i + 1) * hs, :] / mixd_ref[i, hs : hs + 1, :]
        den = -jnp.sum(num * mixd_ref[i, 0:hs, :], axis=0, keepdims=True)
        high = den.astype(bf).astype(f32)
        extra = jnp.where(row == 0, high, jnp.where(row == 1, den - high, 0.0))
        na_ref[i, 0:hs, :] = num.astype(bf)
        na_ref[i, hs:AUG, :] = extra.astype(bf)
        kept = (na_ref[i].astype(f32) * uses).astype(bf)
        sgt_ref[i] = nt(kept, qf_ref[i]).astype(bf)
    for at, value in enumerate((sg * normed, sg, ag_ref[...], gyt_ref[...])):
        sums = row_sums(value)
        for p in range(nh):
            vec_ref[p, at : at + 1, :] = sums[0:1, p * width : (p + 1) * width]


def halves_back(feat, grad, hs):
    parts = []
    for k in range(2):
        soft = feat[k * hs : (k + 1) * hs, :].astype(f32)
        own = grad[k * hs : (k + 1) * hs, :]
        weight = jnp.sum(soft * own, axis=0, keepdims=True) / jnp.sum(soft, axis=0, keepdims=True)
        parts.append(soft * (own - weight))
    return (parts[0] - parts[1]).astype(bf)


def local_back_body(hp, hs, sc, qf_ref, kf_ref, va_ref, na_ref, sin_ref, starts_ref, ql_ref, kfg_ref, vg_ref):
    tokens = qf_ref.shape[2]
    starts = starts_ref[...]
    step = tokens // 2
    uses = starts[0:1, :] < 0
    masks = [ahead_mask(starts, rows, first, width) for first, width, rows in causal_pieces(tokens)]
    for i in range(hp):
        na = na_ref[i]
        through = tn(sin_ref[i], na)
        for which, (first, width, rows) in enumerate(causal_pieces(tokens)):
            at = slice(first, first + width)
            mask = masks[which]
            scores = jnp.where(mask, tn(kf_ref[i, :, 0:rows], qf_ref[i, :, at]), 0.0).astype(bf)
            sgrad = jnp.where(mask, tn(va_ref[i, :, 0:rows], na[:, at]), 0.0).astype(bf)
            qfg = nn(kf_ref[i, :, 0:rows], sgrad) + jnp.where(uses[:, at], through[:, at], 0.0)
            ql_ref[i, :, at] = halves_back(qf_ref[i, :, at], qfg, hs)
            kfg = nt(qf_ref[i, :, at], sgrad)
            vg = nt(na[:, at], scores)[0:hs, :]
            if which == 0:
                kfg_ref[i, :, 0:rows] = kfg
                vg_ref[i, :, 0:rows] = vg
            else:
                kfg_ref[i, :, 0:step] += kfg[:, 0:step]
                vg_ref[i, :, 0:step] += vg[:, 0:step]
                kfg_ref[i, :, step:] = kfg[:, step:]
                vg_ref[i, :, step:] = vg[:, step:]


def join_extra(state, hs):
    row = lax.broadcasted_iota(jnp.int32, state.shape, 0)
    both = state[hs : hs + 1, :] + state[hs + 1 : hs + 2, :]
    return jnp.where(row < hs, state, jnp.where(row == hs, both, 0.0))


def project_back_body(hp, hs, nh, sc, *refs):
    state_refs, first_refs, refs = refs[0:nh], refs[nh : 3 * nh], refs[3 * nh :]
    kf_ref, va_ref, ql_ref, kfg_ref, vg_ref, proj_ref, starts_ref, *pg_refs, fg_ref, mg_ref, pb_ref, pg_ref, first_ref, sems = refs
    p = pl.program_id(0)
    wait_for_piece(first_refs, first_ref, sems, sc)
    included = starts_ref[0:1, :] == sc[1]
    cut = pg_ref.shape[1] // 2
    for i in range(hp):
        total = jnp.where(sc[1 + 2 * nh] > 0, state_refs[-1][i].astype(f32), 0.0)
        for m in range(1, nh):
            total += jnp.where(sc[1 + nh + m] > 0, state_refs[m - 1][i].astype(f32), 0.0)
        state = join_extra(total, hs).astype(bf)
        kfg = kfg_ref[i] + jnp.where(included, tn(state, va_ref[i]), 0.0)
        vg = vg_ref[i] + jnp.where(included, nn(state, kf_ref[i])[0:hs, :], 0.0)
        klg = halves_back(kf_ref[i], kfg, hs)
        qlg = ql_ref[i]
        row = 3 * hs * i
        pg_ref[0, row : row + hs, :] = nn(map_of(first_ref, 2 * p, i, hs, cut), qlg).astype(bf)
        pg_ref[0, row + hs : row + 2 * hs, :] = nn(map_of(first_ref, 2 * p + 1, i, hs, cut), klg).astype(bf)
        pg_ref[0, row + 2 * hs : row + 3 * hs, :] = vg.astype(bf)
        q_grad = nt(proj_ref[0, row : row + hs, :], qlg)
        k_grad = nt(proj_ref[0, row + hs : row + 2 * hs, :], klg)
        mg_ref[0, :, 128 * i : 128 * (i + 1)] = jnp.concatenate([q_grad, k_grad], axis=1)
    for j, ref in enumerate(pg_refs):

        @pl.when(p == j)
        def _(ref=ref):
            ref[...] = pg_ref[0]

    pb_ref[0] = row_sums(pg_ref[0])
    grad = tn(first_ref[2 * p, 0:cut, :], pg_ref[0, 0:cut, :]) + tn(first_ref[2 * p + 1, 0:cut, :], pg_ref[0, cut:, :])

    @pl.when(pl.program_id(0) == 0)
    def _():
        fg_ref[...] = grad

    @pl.when(pl.program_id(0) > 0)
    def _():
        fg_ref[...] += grad


def first_back_body(nh, sc, fg_ref, x_ref, rg_ref, gain_ref, tg_ref, vec_ref):
    model, tokens = fg_ref.shape
    width = model // nh
    normed, inv_std = norm_columns(x_ref[...].astype(f32))
    fg = fg_ref[...]
    gain = column(gain_ref[...], 0, tokens)
    tg = (rg_ref[...] + norm_columns_back(fg, normed, inv_std, gain)).astype(bf)
    for p in range(nh):
        tg_ref[p] = tg[p * width : (p + 1) * width, :]
    for at, value in enumerate((fg * normed, fg)):
        sums = row_sums(value)
        for p in range(nh):
            vec_ref[p, at : at + 1, :] = sums[0:1, p * width : (p + 1) * width]


def split_quarters(nh, nz, sc, total_ref, keep_ref, send_ref):
    part = total_ref.shape[0] // nz
    for k in range(nz):
        o_ref = keep_ref if k % 2 == 0 else send_ref
        at = pl.ds(pl.multiple_of((sc[3 + 2 * nh] ^ k) * part, TILE), part)
        o_ref[(k // 2) * part : (k // 2 + 1) * part, :] = total_ref[at, :]


def feed_sum_body(nh, nz, sc, *refs):
    keep_ref, send_ref, total_ref = refs[nh:]
    rows = total_ref.shape[0]
    total_ref[...] = sum(ref[0:rows, :].astype(f32) for ref in refs[0:nh]).astype(bf)
    split_quarters(nh, nz, sc, total_ref, keep_ref, send_ref)


def last_sum_body(nh, nz, sc, *refs):
    keep_ref, send_ref, total_ref = refs[nh:]
    total_ref[...] = sum(ref[...].astype(f32) for ref in refs[0:nh]).astype(bf)
    split_quarters(nh, nz, sc, total_ref, keep_ref, send_ref)


def pair_sum_body(sc, own_ref, got_ref, keep_ref, send_ref):
    part = keep_ref.shape[0]
    keep_ref[...] = (own_ref[0:part, :].astype(f32) + got_ref[0:part, :].astype(f32)).astype(bf)
    send_ref[...] = (own_ref[part:, :].astype(f32) + got_ref[part:, :].astype(f32)).astype(bf)


def last_grads_body(nh, sc, *refs):
    pg_refs, pg2_refs, refs = refs[0:nh], refs[nh : 2 * nh], refs[2 * nh :]
    hid_ref, hid2_ref, mg_ref, pb_ref, own_ref, early_ref, late_ref, vec1_ref, vec2_ref = refs[0:9]
    mix_ref, mix2_ref, ag_ref, ag2_ref, *o_refs, rows_ref = refs[9:]
    pc, half = pg_refs[0].shape[0], hid_ref.shape[0]
    hs = mg_ref.shape[1]
    width = vec1_ref.shape[2]
    h = sc[2 + 2 * nh]
    for j in range(nh):
        o_ref = o_refs[j]
        o_ref[0:pc, :] = (nt(pg_refs[j][...], hid_ref[...]) + nt(pg2_refs[j][...], hid2_ref[...])).astype(bf)
        o_ref[pc : pc + hs, :] = mg_ref[j].astype(bf)
        ub_ref, k = (own_ref, 0) if j == 0 else (early_ref, j - 1) if j < nh - 1 else (late_ref, 0)
        rows_ref[...] = jnp.zeros_like(rows_ref)
        rows_ref[0:1, :] = pb_ref[j, 0:1, 0:half]
        rows_ref[1:2, 0 : pc - half] = pb_ref[j, 0:1, half:]
        rows_ref[2:3, :] = jnp.where(sc[0] == 0, ub_ref[k, 0:1, :], 0.0)
        rows_ref[3:4, :] = jnp.where(sc[0] == 0, 0.0, ub_ref[k, 0:1, :])
        rows_ref[4:8, 0:width] = vec2_ref[h ^ j, 0:4, :]
        rows_ref[8:10, 0:width] = vec1_ref[h ^ j, 0:2, :]
        at = pc + hs + TILE
        o_ref[pc + hs : at, :] = rows_ref[...].astype(bf)
        rows = slice(j * width, (j + 1) * width)
        o_ref[at : at + width, :] = (nt(mix_ref[rows, :], ag_ref[...]) + nt(mix2_ref[rows, :], ag2_ref[...])).astype(bf)
        o_ref[at + width :, :] = jnp.zeros((o_ref.shape[0] - at - width, half), bf)


def join_quarters(nh, nz, sc, refs, total_ref):
    part = refs[0].shape[0]
    for k in range(2 * nz):
        at = pl.ds(pl.multiple_of((sc[3 + 2 * nh] ^ (k % nz)) * part, TILE), part)
        total_ref[k // nz, at, :] = refs[k][...]


def feed_out_body(nh, nz, sc, *refs):
    up_ref, down_ref, total_ref = refs[2 * nz :]
    join_quarters(nh, nz, sc, refs, total_ref)
    model = down_ref.shape[1]
    half = total_ref.shape[2]
    for k, core in enumerate((sc[0], 1 - sc[0])):
        at = pl.ds(pl.multiple_of(core * half, 128), half)
        up_ref[:, at] = total_ref[k, 0:model, :].astype(f32)
        down_ref[at, :] = total_ref[k, model : 2 * model, :].astype(f32).T


def last_out_body(hs, nh, nz, sc, *refs):
    qkv_ref, out_ref, qm_ref, km_ref, qb_ref, ub_ref, vec_ref, total_ref = refs[2 * nz :]
    join_quarters(nh, nz, sc, refs, total_ref)
    pc = qkv_ref.shape[0]
    half = total_ref.shape[2]
    for k, core in enumerate((sc[0], 1 - sc[0])):
        at = pl.ds(pl.multiple_of(core * half, 128), half)
        qkv_ref[:, at] = total_ref[k, 0:pc, :].astype(f32)
        first = pc + hs + TILE
        out_ref[:, at] = total_ref[k, first : first + out_ref.shape[0], :].astype(f32)
    maps = total_ref[0, pc : pc + hs, :].astype(f32) + total_ref[1, pc : pc + hs, :].astype(f32)
    for i in range(qm_ref.shape[0]):
        qm_ref[i] = maps[:, 128 * i : 128 * i + hs]
        km_ref[i] = maps[:, 128 * i + hs : 128 * i + 2 * hs]
    rows = slice(pc + hs, pc + hs + TILE)
    rows = total_ref[0, rows, :].astype(f32) + total_ref[1, rows, :].astype(f32)
    qb_ref[:, 0:half] = rows[0:1, :]
    qb_ref[:, half:] = rows[1:2, 0 : pc - half]
    ub_ref[:, 0:half] = rows[2:3, :]
    ub_ref[:, half:] = rows[3:4, :]
    vec_ref[...] = rows


def swap(a, axis, k):
    n = lax.axis_size(axis)
    return lax.ppermute(a, axis, [(i, i ^ k) for i in range(n)])


def trade(a, axis):
    return lax.all_to_all(a, axis, 0, 0, tiled=True)


def after(a, *others):
    return lax.optimization_barrier((a,) + others)[0]


def chain_seq(part, forward, weight_of):
    n = lax.axis_size("seq")
    total = None
    for k in range(1, n):
        pairs = [(i, i + k) if forward else (i + k, i) for i in range(n - k)]
        if n == 2:
            return lax.ppermute(part, "seq", pairs)
        sent = part if forward else part * weight_of(k).astype(part.dtype)
        got = lax.ppermute(sent, "seq", pairs).astype(f32) * (weight_of(k) if forward else 1.0)
        total = got if total is None else total + got
    return total.astype(bf)


def local(tokens, attn_gain, attn_shift, qkv_weight, qkv_bias, query_map, key_map, out_weight, out_bias,
          mlp_gain, mlp_shift, up_weight, up_bias, down_weight, down_bias, positions, out_grad):
    nh, ns, nz = lax.axis_size("head"), lax.axis_size("seq"), lax.axis_size("dp")
    length, width = tokens.shape[1], tokens.shape[2]
    model = width * nh
    half = model // 2
    hp, hs = query_map.shape[0], query_map.shape[1]
    heads = hp * nh
    pc = qkv_weight.shape[1]
    hidden = up_weight.shape[1]
    hh = hidden // 2
    tok = length // nh
    h = lax.axis_index("head")
    s2 = lax.axis_index("seq") % 2
    peers = range(1, nh)

    ids = jnp.stack([s2, h, lax.axis_index("dp")]).astype(jnp.int32)
    starts, table = pl.pallas_call(
        functools.partial(tables_body, nh),
        out_shape=[shape((8, tok), jnp.int32), shape((8, 128), jnp.int32)],
        in_specs=[pl.BlockSpec(memory_space=pltpu.SMEM), pl.BlockSpec(memory_space=pltpu.SMEM),
                  pl.BlockSpec(memory_space=pltpu.VMEM)],
        name="tables",
    )(ids, positions, positions)
    sc = table[0, 0 : 4 + 4 * nh]
    run_start = -positions[0, 0]

    def beyond_chip(total):
        base = total
        for k in range(1, ns // 2):
            total += lax.ppermute(base, "seq", [(i, (i + 2 * k) % ns) for i in range(ns)])
        return total

    (both,) = run_kernel(
        functools.partial(chunks_body, nh), "chunks", (1,), ids, [(tokens[0].T, None), (out_grad[0].T, None)],
        [(shape((nh, 2, width, tok), bf), None)],
    )
    both = trade(both, "head")

    core_of = jnp.full((1,), s2, jnp.int32)
    gains = jnp.pad(jnp.stack([attn_gain, attn_shift, mlp_gain, mlp_shift]), ((0, TILE - 4), (0, 0)))
    fl = pc // 2 + hs // 2 + TILE
    fr = fl + width // 2
    own, other_half, wa_own, wb_own = run_kernel(
        pack_body, "pack_weights", (1,), core_of,
        [(a, None) for a in (qkv_weight.T, query_map.reshape(-1, hs), key_map.reshape(-1, hs), qkv_bias[None], up_bias[None],
                             out_bias[None], down_bias[None], out_weight, up_weight, down_weight)],
        [(shape((fr, model), bf), None), (shape((fr, model), bf), None), (shape((hh, 2 * hh), bf), None), (shape((hh, 2 * hh), bf), None)],
        scratch=[pltpu.VMEM((TILE, model), f32)],
    )
    x, gyt = [both[:, k].reshape(model, tok) for k in range(2)]
    own = after(own, sc)
    first_got = [swap(own, "head", m) for m in peers]
    x, gyt = after(x, *first_got[:-1]), after(gyt, *first_got[:-1])
    gyt_peer = swap(gyt, "seq", 1)
    (hid,) = run_kernel(
        first_norm_body, "first_norm", (1,), core_of, [(x, None), (gains, None)], [(shape((model, tok), bf), None)]
    )
    hid_peer = swap(lax.dynamic_slice_in_dim(hid, (1 - s2) * half, half, 0), "seq", 1)
    (gy,) = run_kernel(
        turn_body, "turn_grad", (1,), core_of, [(gyt, None), (gyt_peer, None)], [(shape((2 * tok, model), bf), None)]
    )
    firsts_of = [[own, other_half]] + [[a, swap(after(a, hid), "seq", 1)] for a in first_got[:-1]]
    row_specs = [(pair[0], pl.BlockSpec((TILE, model), lambda *_: (fl // TILE - 1, 0))) for pair in firsts_of + [first_got[-1:]]]
    in_hbm = lambda arrays: [(a, HBM) for a in arrays]
    first_scratch = [pltpu.VMEM((2 * nh, fl, model), bf), pltpu.SemaphoreType.DMA((2 * nh,))]
    wo_scratch = [pltpu.VMEM((model, model), bf), pltpu.SemaphoreType.DMA((2 * nh,))]

    va_spec, state_spec, feat_spec = lead(hp, AUG, tok), lead(hp, AUG, 2 * hs), lead(hp, 2 * hs, tok)
    hid_now = after(hid, gyt_peer, hid_peer)

    def project(first_piece, count, so_far):
        def at(spec):
            return pl.BlockSpec(spec.block_shape, lambda p, sc: (p + first_piece,) + (0,) * (len(spec.block_shape) - 1))

        outs = [(shape((nh, pc, tok), bf), at(lead(1, pc, tok))), (shape((heads, 2 * hs, tok), bf), at(feat_spec)),
                (shape((heads, 2 * hs, tok), bf), at(feat_spec)), (shape((heads, AUG, tok), bf), at(va_spec)),
                (shape((heads, AUG, 2 * hs), bf), at(state_spec))]
        arrays = [a for pair in firsts_of[first_piece : first_piece + count] for a in pair]
        return run_kernel(
            functools.partial(project_body, hp, hs, count), f"project_{first_piece}", (count,), sc,
            [(hid_now, None), (starts, None)] + in_hbm(arrays) + in_hbm(so_far), outs,
            scratch=[pltpu.VMEM((2 * count, fl, model), bf), pltpu.SemaphoreType.DMA((2 * count,))],
            aliases={3 + 2 * count + k: k for k in range(len(so_far))},
        )

    so_far = project(0, nh - 1, ())
    far = after(first_got[-1], so_far[-1])
    firsts_of.append([far, after(swap(far, "seq", 1), so_far[-1])])
    all_first = [a for pair in firsts_of for a in pair]
    proj, qf, kf, va, states = project(nh - 1, 1, so_far)
    wa_own = after(wa_own, *first_got[:-1])
    wa_x, wa_y = swap(wa_own, "head", 1), swap(wa_own, "head", 2)
    (num,) = run_kernel(
        functools.partial(local_mix_body, hp), "local_mix", (nh,), sc,
        [(qf, feat_spec), (kf, feat_spec), (after(va, gy, wa_x, wa_y), va_spec), (starts, None)],
        [(shape((heads, AUG, tok), f32), va_spec)],
    )
    around = [after(swap(states, "head", m), num) for m in peers]

    def states_together(first, arrays):
        (total,) = run_kernel(
            functools.partial(state_sum_body, hp, nh, first), f"state_sum_{first}", (1,), sc, [(a, None) for a in arrays],
            [(shape((heads, AUG, 2 * hs), bf), None)],
        )
        return total

    whole_run = states_together(4 + 2 * nh, [states] + around)
    before = chain_seq(whole_run, True, lambda k: (run_start <= -(k - 1) * length - 1).astype(f32))

    wb_own = after(wb_own, before)
    wb_x, wb_y = swap(wb_own, "head", 1), swap(wb_own, "head", 2)

    sin, mixd, mix, res, *hidt2 = run_kernel(
        functools.partial(mix_out_body, hp, hs, nh), "mix_out", (1,), sc,
        [(a, None) for a in (num, qf, starts, x, gains, *around, before)] + row_specs + in_hbm(all_first),
        [(shape((heads, AUG, 2 * hs), bf), None), (shape((heads, hs + 8, tok), f32), None), (shape((model, tok), bf), None),
         (shape((model, tok), f32), None), (shape((half, tok), bf), None), (shape((half, tok), bf), None)],
        scratch=wo_scratch,
    )
    hidt2_peer = [swap(a, "seq", 1) for a in hidt2]
    wa_far = swap(after(wa_x, mix), "head", 2)
    w_all = [[wa_own, wb_own], [wa_x, wb_x], [wa_y, wb_y]]

    all_rows = 2 * model

    def feed(which, sums, last=False):
        count = len(which)
        if last:
            outs = [shape((tok, model), f32), shape((tok, model), bf), shape((model, tok), f32), shape((model, tok), bf)]
        else:
            outs = [shape((2 * tok, model), f32), shape((model, 2 * tok), f32)]
        return run_kernel(
            functools.partial(feed_body, count, not sums, last), f"feed_{which[0]}", (1,), sc,
            [(a, IN_VMEM) for a in (*hidt2, *hidt2_peer, gyt, gyt_peer, gy)] + [row_specs[j] for j in which]
            + [(a, IN_VMEM) for j in which for a in w_all[j]] + [(a, IN_VMEM) for a in sums],
            [(a, None if last else IN_VMEM) for a in outs] + [(shape((2 * model + TILE, hh), bf), None)] * count + [(shape((count, 8, hh), f32), None)],
            scratch=[pltpu.VMEM((2 * tok, model), bf), pltpu.VMEM((2 * tok, hh), bf), pltpu.VMEM((2 * tok, hh), bf)],
        )

    own_out, own_sg, w_zero, own_ub = feed([0], ())
    w_all[1:3] = [[after(a, own_ub) for a in pair] for pair in w_all[1:3]]
    w_all.append([wa_far, swap(w_all[2][1], "head", 1)])
    part_out, part_sg, *early = feed(list(range(1, nh - 1)), (own_out, own_sg))
    w_parts, early_ub = [w_zero] + early[:-1], early[-1]
    w_got = [swap(w_parts[m], "head", m) for m in range(1, nh - 1)]
    mix_peer = swap(after(mix, early_ub), "seq", 1)
    out_own, out_send, sg_own, sg_send, w_last, late_ub = feed([nh - 1], (part_out, part_sg), True)
    sg_recv = swap(sg_send, "seq", 1)

    vec_block = (shape((nh, 8, width), f32), None)
    rg, ag, vec2, na, sgt = run_kernel(
        functools.partial(second_back_body, hs, nh), "second_back", (1,), sc,
        [(a, None) for a in (sg_own, sg_recv, res, gyt, gains, mixd, starts, qf)] + in_hbm(all_first),
        [(shape((model, tok), f32), None), (shape((model, tok), bf), None), vec_block,
         (shape((heads, AUG, tok), bf), None), (shape((heads, AUG, 2 * hs), bf), None)],
        scratch=wo_scratch,
    )
    sgt = after(sgt, *w_got)
    g_sent = [swap(sgt, "head", m) for m in peers]
    half_spec = pl.BlockSpec((half, tok), lambda p, sc: (sc[0], 0))
    ag_peer = swap(lax.dynamic_slice_in_dim(ag, (1 - s2) * half, half, 0), "seq", 1)

    na_late = na
    ql, kfg, vg = run_kernel(
        functools.partial(local_back_body, hp, hs), "local_back", (nh,), sc,
        [(qf, feat_spec), (kf, feat_spec), (va, va_spec), (na_late, va_spec), (sin, state_spec), (starts, None)],
        [(shape((heads, hs, tok), bf), lead(hp, hs, tok)), (shape((heads, 2 * hs, tok), f32), feat_spec),
         (shape((heads, hs, tok), f32), lead(hp, hs, tok))],
    )
    g_around = [after(a, ql) for a in g_sent]
    w_got.append(swap(after(w_last, *g_around), "head", nh - 1))
    g_whole = states_together(4 + 3 * nh, [sgt] + g_around)
    after_run = chain_seq(g_whole, False, lambda k: (run_start <= -(k - 1) * length - 1).astype(f32))
    def peer_states(a, m):
        return (a, pl.BlockSpec((hp, AUG, 2 * hs), lambda p, sc: (p ^ m, 0, 0)))

    *pg, fg, map_grads, pb = run_kernel(
        functools.partial(project_back_body, hp, hs, nh), "project_back", (nh,), sc,
        [peer_states(a, m) for a, m in zip(g_around + [after_run], [*peers, 0])] + in_hbm(all_first)
        + [(kf, feat_spec), (va, va_spec), (ql, lead(hp, hs, tok)), (after(kfg, ag_peer, mix_peer), feat_spec), (vg, lead(hp, hs, tok)),
           (proj, lead(1, pc, tok)), (starts, None)],
        [(shape((pc, tok), bf), None)] * nh
        + [(shape((model, tok), f32), None),
           (shape((nh, hs, 128 * hp), f32), lead(1, hs, 128 * hp)), (shape((nh, 8, pc), f32), lead(1, 8, pc))],
        scratch=[pltpu.VMEM((1, pc, tok), bf)] + first_scratch,
    )
    pg_peer = [swap(a, "seq", 1) for a in pg]
    tg, vec1 = run_kernel(
        functools.partial(first_back_body, nh), "first_back", (1,), sc,
        [(fg, None), (x, None), (rg, None), (gains, None)], [(shape((nh, width, tok), bf), None), vec_block],
    )
    last_rows = -(-(pc + hs + TILE + width) // (nz * TILE)) * nz * TILE
    last_parts = run_kernel(
        functools.partial(last_grads_body, nh), "last_grads", (1,), sc,
        [(a, None) for a in (*pg, *pg_peer)] + [(hid, half_spec), (hid_peer, None)]
        + [(a, None) for a in (after(map_grads, w_got[-1]), pb, own_ub, early_ub, late_ub, vec1, vec2, mix, mix_peer)]
        + [(ag, half_spec), (ag_peer, None)],
        [(shape((last_rows, half), bf), None)] * nh,
        scratch=[pltpu.VMEM((TILE, half), f32)],
    )

    feed_rows, part_rows = all_rows // nz, last_rows // nz

    def halves_of(body, name, arrays, rows):
        return run_kernel(
            functools.partial(body, nh, nz), name, (1,), sc, [(a, None) for a in arrays],
            [(shape((2 * rows, hh), bf), None)] * 2, scratch=[pltpu.VMEM((nz * rows, hh), bf)],
        )

    def quarter(name, keep, got, rows):
        return run_kernel(
            pair_sum_body, name, (1,), sc, [(keep, None), (got, None)], [(shape((rows, hh), bf), None)] * 2
        )

    def spread(one):
        two = swap(one, "dp", 2)
        return [one, swap(one, "dp", 1), two, swap(two, "dp", 1)]

    feed_keep, feed_send = halves_of(
        feed_sum_body, "feed_sum", (after(w_parts[0], *last_parts), *w_got), feed_rows
    )
    feed_keep, feed_send = beyond_chip(feed_keep), beyond_chip(feed_send)
    out_recv = swap(after(out_send, *pg), "seq", 1)
    (chunks,) = run_kernel(
        functools.partial(block_out_body, nh), "block_out", (1,), sc,
        [(after(res, feed_keep), None), (out_own, None), (out_recv, None), (tg, None)] + row_specs,
        [(shape((nh, 2, width, tok), bf), None)], scratch=[pltpu.VMEM((model, tok), f32)],
    )
    feed_near, feed_next = quarter("feed_pair", feed_keep, swap(feed_send, "dp", 1), feed_rows)
    feed_far = swap(feed_next, "dp", 2)
    last_got = [after(swap(last_parts[m], "head", m), chunks, feed_near) for m in peers]
    last_keep, last_send = halves_of(last_sum_body, "last_sum", (last_parts[0], *last_got), part_rows)
    last_keep, last_send = beyond_chip(last_keep), beyond_chip(last_send)
    last_pair = swap(last_send, "dp", 1)
    feed_one = (feed_near.astype(f32) + after(feed_far, last_keep).astype(f32)).astype(bf)
    last_near, last_next = quarter("last_pair", last_keep, after(last_pair, feed_one), part_rows)
    last_one = (last_near.astype(f32) + swap(last_next, "dp", 2).astype(f32)).astype(bf)
    feed_total, last_total = spread(feed_one), spread(last_one)
    chunks = trade(after(chunks, last_keep), "head")
    block_out, tokens_grad = run_kernel(
        functools.partial(lay_out_body, nh), "lay_out", (1,), sc, [(chunks, None)],
        [(shape((width, length), bf), None)] * 2,
    )
    upweight_grad, downweight_grad = run_kernel(
        functools.partial(feed_out_body, nh, nz), "feed_result", (1,), sc, [(a, None) for a in feed_total] + [(swap(a, "seq", 1), None) for a in feed_total],
        [(shape((model, hidden), f32), None), (shape((hidden, model), f32), None)],
        scratch=[pltpu.VMEM((2, all_rows, hh), bf)],
    )
    last_total = [after(a, upweight_grad, block_out) for a in last_total]
    qkv_grad, outweight_grad, query_grad, key_grad, qkvbias_grad, upbias_grad, rows = run_kernel(
        functools.partial(last_out_body, hs, nh, nz), "last_result", (1,), sc, [(a, None) for a in last_total] + [(swap(a, "seq", 1), None) for a in last_total],
        [(shape((pc, model), f32), None), (shape((width, model), f32), None), (shape((hp, hs, hs), f32), None),
         (shape((hp, hs, hs), f32), None),
         (shape((1, pc), f32), None), (shape((1, hidden), f32), None), (shape((TILE, half), f32), None)],
        scratch=[pltpu.VMEM((2, last_rows, half), bf)],
    )
    vec = rows[4:10, 0:width]
    return (block_out.T[None], tokens_grad.T[None], vec[4], vec[5], qkv_grad.T, qkvbias_grad[0], query_grad, key_grad,
            outweight_grad, vec[2], vec[0], vec[1], upweight_grad, upbias_grad[0], downweight_grad, vec[3])


def solution(mesh):
    wide = P("dp", "seq", "head")
    return jax.shard_map(
        local,
        mesh=mesh,
        in_specs=(wide, P(), P(), P(None, "head"), P("head"), P("head", None, None), P("head", None, None),
                  P("head", None), P("head"), P(), P(), P(None, "head"), P("head"), P("head", None), P("head"),
                  P("dp", "seq"), wide),
        out_specs=(wide, wide, P("head"), P("head"), P(None, "head"), P("head"), P("head", None, None),
                   P("head", None, None), P("head", None), P("head"), P("head"), P("head"), P(None, "head"), P("head"),
                   P("head", None), P("head")),
        check_vma=False,
    )
```

```python
import functools

import jax
import jax.numpy as jnp
from jax import lax
from jax.experimental import pallas as pl
from jax.experimental.pallas import tpu as pltpu
from jax.sharding import PartitionSpec as P

eps = 1e-05
gelu_scale = 0.7978845608028654
bf = jnp.bfloat16
f32 = jnp.float32
AUG = 80
TILE = 16


def nn(a, b):
    return lax.dot_general(a, b, (((1,), (0,)), ((), ())), preferred_element_type=f32)


def nt(a, b):
    return lax.dot_general(a, b, (((1,), (1,)), ((), ())), preferred_element_type=f32)


def tn(a, b):
    return lax.dot_general(a, b, (((0,), (0,)), ((), ())), preferred_element_type=f32)


def shape(dims, dtype):
    return jax.ShapeDtypeStruct(tuple(dims), dtype)


def whole(a):
    dims = tuple(a.shape)
    return pl.BlockSpec(dims, lambda *_: (0,) * len(dims))


def lead(count, *dims):
    return pl.BlockSpec((count,) + dims, lambda p, sc: (p,) + (0,) * len(dims))


def run_kernel(body, name, grid, scalars, ins, outs, scratch=(), aliases=None):
    return pl.pallas_call(
        body,
        out_shape=[o for o, _ in outs],
        grid_spec=pltpu.PrefetchScalarGridSpec(
            num_scalar_prefetch=1,
            grid=grid,
            in_specs=[spec or whole(a) for a, spec in ins],
            out_specs=[spec or whole(o) for o, spec in outs],
            scratch_shapes=list(scratch),
        ),
        compiler_params=pltpu.CompilerParams(vmem_limit_bytes=18 * 2**20),
        cost_estimate=pl.CostEstimate(flops=0, bytes_accessed=0, transcendentals=0),
        input_output_aliases=aliases or {},
        name=name,
    )(scalars, *[a for a, _ in ins])


def norm_columns(values):
    center = values - jnp.mean(values, axis=0, keepdims=True)
    inv_std = lax.rsqrt(jnp.mean(center * center, axis=0, keepdims=True) + eps)
    return center * inv_std, inv_std


def norm_columns_back(grad, normed, inv_std, gain):
    scaled = grad * gain
    return inv_std * (
        scaled
        - jnp.mean(scaled, axis=0, keepdims=True)
        - normed * jnp.mean(scaled * normed, axis=0, keepdims=True)
    )


def column(rows, at, width):
    only = jnp.where(lax.broadcasted_iota(jnp.int32, rows.shape, 0) == at, rows.astype(f32), 0.0).astype(bf)
    upright = tn(only, jnp.ones((TILE, 128), bf))
    return jnp.concatenate([upright] * (width // 128), axis=1)


def row_sums(values):
    ones = jnp.ones((8, values.shape[1]), bf)
    if values.dtype == bf:
        return nt(ones, values)
    high = values.astype(bf)
    return nt(ones, high) + nt(ones, (values - high.astype(f32)).astype(bf))


def gelu_pair(up_pre):
    square = up_pre * up_pre
    tanh_value = jnp.tanh(gelu_scale * (up_pre + 0.044715 * square * up_pre))
    half_one = 0.5 * (1.0 + tanh_value)
    slope = half_one + 0.5 * up_pre * (1.0 - tanh_value * tanh_value) * gelu_scale * (
        1.0 + 3.0 * 0.044715 * square
    )
    return up_pre * half_one, slope


def soft_columns(logits):
    top = jnp.exp(logits - jnp.max(logits, axis=0, keepdims=True))
    return top / jnp.sum(top, axis=0, keepdims=True)


def ahead_mask(starts, rows, first_column, columns):
    j = lax.broadcasted_iota(jnp.int32, (rows, columns), 0)
    i = lax.broadcasted_iota(jnp.int32, (rows, columns), 1) + first_column
    return (j <= i) & (j >= starts[0:1, first_column : first_column + columns])


def causal_pieces(tokens):
    step = tokens // 2
    return ((0, step, step), (step, step, tokens))


HBM = pl.BlockSpec(memory_space=pl.ANY)
IN_VMEM = pl.BlockSpec(memory_space=pltpu.VMEM)


def load_all(refs, places, sems):
    copies = [pltpu.make_async_copy(ref, place, sems.at[k]) for k, (ref, place) in enumerate(zip(refs, places))]
    for copy in copies:
        copy.start()
    return copies


def part_places(refs, scratch, core):
    return [scratch.at[2 * (k // 2) + (core if k % 2 == 0 else 1 - core)] for k in range(len(refs))]


def tables_body(nh, ids, pos_ref, row_ref, starts_ref, table_ref):
    length = pos_ref.shape[1]
    tok = length // nh
    h = ids[1]
    own = row_ref[:, pl.ds(pl.multiple_of(h * tok, 128), tok)]
    lane = lax.broadcasted_iota(jnp.int32, (8, tok), 1)
    starts_ref[...] = lane - own

    def start_of(t):
        return t - pos_ref[0, t]

    def flag(value):
        return jnp.where(value, 1, 0)

    run_last = start_of(length - 1)
    other = [h ^ m for m in range(nh)]
    values = [ids[0], start_of((h + 1) * tok - 1) - h * tok]
    values += [flag((q < h) & (start_of(h * tok) <= (q + 1) * tok - 1)) for q in other[1:]]
    values += [flag(start_of(h * tok) < 0)]
    values += [flag((q > h) & (start_of(q * tok) <= (h + 1) * tok - 1)) for q in other[1:]]
    values += [flag(run_last <= (h + 1) * tok - 1), h, ids[2]]
    values += [flag(run_last <= (q + 1) * tok - 1) for q in other]
    values += [flag(start_of(q * tok) < 0) for q in other]
    lane = lax.broadcasted_iota(jnp.int32, (8, 128), 1)
    table = jnp.zeros((8, 128), jnp.int32)
    for k, value in enumerate(values):
        table = jnp.where(lane == k, value, table)
    table_ref[...] = table


def state_sum_body(hp, nh, first, sc, *refs):
    for i in range(refs[nh].shape[0]):
        total = jnp.zeros(refs[0].shape[1:], f32)
        for m in range(nh):
            total += jnp.where(sc[first + m] > 0, refs[m][((i // hp) ^ m) * hp + i % hp].astype(f32), 0.0)
        refs[nh][i] = total.astype(bf)


def pack_body(sc, qkv_ref, qm_ref, km_ref, qb_ref, ub_ref, ob_ref, db_ref, out_ref, up_ref, down_ref,
              first_ref, other_ref, wa_ref, wb_ref, rows_ref):
    pc, model = qkv_ref.shape
    hs = qm_ref.shape[1]
    width = ob_ref.shape[1]
    rows_ref[...] = jnp.zeros_like(rows_ref)
    rows_ref[0:1, 0:pc] = qb_ref[...].astype(f32)
    rows_ref[1:2, 0 : ub_ref.shape[1]] = ub_ref[...].astype(f32)
    rows_ref[2:3, 0:width] = ob_ref[...].astype(f32)
    rows_ref[3:4, 0:width] = db_ref[...].astype(f32)
    for core, ref in ((sc[0], first_ref), (1 - sc[0], other_ref)):
        cut = pc // 2
        ref[0:cut, :] = qkv_ref[pl.ds(pl.multiple_of(core * cut, TILE), cut), :]
        ref[cut : cut + hs // 2, :] = jnp.zeros((hs // 2, model), bf)
        for i in range(qm_ref.shape[0] // hs):
            for k in range(2):
                rows = slice(i * hs + k * hs // 2, i * hs + (k + 1) * hs // 2)
                at = k * (model // 2) + 128 * i
                own = jnp.where(core == 0, qm_ref[rows, :].astype(f32), km_ref[rows, :].astype(f32))
                ref[cut : cut + hs // 2, at : at + hs] = own.astype(bf)
        cut += hs // 2
        ref[cut : cut + TILE, :] = rows_ref[...].astype(bf)
        half = out_ref.shape[0] // 2
        ref[cut + TILE :, :] = out_ref[pl.ds(pl.multiple_of(core * half, TILE), half), :]
    half = down_ref.shape[0] // 2
    at = pl.ds(pl.multiple_of(sc[0] * half, TILE), half)
    lanes = pl.ds(pl.multiple_of(sc[0] * half, 128), half)
    for k, w_ref in enumerate((wa_ref, wb_ref)):
        part = slice(k * half, (k + 1) * half)
        w_ref[:, 0:half] = up_ref[part, lanes]
        w_ref[:, half:] = down_ref[at, part]


def chunks_body(nh, sc, a_ref, b_ref, o_ref):
    tokens = o_ref.shape[3]
    for q in range(nh):
        for k, ref in enumerate((a_ref, b_ref)):
            o_ref[q, k] = ref[:, q * tokens : (q + 1) * tokens]


def first_norm_body(sc, x_ref, gain_ref, hid_ref):
    normed, _ = norm_columns(x_ref[...].astype(f32))
    width = x_ref.shape[1]
    gains = gain_ref[...]
    hid_ref[...] = (normed * column(gains, 0, width) + column(gains, 1, width)).astype(bf)


def turn_body(sc, a_ref, b_ref, o_ref):
    tokens = a_ref.shape[1]
    o_ref[0:tokens, :] = a_ref[...].T
    o_ref[tokens:, :] = b_ref[...].T


def map_of(first_ref, at, i, hs, cut):
    model = first_ref.shape[2]
    rows = slice(cut, cut + hs // 2)
    return jnp.concatenate(
        [first_ref[at, rows, k * (model // 2) + 128 * i : k * (model // 2) + 128 * i + hs] for k in range(2)], axis=0
    )


def project_body(hp, hs, count, sc, hid_ref, starts_ref, *refs):
    first_refs = refs[0 : 2 * count]
    proj_ref, qf_ref, kf_ref, va_ref, st_ref, w_ref, sems = refs[-7:]
    p = pl.program_id(0)
    wait_for_piece(first_refs, w_ref, sems, sc)
    pc, tokens = proj_ref.shape[1:]
    cut = pc // 2
    bias = column(w_ref[2 * p, cut + hs // 2 : cut + hs // 2 + TILE, 0:pc], 0, tokens)
    for k in range(2):
        rows = slice(k * cut, (k + 1) * cut)
        proj_ref[0, rows, :] = (nn(w_ref[2 * p + k, 0:cut, :], hid_ref[...]) + bias[rows, :]).astype(bf)
    included = (starts_ref[0:1, :] == sc[1]).astype(f32)
    extra = lax.broadcasted_iota(jnp.int32, (AUG - hs, tokens), 0)
    extra = jnp.where(extra < 2, 1.0, 0.0).astype(bf)
    for i in range(hp):
        row = 3 * hs * i
        for part, out in ((0, qf_ref), (1, kf_ref)):
            own_map = map_of(w_ref, 2 * p + part, i, hs, cut)
            logits = tn(own_map, proj_ref[0, row + part * hs : row + (part + 1) * hs, :])
            out[i, 0:hs, :] = soft_columns(logits).astype(bf)
            out[i, hs : 2 * hs, :] = soft_columns(-logits).astype(bf)
        va_ref[i, 0:hs, :] = proj_ref[0, row + 2 * hs : row + 3 * hs, :]
        va_ref[i, hs:AUG, :] = extra
        kept = (va_ref[i].astype(f32) * included).astype(bf)
        st_ref[i] = nt(kept, kf_ref[i]).astype(bf)


def wait_for_piece(first_refs, w_ref, sems, sc):
    p = pl.program_id(0)
    places = part_places(first_refs, w_ref, sc[0])
    rows = w_ref.shape[1]
    copies = [
        pltpu.make_async_copy(ref.at[pl.ds(0, rows), :], place, sems.at[k])
        for k, (ref, place) in enumerate(zip(first_refs, places))
    ]

    @pl.when(p == 0)
    def _():
        for copy in copies:
            copy.start()

    for k, copy in enumerate(copies):

        @pl.when(p == k // 2)
        def _(copy=copy):
            copy.wait()


def local_mix_body(hp, sc, qf_ref, kf_ref, va_ref, starts_ref, num_ref):
    tokens = qf_ref.shape[2]
    starts = starts_ref[...]
    for first, width, rows in causal_pieces(tokens):
        mask = ahead_mask(starts, rows, first, width)
        for i in range(hp):
            scores = tn(kf_ref[i, :, 0:rows], qf_ref[i, :, first : first + width])
            scores = jnp.where(mask, scores, 0.0).astype(bf)
            num_ref[i, :, first : first + width] = nn(va_ref[i, :, 0:rows], scores)


def weighted_state(sc, slot, refs, i, hp):
    total = jnp.where(sc[slot + len(refs) - 1] > 0, refs[-1][i].astype(f32), 0.0)
    for m, ref in enumerate(refs[:-1], 1):
        total += jnp.where(sc[slot + m - 1] > 0, ref[((i // hp) ^ m) * hp + i % hp].astype(f32), 0.0)
    return total


def load_out_weight(sc, first_refs, w_ref, sems):
    rows = w_ref.shape[0] // len(first_refs)
    at = first_refs[0].shape[0] - rows
    places = [
        w_ref.at[pl.ds(pl.multiple_of(rows * (2 * (k // 2) + (sc[0] if k % 2 == 0 else 1 - sc[0])), TILE), rows), :]
        for k in range(len(first_refs))
    ]
    return load_all([ref.at[pl.ds(at, rows), :] for ref in first_refs], places, sems)


def mix_out_body(hp, hs, nh, sc, num_ref, qf_ref, starts_ref, x_ref, gain_ref, *refs):
    state_refs, row_refs, wo_refs = refs[0:nh], refs[nh : 2 * nh], refs[2 * nh : 4 * nh]
    sin_ref, mixd_ref, mix_ref, res_ref, top_ref, low_ref, w_ref, sems = refs[4 * nh :]
    copies = load_out_weight(sc, wo_refs, w_ref, sems)
    uses = starts_ref[0:1, :] < 0
    model, tokens = x_ref.shape
    for i in range(num_ref.shape[0]):
        state = weighted_state(sc, 2, state_refs, i, hp).astype(bf)
        sin_ref[i] = state
        num = num_ref[i] + jnp.where(uses, nn(state, qf_ref[i]), 0.0)
        mixture = num[0:hs, :] / num[hs : hs + 1, :]
        mixd_ref[i, 0:hs, :] = mixture
        mixd_ref[i, hs : hs + 8, :] = num[hs : hs + 8, :]
        mix_ref[i * hs : (i + 1) * hs, :] = mixture.astype(bf)
    for copy in copies:
        copy.wait()
    res_ref[...] = x_ref[...].astype(f32) + tn(w_ref[...], mix_ref[...])
    width = model // nh
    h = sc[2 + 2 * nh]
    for j in range(nh):
        rows = pl.ds(pl.multiple_of((h ^ j) * width, TILE), width)
        res_ref[rows, :] += column(row_refs[j][:, 0:width], 2, tokens)
    normed, _ = norm_columns(res_ref[...].astype(bf).astype(f32))
    gains = gain_ref[...]
    hidden = (normed * column(gains, 2, tokens) + column(gains, 3, tokens)).astype(bf)
    half = top_ref.shape[0]
    top_ref[...] = hidden[0:half, :]
    low_ref[...] = hidden[half:, :]


def feed_body(count, first, last, sc, *refs):
    hidt_ins, gyt_ins, gy_in = refs[0:4], refs[4:6], refs[6]
    row_refs = refs[7 : 7 + count]
    w_ins = refs[7 + count : 7 + 3 * count]
    refs = refs[7 + 3 * count :]
    if first:
        out_ref, sg_ref = refs[0:2]
        refs = refs[2:]
    elif not last:
        out_in, sg_in, out_ref, sg_ref = refs[0:4]
        refs = refs[4:]
    else:
        out_in, sg_in, out_own, out_peer, sg_own, sg_peer = refs[0:6]
        refs = refs[6:]
    w_refs, ub_ref, refs = refs[0:count], refs[count], refs[count + 1 :]
    hid_ref, act_ref, ug_ref = refs
    mid, tokens = hidt_ins[0].shape
    model = 2 * mid
    half = act_ref.shape[1]
    runs = [slice(0, tokens), slice(tokens, 2 * tokens)]
    lo, hi = slice(0, half), slice(half, 2 * half)
    at_half = pl.ds(pl.multiple_of(sc[0] * half, 128), half)
    for k in range(count):
        bias = row_refs[k][:, at_half].astype(f32)[1:2, :]
        first_w, second_w = w_ins[2 * k], w_ins[2 * k + 1]
        for which, rows in enumerate(runs):
            if k == 0:
                for m in range(2):
                    hid_ref[rows, m * mid : (m + 1) * mid] = hidt_ins[2 * which + m][...].T
            up_pre = nn(hid_ref[rows, lo], first_w[:, lo]) + nn(hid_ref[rows, hi], second_w[:, lo]) + bias
            value, slope = gelu_pair(up_pre)
            act_ref[rows, :] = value.astype(bf)
            back = nt(gy_in[rows, lo], first_w[:, hi]) + nt(gy_in[rows, hi], second_w[:, hi])
            ug_ref[rows, :] = (back * slope).astype(bf)
        ub_ref[k] = nn(jnp.ones((8, 2 * tokens), bf), ug_ref[...])
        for m in range(2):
            grads = [nn(hidt_ins[2 * r + m][...], ug_ref[runs[r], :]) for r in range(2)]
            w_refs[k][m * mid : (m + 1) * mid, :] = (grads[0] + grads[1]).astype(bf)
        grads = [nn(gyt_ins[r][...], act_ref[runs[r], :]) for r in range(2)]
        w_refs[k][model : 2 * model, :] = (grads[0] + grads[1]).astype(bf)
        w_refs[k][2 * model :, :] = jnp.zeros((TILE, half), bf)
        for at, w in ((lo, first_w), (hi, second_w)):
            if first and k == 0:
                out_ref[:, at] = nn(act_ref[...], w[:, hi])
                sg_ref[at, :] = nt(w[:, lo], ug_ref[...])
            elif not last and k == 0:
                out_ref[:, at] = out_in[:, at] + nn(act_ref[...], w[:, hi])
                sg_ref[at, :] = sg_in[at, :] + nt(w[:, lo], ug_ref[...])
            elif not last:
                out_ref[:, at] += nn(act_ref[...], w[:, hi])
                sg_ref[at, :] += nt(w[:, lo], ug_ref[...])
            else:
                out = out_in[:, at] + nn(act_ref[...], w[:, hi])
                out_own[:, at] = out[runs[0], :]
                out_peer[:, at] = out[runs[1], :].astype(bf)
                sg = sg_in[at, :] + nt(w[:, lo], ug_ref[...])
                sg_own[at, :] = sg[:, runs[0]]
                sg_peer[at, :] = sg[:, runs[1]].astype(bf)


def block_out_body(nh, sc, res_ref, out_ref, out2_ref, tg_ref, *refs):
    row_refs, o_ref, total_ref = refs[0:nh], refs[nh], refs[nh + 1]
    model, tokens = res_ref.shape
    width = model // nh
    total_ref[...] = res_ref[...] + (out_ref[...] + out2_ref[...].astype(f32)).T
    h = sc[2 + 2 * nh]
    for j in range(nh):
        rows = pl.ds(pl.multiple_of((h ^ j) * width, TILE), width)
        o_ref[j, 1] = tg_ref[j]
        o_ref[h ^ j, 0] = (total_ref[rows, :] + column(row_refs[j][:, 0:width], 3, tokens)).astype(bf)


def lay_out_body(nh, sc, in_ref, *o_refs):
    tokens = in_ref.shape[3]
    for k in range(2):
        for q in range(nh):
            o_refs[k][:, q * tokens : (q + 1) * tokens] = in_ref[q, k]


def second_back_body(hs, nh, sc, sg_ref, sg2_ref, res_ref, gyt_ref, gain_ref, mixd_ref, starts_ref, qf_ref, *refs):
    wo_refs, (rg_ref, ag_ref, vec_ref, na_ref, sgt_ref, w_ref, sems) = refs[0 : 2 * nh], refs[2 * nh :]
    copies = load_out_weight(sc, wo_refs, w_ref, sems)
    model, tokens = sg_ref.shape
    width = model // nh
    normed, inv_std = norm_columns(res_ref[...].astype(bf).astype(f32))
    sg = sg_ref[...] + sg2_ref[...].astype(f32)
    res_grad = gyt_ref[...].astype(f32) + norm_columns_back(sg, normed, inv_std, column(gain_ref[...], 2, tokens))
    rg_ref[...] = res_grad
    ag_ref[...] = res_grad.astype(bf)
    uses = (starts_ref[0:1, :] < 0).astype(f32)
    for copy in copies:
        copy.wait()
    mg = nn(w_ref[...], ag_ref[...])
    row = lax.broadcasted_iota(jnp.int32, (AUG - hs, tokens), 0)
    for i in range(qf_ref.shape[0]):
        num = mg[i * hs : (i + 1) * hs, :] / mixd_ref[i, hs : hs + 1, :]
        den = -jnp.sum(num * mixd_ref[i, 0:hs, :], axis=0, keepdims=True)
        high = den.astype(bf).astype(f32)
        extra = jnp.where(row == 0, high, jnp.where(row == 1, den - high, 0.0))
        na_ref[i, 0:hs, :] = num.astype(bf)
        na_ref[i, hs:AUG, :] = extra.astype(bf)
        kept = (na_ref[i].astype(f32) * uses).astype(bf)
        sgt_ref[i] = nt(kept, qf_ref[i]).astype(bf)
    for at, value in enumerate((sg * normed, sg, ag_ref[...], gyt_ref[...])):
        sums = row_sums(value)
        for p in range(nh):
            vec_ref[p, at : at + 1, :] = sums[0:1, p * width : (p + 1) * width]


def halves_back(feat, grad, hs):
    parts = []
    for k in range(2):
        soft = feat[k * hs : (k + 1) * hs, :].astype(f32)
        own = grad[k * hs : (k + 1) * hs, :]
        weight = jnp.sum(soft * own, axis=0, keepdims=True) / jnp.sum(soft, axis=0, keepdims=True)
        parts.append(soft * (own - weight))
    return (parts[0] - parts[1]).astype(bf)


def local_back_body(hp, hs, sc, qf_ref, kf_ref, va_ref, na_ref, sin_ref, starts_ref, ql_ref, kfg_ref, vg_ref):
    tokens = qf_ref.shape[2]
    starts = starts_ref[...]
    step = tokens // 2
    uses = starts[0:1, :] < 0
    masks = [ahead_mask(starts, rows, first, width) for first, width, rows in causal_pieces(tokens)]
    for i in range(hp):
        na = na_ref[i]
        through = tn(sin_ref[i], na)
        for which, (first, width, rows) in enumerate(causal_pieces(tokens)):
            at = slice(first, first + width)
            mask = masks[which]
            scores = jnp.where(mask, tn(kf_ref[i, :, 0:rows], qf_ref[i, :, at]), 0.0).astype(bf)
            sgrad = jnp.where(mask, tn(va_ref[i, :, 0:rows], na[:, at]), 0.0).astype(bf)
            qfg = nn(kf_ref[i, :, 0:rows], sgrad) + jnp.where(uses[:, at], through[:, at], 0.0)
            ql_ref[i, :, at] = halves_back(qf_ref[i, :, at], qfg, hs)
            kfg = nt(qf_ref[i, :, at], sgrad)
            vg = nt(na[:, at], scores)[0:hs, :]
            if which == 0:
                kfg_ref[i, :, 0:rows] = kfg
                vg_ref[i, :, 0:rows] = vg
            else:
                kfg_ref[i, :, 0:step] += kfg[:, 0:step]
                vg_ref[i, :, 0:step] += vg[:, 0:step]
                kfg_ref[i, :, step:] = kfg[:, step:]
                vg_ref[i, :, step:] = vg[:, step:]


def join_extra(state, hs):
    row = lax.broadcasted_iota(jnp.int32, state.shape, 0)
    both = state[hs : hs + 1, :] + state[hs + 1 : hs + 2, :]
    return jnp.where(row < hs, state, jnp.where(row == hs, both, 0.0))


def project_back_body(hp, hs, nh, sc, *refs):
    state_refs, first_refs, refs = refs[0:nh], refs[nh : 3 * nh], refs[3 * nh :]
    kf_ref, va_ref, ql_ref, kfg_ref, vg_ref, proj_ref, starts_ref, *pg_refs, fg_ref, mg_ref, pb_ref, pg_ref, first_ref, sems = refs
    p = pl.program_id(0)
    wait_for_piece(first_refs, first_ref, sems, sc)
    included = starts_ref[0:1, :] == sc[1]
    cut = pg_ref.shape[1] // 2
    for i in range(hp):
        total = jnp.where(sc[1 + 2 * nh] > 0, state_refs[-1][i].astype(f32), 0.0)
        for m in range(1, nh):
            total += jnp.where(sc[1 + nh + m] > 0, state_refs[m - 1][i].astype(f32), 0.0)
        state = join_extra(total, hs).astype(bf)
        kfg = kfg_ref[i] + jnp.where(included, tn(state, va_ref[i]), 0.0)
        vg = vg_ref[i] + jnp.where(included, nn(state, kf_ref[i])[0:hs, :], 0.0)
        klg = halves_back(kf_ref[i], kfg, hs)
        qlg = ql_ref[i]
        row = 3 * hs * i
        pg_ref[0, row : row + hs, :] = nn(map_of(first_ref, 2 * p, i, hs, cut), qlg).astype(bf)
        pg_ref[0, row + hs : row + 2 * hs, :] = nn(map_of(first_ref, 2 * p + 1, i, hs, cut), klg).astype(bf)
        pg_ref[0, row + 2 * hs : row + 3 * hs, :] = vg.astype(bf)
        q_grad = nt(proj_ref[0, row : row + hs, :], qlg)
        k_grad = nt(proj_ref[0, row + hs : row + 2 * hs, :], klg)
        mg_ref[0, :, 128 * i : 128 * (i + 1)] = jnp.concatenate([q_grad, k_grad], axis=1)
    for j, ref in enumerate(pg_refs):

        @pl.when(p == j)
        def _(ref=ref):
            ref[...] = pg_ref[0]

    pb_ref[0] = row_sums(pg_ref[0])
    grad = tn(first_ref[2 * p, 0:cut, :], pg_ref[0, 0:cut, :]) + tn(first_ref[2 * p + 1, 0:cut, :], pg_ref[0, cut:, :])

    @pl.when(pl.program_id(0) == 0)
    def _():
        fg_ref[...] = grad

    @pl.when(pl.program_id(0) > 0)
    def _():
        fg_ref[...] += grad


def first_back_body(nh, sc, fg_ref, x_ref, rg_ref, gain_ref, tg_ref, vec_ref):
    model, tokens = fg_ref.shape
    width = model // nh
    normed, inv_std = norm_columns(x_ref[...].astype(f32))
    fg = fg_ref[...]
    gain = column(gain_ref[...], 0, tokens)
    tg = (rg_ref[...] + norm_columns_back(fg, normed, inv_std, gain)).astype(bf)
    for p in range(nh):
        tg_ref[p] = tg[p * width : (p + 1) * width, :]
    for at, value in enumerate((fg * normed, fg)):
        sums = row_sums(value)
        for p in range(nh):
            vec_ref[p, at : at + 1, :] = sums[0:1, p * width : (p + 1) * width]


def split_quarters(nh, nz, sc, total_ref, keep_ref, send_ref):
    part = total_ref.shape[0] // nz
    for k in range(nz):
        o_ref = keep_ref if k % 2 == 0 else send_ref
        at = pl.ds(pl.multiple_of((sc[3 + 2 * nh] ^ k) * part, TILE), part)
        o_ref[(k // 2) * part : (k // 2 + 1) * part, :] = total_ref[at, :]


def feed_sum_body(nh, nz, sc, *refs):
    keep_ref, send_ref, total_ref = refs[nh:]
    rows = total_ref.shape[0]
    total_ref[...] = sum(ref[0:rows, :].astype(f32) for ref in refs[0:nh]).astype(bf)
    split_quarters(nh, nz, sc, total_ref, keep_ref, send_ref)


def last_sum_body(nh, nz, sc, *refs):
    keep_ref, send_ref, total_ref = refs[nh:]
    total_ref[...] = sum(ref[...].astype(f32) for ref in refs[0:nh]).astype(bf)
    split_quarters(nh, nz, sc, total_ref, keep_ref, send_ref)


def pair_sum_body(sc, own_ref, got_ref, keep_ref, send_ref):
    part = keep_ref.shape[0]
    keep_ref[...] = (own_ref[0:part, :].astype(f32) + got_ref[0:part, :].astype(f32)).astype(bf)
    send_ref[...] = (own_ref[part:, :].astype(f32) + got_ref[part:, :].astype(f32)).astype(bf)


def last_grads_body(nh, sc, *refs):
    pg_refs, pg2_refs, refs = refs[0:nh], refs[nh : 2 * nh], refs[2 * nh :]
    hid_ref, hid2_ref, mg_ref, pb_ref, own_ref, early_ref, late_ref, vec1_ref, vec2_ref = refs[0:9]
    mix_ref, mix2_ref, ag_ref, ag2_ref, *o_refs, rows_ref = refs[9:]
    pc, half = pg_refs[0].shape[0], hid_ref.shape[0]
    hs = mg_ref.shape[1]
    width = vec1_ref.shape[2]
    h = sc[2 + 2 * nh]
    for j in range(nh):
        o_ref = o_refs[j]
        o_ref[0:pc, :] = (nt(pg_refs[j][...], hid_ref[...]) + nt(pg2_refs[j][...], hid2_ref[...])).astype(bf)
        o_ref[pc : pc + hs, :] = mg_ref[j].astype(bf)
        ub_ref, k = (own_ref, 0) if j == 0 else (early_ref, j - 1) if j < nh - 1 else (late_ref, 0)
        rows_ref[...] = jnp.zeros_like(rows_ref)
        rows_ref[0:1, :] = pb_ref[j, 0:1, 0:half]
        rows_ref[1:2, 0 : pc - half] = pb_ref[j, 0:1, half:]
        rows_ref[2:3, :] = jnp.where(sc[0] == 0, ub_ref[k, 0:1, :], 0.0)
        rows_ref[3:4, :] = jnp.where(sc[0] == 0, 0.0, ub_ref[k, 0:1, :])
        rows_ref[4:8, 0:width] = vec2_ref[h ^ j, 0:4, :]
        rows_ref[8:10, 0:width] = vec1_ref[h ^ j, 0:2, :]
        at = pc + hs + TILE
        o_ref[pc + hs : at, :] = rows_ref[...].astype(bf)
        rows = slice(j * width, (j + 1) * width)
        o_ref[at : at + width, :] = (nt(mix_ref[rows, :], ag_ref[...]) + nt(mix2_ref[rows, :], ag2_ref[...])).astype(bf)
        o_ref[at + width :, :] = jnp.zeros((o_ref.shape[0] - at - width, half), bf)


def join_quarters(nh, nz, sc, refs, total_ref):
    part = refs[0].shape[0]
    for k in range(2 * nz):
        at = pl.ds(pl.multiple_of((sc[3 + 2 * nh] ^ (k % nz)) * part, TILE), part)
        total_ref[k // nz, at, :] = refs[k][...]


def feed_out_body(nh, nz, sc, *refs):
    up_ref, down_ref, total_ref = refs[2 * nz :]
    join_quarters(nh, nz, sc, refs, total_ref)
    model = down_ref.shape[1]
    half = total_ref.shape[2]
    for k, core in enumerate((sc[0], 1 - sc[0])):
        at = pl.ds(pl.multiple_of(core * half, 128), half)
        up_ref[:, at] = total_ref[k, 0:model, :].astype(f32)
        down_ref[at, :] = total_ref[k, model : 2 * model, :].astype(f32).T


def last_out_body(hs, nh, nz, sc, *refs):
    qkv_ref, out_ref, qm_ref, km_ref, qb_ref, ub_ref, vec_ref, total_ref = refs[2 * nz :]
    join_quarters(nh, nz, sc, refs, total_ref)
    pc = qkv_ref.shape[0]
    half = total_ref.shape[2]
    for k, core in enumerate((sc[0], 1 - sc[0])):
        at = pl.ds(pl.multiple_of(core * half, 128), half)
        qkv_ref[:, at] = total_ref[k, 0:pc, :].astype(f32)
        first = pc + hs + TILE
        out_ref[:, at] = total_ref[k, first : first + out_ref.shape[0], :].astype(f32)
    maps = total_ref[0, pc : pc + hs, :].astype(f32) + total_ref[1, pc : pc + hs, :].astype(f32)
    for i in range(qm_ref.shape[0]):
        qm_ref[i] = maps[:, 128 * i : 128 * i + hs]
        km_ref[i] = maps[:, 128 * i + hs : 128 * i + 2 * hs]
    rows = slice(pc + hs, pc + hs + TILE)
    rows = total_ref[0, rows, :].astype(f32) + total_ref[1, rows, :].astype(f32)
    qb_ref[:, 0:half] = rows[0:1, :]
    qb_ref[:, half:] = rows[1:2, 0 : pc - half]
    ub_ref[:, 0:half] = rows[2:3, :]
    ub_ref[:, half:] = rows[3:4, :]
    vec_ref[...] = rows


def swap(a, axis, k):
    n = lax.axis_size(axis)
    return lax.ppermute(a, axis, [(i, i ^ k) for i in range(n)])


def trade(a, axis):
    return lax.all_to_all(a, axis, 0, 0, tiled=True)


def after(a, *others):
    return lax.optimization_barrier((a,) + others)[0]


def chain_seq(part, forward, weight_of):
    n = lax.axis_size("seq")
    total = None
    for k in range(1, n):
        pairs = [(i, i + k) if forward else (i + k, i) for i in range(n - k)]
        if n == 2:
            return lax.ppermute(part, "seq", pairs)
        sent = part if forward else part * weight_of(k).astype(part.dtype)
        got = lax.ppermute(sent, "seq", pairs).astype(f32) * (weight_of(k) if forward else 1.0)
        total = got if total is None else total + got
    return total.astype(bf)


def local(tokens, attn_gain, attn_shift, qkv_weight, qkv_bias, query_map, key_map, out_weight, out_bias,
          mlp_gain, mlp_shift, up_weight, up_bias, down_weight, down_bias, positions, out_grad):
    nh, ns, nz = lax.axis_size("head"), lax.axis_size("seq"), lax.axis_size("dp")
    length, width = tokens.shape[1], tokens.shape[2]
    model = width * nh
    half = model // 2
    hp, hs = query_map.shape[0], query_map.shape[1]
    heads = hp * nh
    pc = qkv_weight.shape[1]
    hidden = up_weight.shape[1]
    hh = hidden // 2
    tok = length // nh
    h = lax.axis_index("head")
    s2 = lax.axis_index("seq") % 2
    peers = range(1, nh)

    ids = jnp.stack([s2, h, lax.axis_index("dp")]).astype(jnp.int32)
    starts, table = pl.pallas_call(
        functools.partial(tables_body, nh),
        out_shape=[shape((8, tok), jnp.int32), shape((8, 128), jnp.int32)],
        in_specs=[pl.BlockSpec(memory_space=pltpu.SMEM), pl.BlockSpec(memory_space=pltpu.SMEM),
                  pl.BlockSpec(memory_space=pltpu.VMEM)],
        name="tables",
    )(ids, positions, positions)
    sc = table[0, 0 : 4 + 4 * nh]
    run_start = -positions[0, 0]

    def beyond_chip(total):
        base = total
        for k in range(1, ns // 2):
            total += lax.ppermute(base, "seq", [(i, (i + 2 * k) % ns) for i in range(ns)])
        return total

    (both,) = run_kernel(
        functools.partial(chunks_body, nh), "chunks", (1,), ids, [(tokens[0].T, None), (out_grad[0].T, None)],
        [(shape((nh, 2, width, tok), bf), None)],
    )
    both = trade(both, "head")

    core_of = jnp.full((1,), s2, jnp.int32)
    gains = jnp.pad(jnp.stack([attn_gain, attn_shift, mlp_gain, mlp_shift]), ((0, TILE - 4), (0, 0)))
    fl = pc // 2 + hs // 2 + TILE
    fr = fl + width // 2
    own, other_half, wa_own, wb_own = run_kernel(
        pack_body, "pack_weights", (1,), core_of,
        [(a, None) for a in (qkv_weight.T, query_map.reshape(-1, hs), key_map.reshape(-1, hs), qkv_bias[None], up_bias[None],
                             out_bias[None], down_bias[None], out_weight, up_weight, down_weight)],
        [(shape((fr, model), bf), None), (shape((fr, model), bf), None), (shape((hh, 2 * hh), bf), None), (shape((hh, 2 * hh), bf), None)],
        scratch=[pltpu.VMEM((TILE, model), f32)],
    )
    x, gyt = [both[:, k].reshape(model, tok) for k in range(2)]
    own = after(own, sc)
    first_got = [swap(own, "head", 1), swap(own, "head", 2)]
    mid = fr // 2 // TILE * TILE
    far_parts = [swap(first_got[0][0:mid], "head", 2), swap(first_got[1][mid:], "head", 1)]
    x, gyt = after(x, *first_got), after(gyt, *first_got)
    gyt_peer = swap(gyt, "seq", 1)
    (hid,) = run_kernel(
        first_norm_body, "first_norm", (1,), core_of, [(x, None), (gains, None)], [(shape((model, tok), bf), None)]
    )
    hid_peer = swap(lax.dynamic_slice_in_dim(hid, (1 - s2) * half, half, 0), "seq", 1)
    (gy,) = run_kernel(
        turn_body, "turn_grad", (1,), core_of, [(gyt, None), (gyt_peer, None)], [(shape((2 * tok, model), bf), None)]
    )
    firsts_of = [[own, other_half]] + [[a, swap(after(a, hid), "seq", 1)] for a in first_got]
    in_hbm = lambda arrays: [(a, HBM) for a in arrays]
    first_scratch = [pltpu.VMEM((2 * nh, fl, model), bf), pltpu.SemaphoreType.DMA((2 * nh,))]
    wo_scratch = [pltpu.VMEM((model, model), bf), pltpu.SemaphoreType.DMA((2 * nh,))]

    va_spec, state_spec, feat_spec = lead(hp, AUG, tok), lead(hp, AUG, 2 * hs), lead(hp, 2 * hs, tok)
    hid_now = after(hid, gyt_peer, hid_peer)

    def project(first_piece, count, so_far):
        def at(spec):
            return pl.BlockSpec(spec.block_shape, lambda p, sc: (p + first_piece,) + (0,) * (len(spec.block_shape) - 1))

        outs = [(shape((nh, pc, tok), bf), at(lead(1, pc, tok))), (shape((heads, 2 * hs, tok), bf), at(feat_spec)),
                (shape((heads, 2 * hs, tok), bf), at(feat_spec)), (shape((heads, AUG, tok), bf), at(va_spec)),
                (shape((heads, AUG, 2 * hs), bf), at(state_spec))]
        arrays = [a for pair in firsts_of[first_piece : first_piece + count] for a in pair]
        return run_kernel(
            functools.partial(project_body, hp, hs, count), f"project_{first_piece}", (count,), sc,
            [(hid_now, None), (starts, None)] + in_hbm(arrays) + in_hbm(so_far), outs,
            scratch=[pltpu.VMEM((2 * count, fl, model), bf), pltpu.SemaphoreType.DMA((2 * count,))],
            aliases={3 + 2 * count + k: k for k in range(len(so_far))},
        )

    so_far = project(0, nh - 1, ())
    far = jnp.concatenate([after(a, so_far[-1]) for a in far_parts])
    firsts_of.append([far, after(swap(far, "seq", 1), so_far[-1])])
    all_first = [a for pair in firsts_of for a in pair]
    row_specs = [(pair[0], pl.BlockSpec((TILE, model), lambda *_: (fl // TILE - 1, 0))) for pair in firsts_of]
    proj, qf, kf, va, states = project(nh - 1, 1, so_far)
    wa_own = after(wa_own, *far_parts)
    wa_x, wa_y = swap(wa_own, "head", 1), swap(wa_own, "head", 2)
    (num,) = run_kernel(
        functools.partial(local_mix_body, hp), "local_mix", (nh,), sc,
        [(qf, feat_spec), (kf, feat_spec), (after(va, gy, wa_x, wa_y), va_spec), (starts, None)],
        [(shape((heads, AUG, tok), f32), va_spec)],
    )
    around = [after(swap(states, "head", m), num) for m in peers]

    def states_together(first, arrays):
        (total,) = run_kernel(
            functools.partial(state_sum_body, hp, nh, first), f"state_sum_{first}", (1,), sc, [(a, None) for a in arrays],
            [(shape((heads, AUG, 2 * hs), bf), None)],
        )
        return total

    whole_run = states_together(4 + 2 * nh, [states] + around)
    before = chain_seq(whole_run, True, lambda k: (run_start <= -(k - 1) * length - 1).astype(f32))

    wb_own = after(wb_own, before)
    wb_x, wb_y = swap(wb_own, "head", 1), swap(wb_own, "head", 2)

    sin, mixd, mix, res, *hidt2 = run_kernel(
        functools.partial(mix_out_body, hp, hs, nh), "mix_out", (1,), sc,
        [(a, None) for a in (num, qf, starts, x, gains, *around, before)] + row_specs + in_hbm(all_first),
        [(shape((heads, AUG, 2 * hs), bf), None), (shape((heads, hs + 8, tok), f32), None), (shape((model, tok), bf), None),
         (shape((model, tok), f32), None), (shape((half, tok), bf), None), (shape((half, tok), bf), None)],
        scratch=wo_scratch,
    )
    hidt2_peer = [swap(a, "seq", 1) for a in hidt2]
    wa_far = swap(after(wa_x, mix), "head", 2)
    w_all = [[wa_own, wb_own], [wa_x, wb_x], [wa_y, wb_y]]

    all_rows = 2 * model

    def feed(which, sums, last=False):
        count = len(which)
        if last:
            outs = [shape((tok, model), f32), shape((tok, model), bf), shape((model, tok), f32), shape((model, tok), bf)]
        else:
            outs = [shape((2 * tok, model), f32), shape((model, 2 * tok), f32)]
        return run_kernel(
            functools.partial(feed_body, count, not sums, last), f"feed_{which[0]}", (1,), sc,
            [(a, IN_VMEM) for a in (*hidt2, *hidt2_peer, gyt, gyt_peer, gy)] + [row_specs[j] for j in which]
            + [(a, IN_VMEM) for j in which for a in w_all[j]] + [(a, IN_VMEM) for a in sums],
            [(a, None if last else IN_VMEM) for a in outs] + [(shape((2 * model + TILE, hh), bf), None)] * count + [(shape((count, 8, hh), f32), None)],
            scratch=[pltpu.VMEM((2 * tok, model), bf), pltpu.VMEM((2 * tok, hh), bf), pltpu.VMEM((2 * tok, hh), bf)],
        )

    own_out, own_sg, w_zero, own_ub = feed([0], ())
    w_all[1:3] = [[after(a, own_ub) for a in pair] for pair in w_all[1:3]]
    w_all.append([wa_far, swap(w_all[2][1], "head", 1)])
    part_out, part_sg, *early = feed(list(range(1, nh - 1)), (own_out, own_sg))
    w_parts, early_ub = [w_zero] + early[:-1], early[-1]
    w_got = [swap(w_parts[m], "head", m) for m in range(1, nh - 1)]
    mix_peer = swap(after(mix, early_ub), "seq", 1)
    out_own, out_send, sg_own, sg_send, w_last, late_ub = feed([nh - 1], (part_out, part_sg), True)
    sg_recv = swap(sg_send, "seq", 1)

    vec_block = (shape((nh, 8, width), f32), None)
    rg, ag, vec2, na, sgt = run_kernel(
        functools.partial(second_back_body, hs, nh), "second_back", (1,), sc,
        [(a, None) for a in (sg_own, sg_recv, res, gyt, gains, mixd, starts, qf)] + in_hbm(all_first),
        [(shape((model, tok), f32), None), (shape((model, tok), bf), None), vec_block,
         (shape((heads, AUG, tok), bf), None), (shape((heads, AUG, 2 * hs), bf), None)],
        scratch=wo_scratch,
    )
    sgt = after(sgt, *w_got)
    g_sent = [swap(sgt, "head", m) for m in peers]
    half_spec = pl.BlockSpec((half, tok), lambda p, sc: (sc[0], 0))
    ag_peer = swap(lax.dynamic_slice_in_dim(ag, (1 - s2) * half, half, 0), "seq", 1)

    na_late = na
    ql, kfg, vg = run_kernel(
        functools.partial(local_back_body, hp, hs), "local_back", (nh,), sc,
        [(qf, feat_spec), (kf, feat_spec), (va, va_spec), (na_late, va_spec), (sin, state_spec), (starts, None)],
        [(shape((heads, hs, tok), bf), lead(hp, hs, tok)), (shape((heads, 2 * hs, tok), f32), feat_spec),
         (shape((heads, hs, tok), f32), lead(hp, hs, tok))],
    )
    g_around = [after(a, ql) for a in g_sent]
    w_got.append(swap(after(w_last, *g_around), "head", nh - 1))
    g_whole = states_together(4 + 3 * nh, [sgt] + g_around)
    after_run = chain_seq(g_whole, False, lambda k: (run_start <= -(k - 1) * length - 1).astype(f32))
    def peer_states(a, m):
        return (a, pl.BlockSpec((hp, AUG, 2 * hs), lambda p, sc: (p ^ m, 0, 0)))

    *pg, fg, map_grads, pb = run_kernel(
        functools.partial(project_back_body, hp, hs, nh), "project_back", (nh,), sc,
        [peer_states(a, m) for a, m in zip(g_around + [after_run], [*peers, 0])] + in_hbm(all_first)
        + [(kf, feat_spec), (va, va_spec), (ql, lead(hp, hs, tok)), (after(kfg, ag_peer, mix_peer), feat_spec), (vg, lead(hp, hs, tok)),
           (proj, lead(1, pc, tok)), (starts, None)],
        [(shape((pc, tok), bf), None)] * nh
        + [(shape((model, tok), f32), None),
           (shape((nh, hs, 128 * hp), f32), lead(1, hs, 128 * hp)), (shape((nh, 8, pc), f32), lead(1, 8, pc))],
        scratch=[pltpu.VMEM((1, pc, tok), bf)] + first_scratch,
    )
    pg_peer = [swap(a, "seq", 1) for a in pg]
    tg, vec1 = run_kernel(
        functools.partial(first_back_body, nh), "first_back", (1,), sc,
        [(fg, None), (x, None), (rg, None), (gains, None)], [(shape((nh, width, tok), bf), None), vec_block],
    )
    last_rows = -(-(pc + hs + TILE + width) // (nz * TILE)) * nz * TILE
    last_parts = run_kernel(
        functools.partial(last_grads_body, nh), "last_grads", (1,), sc,
        [(a, None) for a in (*pg, *pg_peer)] + [(hid, half_spec), (hid_peer, None)]
        + [(a, None) for a in (after(map_grads, w_got[-1]), pb, own_ub, early_ub, late_ub, vec1, vec2, mix, mix_peer)]
        + [(ag, half_spec), (ag_peer, None)],
        [(shape((last_rows, half), bf), None)] * nh,
        scratch=[pltpu.VMEM((TILE, half), f32)],
    )

    feed_rows, part_rows = all_rows // nz, last_rows // nz

    def halves_of(body, name, arrays, rows):
        return run_kernel(
            functools.partial(body, nh, nz), name, (1,), sc, [(a, None) for a in arrays],
            [(shape((2 * rows, hh), bf), None)] * 2, scratch=[pltpu.VMEM((nz * rows, hh), bf)],
        )

    def quarter(name, keep, got, rows):
        return run_kernel(
            pair_sum_body, name, (1,), sc, [(keep, None), (got, None)], [(shape((rows, hh), bf), None)] * 2
        )

    def spread(one):
        two = swap(one, "dp", 2)
        return [one, swap(one, "dp", 1), two, swap(two, "dp", 1)]

    feed_keep, feed_send = halves_of(
        feed_sum_body, "feed_sum", (after(w_parts[0], *last_parts), *w_got), feed_rows
    )
    feed_keep, feed_send = beyond_chip(feed_keep), beyond_chip(feed_send)
    out_recv = swap(after(out_send, *pg), "seq", 1)
    (chunks,) = run_kernel(
        functools.partial(block_out_body, nh), "block_out", (1,), sc,
        [(after(res, feed_keep), None), (out_own, None), (out_recv, None), (tg, None)] + row_specs,
        [(shape((nh, 2, width, tok), bf), None)], scratch=[pltpu.VMEM((model, tok), f32)],
    )
    feed_near, feed_next = quarter("feed_pair", feed_keep, swap(feed_send, "dp", 1), feed_rows)
    feed_far = swap(feed_next, "dp", 2)
    last_got = [after(swap(last_parts[m], "head", m), chunks, feed_near) for m in peers]
    last_keep, last_send = halves_of(last_sum_body, "last_sum", (last_parts[0], *last_got), part_rows)
    last_keep, last_send = beyond_chip(last_keep), beyond_chip(last_send)
    last_pair = swap(last_send, "dp", 1)
    feed_one = (feed_near.astype(f32) + after(feed_far, last_keep).astype(f32)).astype(bf)
    last_near, last_next = quarter("last_pair", last_keep, after(last_pair, feed_one), part_rows)
    last_one = (last_near.astype(f32) + swap(last_next, "dp", 2).astype(f32)).astype(bf)
    feed_total, last_total = spread(feed_one), spread(last_one)
    chunks = trade(after(chunks, last_keep), "head")
    block_out, tokens_grad = run_kernel(
        functools.partial(lay_out_body, nh), "lay_out", (1,), sc, [(chunks, None)],
        [(shape((width, length), bf), None)] * 2,
    )
    upweight_grad, downweight_grad = run_kernel(
        functools.partial(feed_out_body, nh, nz), "feed_result", (1,), sc, [(a, None) for a in feed_total] + [(swap(a, "seq", 1), None) for a in feed_total],
        [(shape((model, hidden), f32), None), (shape((hidden, model), f32), None)],
        scratch=[pltpu.VMEM((2, all_rows, hh), bf)],
    )
    last_total = [after(a, upweight_grad, block_out) for a in last_total]
    qkv_grad, outweight_grad, query_grad, key_grad, qkvbias_grad, upbias_grad, rows = run_kernel(
        functools.partial(last_out_body, hs, nh, nz), "last_result", (1,), sc, [(a, None) for a in last_total] + [(swap(a, "seq", 1), None) for a in last_total],
        [(shape((pc, model), f32), None), (shape((width, model), f32), None), (shape((hp, hs, hs), f32), None),
         (shape((hp, hs, hs), f32), None),
         (shape((1, pc), f32), None), (shape((1, hidden), f32), None), (shape((TILE, half), f32), None)],
        scratch=[pltpu.VMEM((2, last_rows, half), bf)],
    )
    vec = rows[4:10, 0:width]
    return (block_out.T[None], tokens_grad.T[None], vec[4], vec[5], qkv_grad.T, qkvbias_grad[0], query_grad, key_grad,
            outweight_grad, vec[2], vec[0], vec[1], upweight_grad, upbias_grad[0], downweight_grad, vec[3])


def solution(mesh):
    wide = P("dp", "seq", "head")
    return jax.shard_map(
        local,
        mesh=mesh,
        in_specs=(wide, P(), P(), P(None, "head"), P("head"), P("head", None, None), P("head", None, None),
                  P("head", None), P("head"), P(), P(), P(None, "head"), P("head"), P("head", None), P("head"),
                  P("dp", "seq"), wide),
        out_specs=(wide, wide, P("head"), P("head"), P(None, "head"), P("head"), P("head", None, None),
                   P("head", None, None), P("head", None), P("head"), P("head"), P("head"), P(None, "head"), P("head"),
                   P("head", None), P("head")),
        check_vma=False,
    )
```

```python
import functools

import jax
import jax.numpy as jnp
from jax import lax
from jax.experimental import pallas as pl
from jax.experimental.pallas import tpu as pltpu
from jax.sharding import PartitionSpec as P

eps = 1e-05
gelu_scale = 0.7978845608028654
bf = jnp.bfloat16
f32 = jnp.float32
AUG = 80
TILE = 16


def nn(a, b):
    return lax.dot_general(a, b, (((1,), (0,)), ((), ())), preferred_element_type=f32)


def nt(a, b):
    return lax.dot_general(a, b, (((1,), (1,)), ((), ())), preferred_element_type=f32)


def tn(a, b):
    return lax.dot_general(a, b, (((0,), (0,)), ((), ())), preferred_element_type=f32)


def shape(dims, dtype):
    return jax.ShapeDtypeStruct(tuple(dims), dtype)


def whole(a):
    dims = tuple(a.shape)
    return pl.BlockSpec(dims, lambda *_: (0,) * len(dims))


def lead(count, *dims):
    return pl.BlockSpec((count,) + dims, lambda p, sc: (p,) + (0,) * len(dims))


def run_kernel(body, name, grid, scalars, ins, outs, scratch=(), aliases=None):
    return pl.pallas_call(
        body,
        out_shape=[o for o, _ in outs],
        grid_spec=pltpu.PrefetchScalarGridSpec(
            num_scalar_prefetch=1,
            grid=grid,
            in_specs=[spec or whole(a) for a, spec in ins],
            out_specs=[spec or whole(o) for o, spec in outs],
            scratch_shapes=list(scratch),
        ),
        compiler_params=pltpu.CompilerParams(vmem_limit_bytes=18 * 2**20),
        cost_estimate=pl.CostEstimate(flops=0, bytes_accessed=0, transcendentals=0),
        input_output_aliases=aliases or {},
        name=name,
    )(scalars, *[a for a, _ in ins])


def norm_columns(values):
    center = values - jnp.mean(values, axis=0, keepdims=True)
    inv_std = lax.rsqrt(jnp.mean(center * center, axis=0, keepdims=True) + eps)
    return center * inv_std, inv_std


def norm_columns_back(grad, normed, inv_std, gain):
    scaled = grad * gain
    return inv_std * (
        scaled
        - jnp.mean(scaled, axis=0, keepdims=True)
        - normed * jnp.mean(scaled * normed, axis=0, keepdims=True)
    )


def column(rows, at, width):
    only = jnp.where(lax.broadcasted_iota(jnp.int32, rows.shape, 0) == at, rows.astype(f32), 0.0).astype(bf)
    upright = tn(only, jnp.ones((TILE, 128), bf))
    return jnp.concatenate([upright] * (width // 128), axis=1)


def row_sums(values):
    ones = jnp.ones((8, values.shape[1]), bf)
    if values.dtype == bf:
        return nt(ones, values)
    high = values.astype(bf)
    return nt(ones, high) + nt(ones, (values - high.astype(f32)).astype(bf))


def gelu_pair(up_pre):
    square = up_pre * up_pre
    tanh_value = jnp.tanh(gelu_scale * (up_pre + 0.044715 * square * up_pre))
    half_one = 0.5 * (1.0 + tanh_value)
    slope = half_one + 0.5 * up_pre * (1.0 - tanh_value * tanh_value) * gelu_scale * (
        1.0 + 3.0 * 0.044715 * square
    )
    return up_pre * half_one, slope


def soft_columns(logits):
    top = jnp.exp(logits - jnp.max(logits, axis=0, keepdims=True))
    return top / jnp.sum(top, axis=0, keepdims=True)


def ahead_mask(starts, rows, first_column, columns):
    j = lax.broadcasted_iota(jnp.int32, (rows, columns), 0)
    i = lax.broadcasted_iota(jnp.int32, (rows, columns), 1) + first_column
    return (j <= i) & (j >= starts[0:1, first_column : first_column + columns])


def causal_pieces(tokens):
    step = tokens // 2
    return ((0, step, step), (step, step, tokens))


HBM = pl.BlockSpec(memory_space=pl.ANY)
IN_VMEM = pl.BlockSpec(memory_space=pltpu.VMEM)


def load_all(refs, places, sems):
    copies = [pltpu.make_async_copy(ref, place, sems.at[k]) for k, (ref, place) in enumerate(zip(refs, places))]
    for copy in copies:
        copy.start()
    return copies


def part_places(refs, scratch, core):
    return [scratch.at[2 * (k // 2) + (core if k % 2 == 0 else 1 - core)] for k in range(len(refs))]


def tables_body(nh, ids, pos_ref, row_ref, starts_ref, table_ref):
    length = pos_ref.shape[1]
    tok = length // nh
    h = ids[1]
    own = row_ref[:, pl.ds(pl.multiple_of(h * tok, 128), tok)]
    lane = lax.broadcasted_iota(jnp.int32, (8, tok), 1)
    starts_ref[...] = lane - own

    def start_of(t):
        return t - pos_ref[0, t]

    def flag(value):
        return jnp.where(value, 1, 0)

    run_last = start_of(length - 1)
    other = [h ^ m for m in range(nh)]
    values = [ids[0], start_of((h + 1) * tok - 1) - h * tok]
    values += [flag((q < h) & (start_of(h * tok) <= (q + 1) * tok - 1)) for q in other[1:]]
    values += [flag(start_of(h * tok) < 0)]
    values += [flag((q > h) & (start_of(q * tok) <= (h + 1) * tok - 1)) for q in other[1:]]
    values += [flag(run_last <= (h + 1) * tok - 1), h, ids[2]]
    values += [flag(run_last <= (q + 1) * tok - 1) for q in other]
    values += [flag(start_of(q * tok) < 0) for q in other]
    lane = lax.broadcasted_iota(jnp.int32, (8, 128), 1)
    table = jnp.zeros((8, 128), jnp.int32)
    for k, value in enumerate(values):
        table = jnp.where(lane == k, value, table)
    table_ref[...] = table


def state_sum_body(hp, nh, first, sc, *refs):
    for i in range(refs[nh].shape[0]):
        total = jnp.zeros(refs[0].shape[1:], f32)
        for m in range(nh):
            total += jnp.where(sc[first + m] > 0, refs[m][((i // hp) ^ m) * hp + i % hp].astype(f32), 0.0)
        refs[nh][i] = total.astype(bf)


def pack_body(sc, qkv_ref, qm_ref, km_ref, qb_ref, ub_ref, ob_ref, db_ref, out_ref, up_ref, down_ref,
              first_ref, other_ref, wa_ref, wb_ref, rows_ref):
    pc, model = qkv_ref.shape
    hs = qm_ref.shape[1]
    width = ob_ref.shape[1]
    rows_ref[...] = jnp.zeros_like(rows_ref)
    rows_ref[0:1, 0:pc] = qb_ref[...].astype(f32)
    rows_ref[1:2, 0 : ub_ref.shape[1]] = ub_ref[...].astype(f32)
    rows_ref[2:3, 0:width] = ob_ref[...].astype(f32)
    rows_ref[3:4, 0:width] = db_ref[...].astype(f32)
    for core, ref in ((sc[0], first_ref), (1 - sc[0], other_ref)):
        cut = pc // 2
        ref[0:cut, :] = qkv_ref[pl.ds(pl.multiple_of(core * cut, TILE), cut), :]
        ref[cut : cut + hs // 2, :] = jnp.zeros((hs // 2, model), bf)
        for i in range(qm_ref.shape[0] // hs):
            for k in range(2):
                rows = slice(i * hs + k * hs // 2, i * hs + (k + 1) * hs // 2)
                at = k * (model // 2) + 128 * i
                own = jnp.where(core == 0, qm_ref[rows, :].astype(f32), km_ref[rows, :].astype(f32))
                ref[cut : cut + hs // 2, at : at + hs] = own.astype(bf)
        cut += hs // 2
        ref[cut : cut + TILE, :] = rows_ref[...].astype(bf)
        half = out_ref.shape[0] // 2
        ref[cut + TILE :, :] = out_ref[pl.ds(pl.multiple_of(core * half, TILE), half), :]
    half = down_ref.shape[0] // 2
    at = pl.ds(pl.multiple_of(sc[0] * half, TILE), half)
    lanes = pl.ds(pl.multiple_of(sc[0] * half, 128), half)
    for k, w_ref in enumerate((wa_ref, wb_ref)):
        part = slice(k * half, (k + 1) * half)
        w_ref[:, 0:half] = up_ref[part, lanes]
        w_ref[:, half:] = down_ref[at, part]


def chunks_body(nh, sc, a_ref, b_ref, o_ref):
    tokens = o_ref.shape[3]
    for q in range(nh):
        for k, ref in enumerate((a_ref, b_ref)):
            o_ref[q, k] = ref[:, q * tokens : (q + 1) * tokens]


def first_norm_body(sc, x_ref, gain_ref, hid_ref):
    normed, _ = norm_columns(x_ref[...].astype(f32))
    width = x_ref.shape[1]
    gains = gain_ref[...]
    hid_ref[...] = (normed * column(gains, 0, width) + column(gains, 1, width)).astype(bf)


def turn_body(sc, a_ref, b_ref, o_ref):
    tokens = a_ref.shape[1]
    o_ref[0:tokens, :] = a_ref[...].T
    o_ref[tokens:, :] = b_ref[...].T


def map_of(first_ref, at, i, hs, cut):
    model = first_ref.shape[2]
    rows = slice(cut, cut + hs // 2)
    return jnp.concatenate(
        [first_ref[at, rows, k * (model // 2) + 128 * i : k * (model // 2) + 128 * i + hs] for k in range(2)], axis=0
    )


def project_body(hp, hs, count, sc, hid_ref, starts_ref, *refs):
    first_refs = refs[0 : 2 * count]
    proj_ref, qf_ref, kf_ref, va_ref, st_ref, w_ref, sems = refs[-7:]
    p = pl.program_id(0)
    wait_for_piece(first_refs, w_ref, sems, sc)
    pc, tokens = proj_ref.shape[1:]
    cut = pc // 2
    bias = column(w_ref[2 * p, cut + hs // 2 : cut + hs // 2 + TILE, 0:pc], 0, tokens)
    for k in range(2):
        rows = slice(k * cut, (k + 1) * cut)
        proj_ref[0, rows, :] = (nn(w_ref[2 * p + k, 0:cut, :], hid_ref[...]) + bias[rows, :]).astype(bf)
    included = (starts_ref[0:1, :] == sc[1]).astype(f32)
    extra = lax.broadcasted_iota(jnp.int32, (AUG - hs, tokens), 0)
    extra = jnp.where(extra < 2, 1.0, 0.0).astype(bf)
    for i in range(hp):
        row = 3 * hs * i
        for part, out in ((0, qf_ref), (1, kf_ref)):
            own_map = map_of(w_ref, 2 * p + part, i, hs, cut)
            logits = tn(own_map, proj_ref[0, row + part * hs : row + (part + 1) * hs, :])
            out[i, 0:hs, :] = soft_columns(logits).astype(bf)
            out[i, hs : 2 * hs, :] = soft_columns(-logits).astype(bf)
        va_ref[i, 0:hs, :] = proj_ref[0, row + 2 * hs : row + 3 * hs, :]
        va_ref[i, hs:AUG, :] = extra
        kept = (va_ref[i].astype(f32) * included).astype(bf)
        st_ref[i] = nt(kept, kf_ref[i]).astype(bf)


def wait_for_piece(first_refs, w_ref, sems, sc):
    p = pl.program_id(0)
    places = part_places(first_refs, w_ref, sc[0])
    rows = w_ref.shape[1]
    copies = [
        pltpu.make_async_copy(ref.at[pl.ds(0, rows), :], place, sems.at[k])
        for k, (ref, place) in enumerate(zip(first_refs, places))
    ]

    @pl.when(p == 0)
    def _():
        for copy in copies:
            copy.start()

    for k, copy in enumerate(copies):

        @pl.when(p == k // 2)
        def _(copy=copy):
            copy.wait()


def local_mix_body(hp, sc, qf_ref, kf_ref, va_ref, starts_ref, num_ref):
    tokens = qf_ref.shape[2]
    starts = starts_ref[...]
    for first, width, rows in causal_pieces(tokens):
        mask = ahead_mask(starts, rows, first, width)
        for i in range(hp):
            scores = tn(kf_ref[i, :, 0:rows], qf_ref[i, :, first : first + width])
            scores = jnp.where(mask, scores, 0.0).astype(bf)
            num_ref[i, :, first : first + width] = nn(va_ref[i, :, 0:rows], scores)


def weighted_state(sc, slot, refs, i, hp):
    total = jnp.where(sc[slot + len(refs) - 1] > 0, refs[-1][i].astype(f32), 0.0)
    for m, ref in enumerate(refs[:-1], 1):
        total += jnp.where(sc[slot + m - 1] > 0, ref[((i // hp) ^ m) * hp + i % hp].astype(f32), 0.0)
    return total


def load_out_weight(sc, first_refs, w_ref, sems):
    rows = w_ref.shape[0] // len(first_refs)
    at = first_refs[0].shape[0] - rows
    places = [
        w_ref.at[pl.ds(pl.multiple_of(rows * (2 * (k // 2) + (sc[0] if k % 2 == 0 else 1 - sc[0])), TILE), rows), :]
        for k in range(len(first_refs))
    ]
    return load_all([ref.at[pl.ds(at, rows), :] for ref in first_refs], places, sems)


def mix_out_body(hp, hs, nh, sc, num_ref, qf_ref, starts_ref, x_ref, gain_ref, *refs):
    state_refs, row_refs, wo_refs = refs[0:nh], refs[nh : 2 * nh], refs[2 * nh : 4 * nh]
    sin_ref, mixd_ref, mix_ref, res_ref, top_ref, low_ref, w_ref, sems = refs[4 * nh :]
    copies = load_out_weight(sc, wo_refs, w_ref, sems)
    uses = starts_ref[0:1, :] < 0
    model, tokens = x_ref.shape
    for i in range(num_ref.shape[0]):
        state = weighted_state(sc, 2, state_refs, i, hp).astype(bf)
        sin_ref[i] = state
        num = num_ref[i] + jnp.where(uses, nn(state, qf_ref[i]), 0.0)
        mixture = num[0:hs, :] / num[hs : hs + 1, :]
        mixd_ref[i, 0:hs, :] = mixture
        mixd_ref[i, hs : hs + 8, :] = num[hs : hs + 8, :]
        mix_ref[i * hs : (i + 1) * hs, :] = mixture.astype(bf)
    for copy in copies:
        copy.wait()
    res_ref[...] = x_ref[...].astype(f32) + tn(w_ref[...], mix_ref[...])
    width = model // nh
    h = sc[2 + 2 * nh]
    for j in range(nh):
        rows = pl.ds(pl.multiple_of((h ^ j) * width, TILE), width)
        res_ref[rows, :] += column(row_refs[j][:, 0:width], 2, tokens)
    normed, _ = norm_columns(res_ref[...].astype(bf).astype(f32))
    gains = gain_ref[...]
    hidden = (normed * column(gains, 2, tokens) + column(gains, 3, tokens)).astype(bf)
    half = top_ref.shape[0]
    top_ref[...] = hidden[0:half, :]
    low_ref[...] = hidden[half:, :]


def feed_body(count, first, last, sc, *refs):
    hidt_ins, gyt_ins, gy_in = refs[0:4], refs[4:6], refs[6]
    row_refs = refs[7 : 7 + count]
    w_ins = refs[7 + count : 7 + 3 * count]
    refs = refs[7 + 3 * count :]
    if first:
        out_ref, sg_ref = refs[0:2]
        refs = refs[2:]
    elif not last:
        out_in, sg_in, out_ref, sg_ref = refs[0:4]
        refs = refs[4:]
    else:
        out_in, sg_in, out_own, out_peer, sg_own, sg_peer = refs[0:6]
        refs = refs[6:]
    w_refs, ub_ref, refs = refs[0:count], refs[count], refs[count + 1 :]
    hid_ref, act_ref, ug_ref = refs
    mid, tokens = hidt_ins[0].shape
    model = 2 * mid
    half = act_ref.shape[1]
    runs = [slice(0, tokens), slice(tokens, 2 * tokens)]
    lo, hi = slice(0, half), slice(half, 2 * half)
    at_half = pl.ds(pl.multiple_of(sc[0] * half, 128), half)
    for k in range(count):
        bias = row_refs[k][:, at_half].astype(f32)[1:2, :]
        first_w, second_w = w_ins[2 * k], w_ins[2 * k + 1]
        for which, rows in enumerate(runs):
            if k == 0:
                for m in range(2):
                    hid_ref[rows, m * mid : (m + 1) * mid] = hidt_ins[2 * which + m][...].T
            up_pre = nn(hid_ref[rows, lo], first_w[:, lo]) + nn(hid_ref[rows, hi], second_w[:, lo]) + bias
            value, slope = gelu_pair(up_pre)
            act_ref[rows, :] = value.astype(bf)
            back = nt(gy_in[rows, lo], first_w[:, hi]) + nt(gy_in[rows, hi], second_w[:, hi])
            ug_ref[rows, :] = (back * slope).astype(bf)
        ub_ref[k] = nn(jnp.ones((8, 2 * tokens), bf), ug_ref[...])
        for m in range(2):
            grads = [nn(hidt_ins[2 * r + m][...], ug_ref[runs[r], :]) for r in range(2)]
            w_refs[k][m * mid : (m + 1) * mid, :] = (grads[0] + grads[1]).astype(bf)
        grads = [nn(gyt_ins[r][...], act_ref[runs[r], :]) for r in range(2)]
        w_refs[k][model : 2 * model, :] = (grads[0] + grads[1]).astype(bf)
        w_refs[k][2 * model :, :] = jnp.zeros((TILE, half), bf)
        for at, w in ((lo, first_w), (hi, second_w)):
            if first and k == 0:
                out_ref[:, at] = nn(act_ref[...], w[:, hi])
                sg_ref[at, :] = nt(w[:, lo], ug_ref[...])
            elif not last and k == 0:
                out_ref[:, at] = out_in[:, at] + nn(act_ref[...], w[:, hi])
                sg_ref[at, :] = sg_in[at, :] + nt(w[:, lo], ug_ref[...])
            elif not last:
                out_ref[:, at] += nn(act_ref[...], w[:, hi])
                sg_ref[at, :] += nt(w[:, lo], ug_ref[...])
            else:
                out = out_in[:, at] + nn(act_ref[...], w[:, hi])
                out_own[:, at] = out[runs[0], :]
                out_peer[:, at] = out[runs[1], :].astype(bf)
                sg = sg_in[at, :] + nt(w[:, lo], ug_ref[...])
                sg_own[at, :] = sg[:, runs[0]]
                sg_peer[at, :] = sg[:, runs[1]].astype(bf)


def block_out_body(nh, sc, res_ref, out_ref, out2_ref, tg_ref, *refs):
    row_refs, o_ref, total_ref = refs[0:nh], refs[nh], refs[nh + 1]
    model, tokens = res_ref.shape
    width = model // nh
    total_ref[...] = res_ref[...] + (out_ref[...] + out2_ref[...].astype(f32)).T
    h = sc[2 + 2 * nh]
    for j in range(nh):
        rows = pl.ds(pl.multiple_of((h ^ j) * width, TILE), width)
        o_ref[j, 1] = tg_ref[j]
        o_ref[h ^ j, 0] = (total_ref[rows, :] + column(row_refs[j][:, 0:width], 3, tokens)).astype(bf)


def lay_out_body(nh, sc, in_ref, *o_refs):
    tokens = in_ref.shape[3]
    for k in range(2):
        for q in range(nh):
            o_refs[k][:, q * tokens : (q + 1) * tokens] = in_ref[q, k]


def second_back_body(hs, nh, sc, sg_ref, sg2_ref, res_ref, gyt_ref, gain_ref, mixd_ref, starts_ref, qf_ref, *refs):
    wo_refs, (rg_ref, ag_ref, vec_ref, na_ref, sgt_ref, w_ref, sems) = refs[0 : 2 * nh], refs[2 * nh :]
    copies = load_out_weight(sc, wo_refs, w_ref, sems)
    model, tokens = sg_ref.shape
    width = model // nh
    normed, inv_std = norm_columns(res_ref[...].astype(bf).astype(f32))
    sg = sg_ref[...] + sg2_ref[...].astype(f32)
    res_grad = gyt_ref[...].astype(f32) + norm_columns_back(sg, normed, inv_std, column(gain_ref[...], 2, tokens))
    rg_ref[...] = res_grad
    ag_ref[...] = res_grad.astype(bf)
    uses = (starts_ref[0:1, :] < 0).astype(f32)
    for copy in copies:
        copy.wait()
    mg = nn(w_ref[...], ag_ref[...])
    row = lax.broadcasted_iota(jnp.int32, (AUG - hs, tokens), 0)
    for i in range(qf_ref.shape[0]):
        num = mg[i * hs : (i + 1) * hs, :] / mixd_ref[i, hs : hs + 1, :]
        den = -jnp.sum(num * mixd_ref[i, 0:hs, :], axis=0, keepdims=True)
        high = den.astype(bf).astype(f32)
        extra = jnp.where(row == 0, high, jnp.where(row == 1, den - high, 0.0))
        na_ref[i, 0:hs, :] = num.astype(bf)
        na_ref[i, hs:AUG, :] = extra.astype(bf)
        kept = (na_ref[i].astype(f32) * uses).astype(bf)
        sgt_ref[i] = nt(kept, qf_ref[i]).astype(bf)
    for at, value in enumerate((sg * normed, sg, ag_ref[...], gyt_ref[...])):
        sums = row_sums(value)
        for p in range(nh):
            vec_ref[p, at : at + 1, :] = sums[0:1, p * width : (p + 1) * width]


def halves_back(feat, grad, hs):
    parts = []
    for k in range(2):
        soft = feat[k * hs : (k + 1) * hs, :].astype(f32)
        own = grad[k * hs : (k + 1) * hs, :]
        weight = jnp.sum(soft * own, axis=0, keepdims=True) / jnp.sum(soft, axis=0, keepdims=True)
        parts.append(soft * (own - weight))
    return (parts[0] - parts[1]).astype(bf)


def local_back_body(hp, hs, sc, qf_ref, kf_ref, va_ref, na_ref, sin_ref, starts_ref, ql_ref, kfg_ref, vg_ref):
    tokens = qf_ref.shape[2]
    starts = starts_ref[...]
    step = tokens // 2
    uses = starts[0:1, :] < 0
    masks = [ahead_mask(starts, rows, first, width) for first, width, rows in causal_pieces(tokens)]
    for i in range(hp):
        na = na_ref[i]
        through = tn(sin_ref[i], na)
        for which, (first, width, rows) in enumerate(causal_pieces(tokens)):
            at = slice(first, first + width)
            mask = masks[which]
            scores = jnp.where(mask, tn(kf_ref[i, :, 0:rows], qf_ref[i, :, at]), 0.0).astype(bf)
            sgrad = jnp.where(mask, tn(va_ref[i, :, 0:rows], na[:, at]), 0.0).astype(bf)
            qfg = nn(kf_ref[i, :, 0:rows], sgrad) + jnp.where(uses[:, at], through[:, at], 0.0)
            ql_ref[i, :, at] = halves_back(qf_ref[i, :, at], qfg, hs)
            kfg = nt(qf_ref[i, :, at], sgrad)
            vg = nt(na[:, at], scores)[0:hs, :]
            if which == 0:
                kfg_ref[i, :, 0:rows] = kfg
                vg_ref[i, :, 0:rows] = vg
            else:
                kfg_ref[i, :, 0:step] += kfg[:, 0:step]
                vg_ref[i, :, 0:step] += vg[:, 0:step]
                kfg_ref[i, :, step:] = kfg[:, step:]
                vg_ref[i, :, step:] = vg[:, step:]


def join_extra(state, hs):
    row = lax.broadcasted_iota(jnp.int32, state.shape, 0)
    both = state[hs : hs + 1, :] + state[hs + 1 : hs + 2, :]
    return jnp.where(row < hs, state, jnp.where(row == hs, both, 0.0))


def project_back_body(hp, hs, nh, sc, *refs):
    state_refs, first_refs, refs = refs[0:nh], refs[nh : 3 * nh], refs[3 * nh :]
    kf_ref, va_ref, ql_ref, kfg_ref, vg_ref, proj_ref, starts_ref, *pg_refs, fg_ref, mg_ref, pb_ref, pg_ref, first_ref, sems = refs
    p = pl.program_id(0)
    wait_for_piece(first_refs, first_ref, sems, sc)
    included = starts_ref[0:1, :] == sc[1]
    cut = pg_ref.shape[1] // 2
    for i in range(hp):
        total = jnp.where(sc[1 + 2 * nh] > 0, state_refs[-1][i].astype(f32), 0.0)
        for m in range(1, nh):
            total += jnp.where(sc[1 + nh + m] > 0, state_refs[m - 1][i].astype(f32), 0.0)
        state = join_extra(total, hs).astype(bf)
        kfg = kfg_ref[i] + jnp.where(included, tn(state, va_ref[i]), 0.0)
        vg = vg_ref[i] + jnp.where(included, nn(state, kf_ref[i])[0:hs, :], 0.0)
        klg = halves_back(kf_ref[i], kfg, hs)
        qlg = ql_ref[i]
        row = 3 * hs * i
        pg_ref[0, row : row + hs, :] = nn(map_of(first_ref, 2 * p, i, hs, cut), qlg).astype(bf)
        pg_ref[0, row + hs : row + 2 * hs, :] = nn(map_of(first_ref, 2 * p + 1, i, hs, cut), klg).astype(bf)
        pg_ref[0, row + 2 * hs : row + 3 * hs, :] = vg.astype(bf)
        q_grad = nt(proj_ref[0, row : row + hs, :], qlg)
        k_grad = nt(proj_ref[0, row + hs : row + 2 * hs, :], klg)
        mg_ref[0, :, 128 * i : 128 * (i + 1)] = jnp.concatenate([q_grad, k_grad], axis=1)
    for j, ref in enumerate(pg_refs):

        @pl.when(p == j)
        def _(ref=ref):
            ref[...] = pg_ref[0]

    pb_ref[0] = row_sums(pg_ref[0])
    grad = tn(first_ref[2 * p, 0:cut, :], pg_ref[0, 0:cut, :]) + tn(first_ref[2 * p + 1, 0:cut, :], pg_ref[0, cut:, :])

    @pl.when(pl.program_id(0) == 0)
    def _():
        fg_ref[...] = grad

    @pl.when(pl.program_id(0) > 0)
    def _():
        fg_ref[...] += grad


def first_back_body(nh, sc, fg_ref, x_ref, rg_ref, gain_ref, tg_ref, vec_ref):
    model, tokens = fg_ref.shape
    width = model // nh
    normed, inv_std = norm_columns(x_ref[...].astype(f32))
    fg = fg_ref[...]
    gain = column(gain_ref[...], 0, tokens)
    tg = (rg_ref[...] + norm_columns_back(fg, normed, inv_std, gain)).astype(bf)
    for p in range(nh):
        tg_ref[p] = tg[p * width : (p + 1) * width, :]
    for at, value in enumerate((fg * normed, fg)):
        sums = row_sums(value)
        for p in range(nh):
            vec_ref[p, at : at + 1, :] = sums[0:1, p * width : (p + 1) * width]


def split_quarters(nh, nz, sc, total_ref, keep_ref, send_ref):
    part = total_ref.shape[0] // nz
    for k in range(nz):
        o_ref = keep_ref if k % 2 == 0 else send_ref
        at = pl.ds(pl.multiple_of((sc[3 + 2 * nh] ^ k) * part, TILE), part)
        o_ref[(k // 2) * part : (k // 2 + 1) * part, :] = total_ref[at, :]


def feed_sum_body(nh, nz, sc, *refs):
    keep_ref, send_ref, total_ref = refs[nh:]
    rows = total_ref.shape[0]
    total_ref[...] = sum(ref[0:rows, :].astype(f32) for ref in refs[0:nh]).astype(bf)
    split_quarters(nh, nz, sc, total_ref, keep_ref, send_ref)


def last_sum_body(nh, nz, sc, *refs):
    keep_ref, send_ref, total_ref = refs[nh:]
    total_ref[...] = sum(ref[...].astype(f32) for ref in refs[0:nh]).astype(bf)
    split_quarters(nh, nz, sc, total_ref, keep_ref, send_ref)


def pair_sum_body(sc, own_ref, got_ref, keep_ref, send_ref):
    part = keep_ref.shape[0]
    keep_ref[...] = (own_ref[0:part, :].astype(f32) + got_ref[0:part, :].astype(f32)).astype(bf)
    send_ref[...] = (own_ref[part:, :].astype(f32) + got_ref[part:, :].astype(f32)).astype(bf)


def last_grads_body(nh, sc, *refs):
    pg_refs, pg2_refs, refs = refs[0:nh], refs[nh : 2 * nh], refs[2 * nh :]
    hid_ref, hid2_ref, mg_ref, pb_ref, own_ref, early_ref, late_ref, vec1_ref, vec2_ref = refs[0:9]
    mix_ref, mix2_ref, ag_ref, ag2_ref, *o_refs, rows_ref = refs[9:]
    pc, half = pg_refs[0].shape[0], hid_ref.shape[0]
    hs = mg_ref.shape[1]
    width = vec1_ref.shape[2]
    h = sc[2 + 2 * nh]
    for j in range(nh):
        o_ref = o_refs[j]
        o_ref[0:pc, :] = (nt(pg_refs[j][...], hid_ref[...]) + nt(pg2_refs[j][...], hid2_ref[...])).astype(bf)
        o_ref[pc : pc + hs, :] = mg_ref[j].astype(bf)
        ub_ref, k = (own_ref, 0) if j == 0 else (early_ref, j - 1) if j < nh - 1 else (late_ref, 0)
        rows_ref[...] = jnp.zeros_like(rows_ref)
        rows_ref[0:1, :] = pb_ref[j, 0:1, 0:half]
        rows_ref[1:2, 0 : pc - half] = pb_ref[j, 0:1, half:]
        rows_ref[2:3, :] = jnp.where(sc[0] == 0, ub_ref[k, 0:1, :], 0.0)
        rows_ref[3:4, :] = jnp.where(sc[0] == 0, 0.0, ub_ref[k, 0:1, :])
        rows_ref[4:8, 0:width] = vec2_ref[h ^ j, 0:4, :]
        rows_ref[8:10, 0:width] = vec1_ref[h ^ j, 0:2, :]
        at = pc + hs + TILE
        o_ref[pc + hs : at, :] = rows_ref[...].astype(bf)
        rows = slice(j * width, (j + 1) * width)
        o_ref[at : at + width, :] = (nt(mix_ref[rows, :], ag_ref[...]) + nt(mix2_ref[rows, :], ag2_ref[...])).astype(bf)
        o_ref[at + width :, :] = jnp.zeros((o_ref.shape[0] - at - width, half), bf)


def join_quarters(nh, nz, sc, refs, total_ref):
    part = refs[0].shape[0]
    for k in range(2 * nz):
        at = pl.ds(pl.multiple_of((sc[3 + 2 * nh] ^ (k % nz)) * part, TILE), part)
        total_ref[k // nz, at, :] = refs[k][...]


def feed_out_body(nh, nz, sc, *refs):
    up_ref, down_ref, total_ref = refs[2 * nz :]
    join_quarters(nh, nz, sc, refs, total_ref)
    model = down_ref.shape[1]
    half = total_ref.shape[2]
    for k, core in enumerate((sc[0], 1 - sc[0])):
        at = pl.ds(pl.multiple_of(core * half, 128), half)
        up_ref[:, at] = total_ref[k, 0:model, :].astype(f32)
        down_ref[at, :] = total_ref[k, model : 2 * model, :].astype(f32).T


def last_out_body(hs, nh, nz, sc, *refs):
    qkv_ref, out_ref, qm_ref, km_ref, qb_ref, ub_ref, vec_ref, total_ref = refs[2 * nz :]
    join_quarters(nh, nz, sc, refs, total_ref)
    pc = qkv_ref.shape[0]
    half = total_ref.shape[2]
    for k, core in enumerate((sc[0], 1 - sc[0])):
        at = pl.ds(pl.multiple_of(core * half, 128), half)
        qkv_ref[:, at] = total_ref[k, 0:pc, :].astype(f32)
        first = pc + hs + TILE
        out_ref[:, at] = total_ref[k, first : first + out_ref.shape[0], :].astype(f32)
    maps = total_ref[0, pc : pc + hs, :].astype(f32) + total_ref[1, pc : pc + hs, :].astype(f32)
    for i in range(qm_ref.shape[0]):
        qm_ref[i] = maps[:, 128 * i : 128 * i + hs]
        km_ref[i] = maps[:, 128 * i + hs : 128 * i + 2 * hs]
    rows = slice(pc + hs, pc + hs + TILE)
    rows = total_ref[0, rows, :].astype(f32) + total_ref[1, rows, :].astype(f32)
    qb_ref[:, 0:half] = rows[0:1, :]
    qb_ref[:, half:] = rows[1:2, 0 : pc - half]
    ub_ref[:, 0:half] = rows[2:3, :]
    ub_ref[:, half:] = rows[3:4, :]
    vec_ref[...] = rows


def swap(a, axis, k):
    n = lax.axis_size(axis)
    return lax.ppermute(a, axis, [(i, i ^ k) for i in range(n)])


def trade(a, axis):
    return lax.all_to_all(a, axis, 0, 0, tiled=True)


def after(a, *others):
    return lax.optimization_barrier((a,) + others)[0]


def chain_seq(part, forward, weight_of):
    n = lax.axis_size("seq")
    total = None
    for k in range(1, n):
        pairs = [(i, i + k) if forward else (i + k, i) for i in range(n - k)]
        if n == 2:
            return lax.ppermute(part, "seq", pairs)
        sent = part if forward else part * weight_of(k).astype(part.dtype)
        got = lax.ppermute(sent, "seq", pairs).astype(f32) * (weight_of(k) if forward else 1.0)
        total = got if total is None else total + got
    return total.astype(bf)


def local(tokens, attn_gain, attn_shift, qkv_weight, qkv_bias, query_map, key_map, out_weight, out_bias,
          mlp_gain, mlp_shift, up_weight, up_bias, down_weight, down_bias, positions, out_grad):
    nh, ns, nz = lax.axis_size("head"), lax.axis_size("seq"), lax.axis_size("dp")
    length, width = tokens.shape[1], tokens.shape[2]
    model = width * nh
    half = model // 2
    hp, hs = query_map.shape[0], query_map.shape[1]
    heads = hp * nh
    pc = qkv_weight.shape[1]
    hidden = up_weight.shape[1]
    hh = hidden // 2
    tok = length // nh
    h = lax.axis_index("head")
    s2 = lax.axis_index("seq") % 2
    peers = range(1, nh)

    ids = jnp.stack([s2, h, lax.axis_index("dp")]).astype(jnp.int32)
    starts, table = pl.pallas_call(
        functools.partial(tables_body, nh),
        out_shape=[shape((8, tok), jnp.int32), shape((8, 128), jnp.int32)],
        in_specs=[pl.BlockSpec(memory_space=pltpu.SMEM), pl.BlockSpec(memory_space=pltpu.SMEM),
                  pl.BlockSpec(memory_space=pltpu.VMEM)],
        name="tables",
    )(ids, positions, positions)
    sc = table[0, 0 : 4 + 4 * nh]
    run_start = -positions[0, 0]

    def beyond_chip(total):
        base = total
        for k in range(1, ns // 2):
            total += lax.ppermute(base, "seq", [(i, (i + 2 * k) % ns) for i in range(ns)])
        return total

    (both,) = run_kernel(
        functools.partial(chunks_body, nh), "chunks", (1,), ids, [(tokens[0].T, None), (out_grad[0].T, None)],
        [(shape((nh, 2, width, tok), bf), None)],
    )
    both = trade(both, "head")

    core_of = jnp.full((1,), s2, jnp.int32)
    gains = jnp.pad(jnp.stack([attn_gain, attn_shift, mlp_gain, mlp_shift]), ((0, TILE - 4), (0, 0)))
    fl = pc // 2 + hs // 2 + TILE
    fr = fl + width // 2
    own, other_half, wa_own, wb_own = run_kernel(
        pack_body, "pack_weights", (1,), core_of,
        [(a, None) for a in (qkv_weight.T, query_map.reshape(-1, hs), key_map.reshape(-1, hs), qkv_bias[None], up_bias[None],
                             out_bias[None], down_bias[None], out_weight, up_weight, down_weight)],
        [(shape((fr, model), bf), None), (shape((fr, model), bf), None), (shape((hh, 2 * hh), bf), None), (shape((hh, 2 * hh), bf), None)],
        scratch=[pltpu.VMEM((TILE, model), f32)],
    )
    x, gyt = [both[:, k].reshape(model, tok) for k in range(2)]
    own = after(own, sc)
    first_got = [swap(own, "head", 1), swap(own, "head", 2)]
    mid = fr // 2 // TILE * TILE
    far_parts = [swap(first_got[0][0:mid], "head", 2), swap(first_got[1][mid:], "head", 1)]
    x, gyt = after(x, *first_got), after(gyt, *first_got)
    gyt_peer = swap(gyt, "seq", 1)
    (hid,) = run_kernel(
        first_norm_body, "first_norm", (1,), core_of, [(x, None), (gains, None)], [(shape((model, tok), bf), None)]
    )
    hid_peer = swap(lax.dynamic_slice_in_dim(hid, (1 - s2) * half, half, 0), "seq", 1)
    (gy,) = run_kernel(
        turn_body, "turn_grad", (1,), core_of, [(gyt, None), (gyt_peer, None)], [(shape((2 * tok, model), bf), None)]
    )
    firsts_of = [[own, other_half]] + [[a, swap(after(a, hid), "seq", 1)] for a in first_got]
    in_hbm = lambda arrays: [(a, HBM) for a in arrays]
    first_scratch = [pltpu.VMEM((2 * nh, fl, model), bf), pltpu.SemaphoreType.DMA((2 * nh,))]
    wo_scratch = [pltpu.VMEM((model, model), bf), pltpu.SemaphoreType.DMA((2 * nh,))]

    va_spec, state_spec, feat_spec = lead(hp, AUG, tok), lead(hp, AUG, 2 * hs), lead(hp, 2 * hs, tok)
    hid_now = after(hid, gyt_peer, hid_peer)

    def project(first_piece, count, so_far):
        def at(spec):
            return pl.BlockSpec(spec.block_shape, lambda p, sc: (p + first_piece,) + (0,) * (len(spec.block_shape) - 1))

        outs = [(shape((nh, pc, tok), bf), at(lead(1, pc, tok))), (shape((heads, 2 * hs, tok), bf), at(feat_spec)),
                (shape((heads, 2 * hs, tok), bf), at(feat_spec)), (shape((heads, AUG, tok), bf), at(va_spec)),
                (shape((heads, AUG, 2 * hs), bf), at(state_spec))]
        arrays = [a for pair in firsts_of[first_piece : first_piece + count] for a in pair]
        return run_kernel(
            functools.partial(project_body, hp, hs, count), f"project_{first_piece}", (count,), sc,
            [(hid_now, None), (starts, None)] + in_hbm(arrays) + in_hbm(so_far), outs,
            scratch=[pltpu.VMEM((2 * count, fl, model), bf), pltpu.SemaphoreType.DMA((2 * count,))],
            aliases={3 + 2 * count + k: k for k in range(len(so_far))},
        )

    so_far = project(0, nh - 1, ())
    far = jnp.concatenate([after(a, so_far[-1]) for a in far_parts])
    firsts_of.append([far, after(swap(far, "seq", 1), so_far[-1])])
    all_first = [a for pair in firsts_of for a in pair]
    row_specs = [(pair[0], pl.BlockSpec((TILE, model), lambda *_: (fl // TILE - 1, 0))) for pair in firsts_of]
    proj, qf, kf, va, states = project(nh - 1, 1, so_far)
    wa_own = after(wa_own, *far_parts)
    wa_x, wa_y = swap(wa_own, "head", 1), swap(wa_own, "head", 2)
    (num,) = run_kernel(
        functools.partial(local_mix_body, hp), "local_mix", (nh,), sc,
        [(qf, feat_spec), (kf, feat_spec), (after(va, gy, wa_x, wa_y), va_spec), (starts, None)],
        [(shape((heads, AUG, tok), f32), va_spec)],
    )
    around = [after(swap(states, "head", m), num) for m in peers]

    def states_together(first, arrays):
        (total,) = run_kernel(
            functools.partial(state_sum_body, hp, nh, first), f"state_sum_{first}", (1,), sc, [(a, None) for a in arrays],
            [(shape((heads, AUG, 2 * hs), bf), None)],
        )
        return total

    whole_run = states_together(4 + 2 * nh, [states] + around)
    before = chain_seq(whole_run, True, lambda k: (run_start <= -(k - 1) * length - 1).astype(f32))

    wb_own = after(wb_own, before)
    wb_x, wb_y = swap(wb_own, "head", 1), swap(wb_own, "head", 2)

    sin, mixd, mix, res, *hidt2 = run_kernel(
        functools.partial(mix_out_body, hp, hs, nh), "mix_out", (1,), sc,
        [(a, None) for a in (num, qf, starts, x, gains, *around, before)] + row_specs + in_hbm(all_first),
        [(shape((heads, AUG, 2 * hs), bf), None), (shape((heads, hs + 8, tok), f32), None), (shape((model, tok), bf), None),
         (shape((model, tok), f32), None), (shape((half, tok), bf), None), (shape((half, tok), bf), None)],
        scratch=wo_scratch,
    )
    hidt2_peer = [swap(a, "seq", 1) for a in hidt2]
    wa_far = swap(after(wa_x, mix), "head", 2)
    w_all = [[wa_own, wb_own], [wa_x, wb_x], [wa_y, wb_y]]

    all_rows = 2 * model

    def feed(which, sums, last=False):
        count = len(which)
        if last:
            outs = [shape((tok, model), f32), shape((tok, model), bf), shape((model, tok), f32), shape((model, tok), bf)]
        else:
            outs = [shape((2 * tok, model), f32), shape((model, 2 * tok), f32)]
        return run_kernel(
            functools.partial(feed_body, count, not sums, last), f"feed_{which[0]}", (1,), sc,
            [(a, IN_VMEM) for a in (*hidt2, *hidt2_peer, gyt, gyt_peer, gy)] + [row_specs[j] for j in which]
            + [(a, IN_VMEM) for j in which for a in w_all[j]] + [(a, IN_VMEM) for a in sums],
            [(a, None if last else IN_VMEM) for a in outs] + [(shape((2 * model + TILE, hh), bf), None)] * count + [(shape((count, 8, hh), f32), None)],
            scratch=[pltpu.VMEM((2 * tok, model), bf), pltpu.VMEM((2 * tok, hh), bf), pltpu.VMEM((2 * tok, hh), bf)],
        )

    own_out, own_sg, w_zero, own_ub = feed([0], ())
    w_all[1:3] = [[after(a, own_ub) for a in pair] for pair in w_all[1:3]]
    w_all.append([wa_far, swap(w_all[2][1], "head", 1)])
    part_out, part_sg, *early = feed(list(range(1, nh - 1)), (own_out, own_sg))
    w_parts, early_ub = [w_zero] + early[:-1], early[-1]
    w_got = [swap(w_parts[m], "head", m) for m in range(1, nh - 1)]
    mix_peer = swap(after(mix, early_ub), "seq", 1)
    out_own, out_send, sg_own, sg_send, w_last, late_ub = feed([nh - 1], (part_out, part_sg), True)
    sg_recv = swap(sg_send, "seq", 1)

    vec_block = (shape((nh, 8, width), f32), None)
    rg, ag, vec2, na, sgt = run_kernel(
        functools.partial(second_back_body, hs, nh), "second_back", (1,), sc,
        [(a, None) for a in (sg_own, sg_recv, res, gyt, gains, mixd, starts, qf)] + in_hbm(all_first),
        [(shape((model, tok), f32), None), (shape((model, tok), bf), None), vec_block,
         (shape((heads, AUG, tok), bf), None), (shape((heads, AUG, 2 * hs), bf), None)],
        scratch=wo_scratch,
    )
    sgt = after(sgt, *w_got)
    g_sent = [swap(sgt, "head", m) for m in peers]
    half_spec = pl.BlockSpec((half, tok), lambda p, sc: (sc[0], 0))
    ag_peer = swap(lax.dynamic_slice_in_dim(ag, (1 - s2) * half, half, 0), "seq", 1)

    na_late = na
    ql, kfg, vg = run_kernel(
        functools.partial(local_back_body, hp, hs), "local_back", (nh,), sc,
        [(qf, feat_spec), (kf, feat_spec), (va, va_spec), (na_late, va_spec), (sin, state_spec), (starts, None)],
        [(shape((heads, hs, tok), bf), lead(hp, hs, tok)), (shape((heads, 2 * hs, tok), f32), feat_spec),
         (shape((heads, hs, tok), f32), lead(hp, hs, tok))],
    )
    g_around = [after(a, ql) for a in g_sent]
    w_got.append(swap(after(w_last, *g_around), "head", nh - 1))
    g_whole = states_together(4 + 3 * nh, [sgt] + g_around)
    after_run = chain_seq(g_whole, False, lambda k: (run_start <= -(k - 1) * length - 1).astype(f32))
    def peer_states(a, m):
        return (a, pl.BlockSpec((hp, AUG, 2 * hs), lambda p, sc: (p ^ m, 0, 0)))

    *pg, fg, map_grads, pb = run_kernel(
        functools.partial(project_back_body, hp, hs, nh), "project_back", (nh,), sc,
        [peer_states(a, m) for a, m in zip(g_around + [after_run], [*peers, 0])] + in_hbm(all_first)
        + [(kf, feat_spec), (va, va_spec), (ql, lead(hp, hs, tok)), (after(kfg, ag_peer, mix_peer), feat_spec), (vg, lead(hp, hs, tok)),
           (proj, lead(1, pc, tok)), (starts, None)],
        [(shape((pc, tok), bf), None)] * nh
        + [(shape((model, tok), f32), None),
           (shape((nh, hs, 128 * hp), f32), lead(1, hs, 128 * hp)), (shape((nh, 8, pc), f32), lead(1, 8, pc))],
        scratch=[pltpu.VMEM((1, pc, tok), bf)] + first_scratch,
    )
    pg_peer = [swap(a, "seq", 1) for a in pg]
    tg, vec1 = run_kernel(
        functools.partial(first_back_body, nh), "first_back", (1,), sc,
        [(fg, None), (x, None), (rg, None), (gains, None)], [(shape((nh, width, tok), bf), None), vec_block],
    )
    last_rows = -(-(pc + hs + TILE + width) // (nz * TILE)) * nz * TILE
    last_parts = run_kernel(
        functools.partial(last_grads_body, nh), "last_grads", (1,), sc,
        [(a, None) for a in (*pg, *pg_peer)] + [(hid, half_spec), (hid_peer, None)]
        + [(a, None) for a in (after(map_grads, w_got[-1]), pb, own_ub, early_ub, late_ub, vec1, vec2, mix, mix_peer)]
        + [(ag, half_spec), (ag_peer, None)],
        [(shape((last_rows, half), bf), None)] * nh,
        scratch=[pltpu.VMEM((TILE, half), f32)],
    )

    feed_rows, part_rows = all_rows // nz, last_rows // nz

    def halves_of(body, name, arrays, rows):
        return run_kernel(
            functools.partial(body, nh, nz), name, (1,), sc, [(a, None) for a in arrays],
            [(shape((2 * rows, hh), bf), None)] * 2, scratch=[pltpu.VMEM((nz * rows, hh), bf)],
        )

    def quarter(name, keep, got, rows):
        return run_kernel(
            pair_sum_body, name, (1,), sc, [(keep, None), (got, None)], [(shape((rows, hh), bf), None)] * 2
        )

    def spread(one):
        two = swap(one, "dp", 2)
        return [one, swap(one, "dp", 1), two, swap(two, "dp", 1)]

    feed_keep, feed_send = halves_of(
        feed_sum_body, "feed_sum", (after(w_parts[0], *last_parts), *w_got), feed_rows
    )
    feed_keep, feed_send = beyond_chip(feed_keep), beyond_chip(feed_send)
    out_recv = swap(after(out_send, *pg), "seq", 1)
    (chunks,) = run_kernel(
        functools.partial(block_out_body, nh), "block_out", (1,), sc,
        [(after(res, feed_keep), None), (out_own, None), (out_recv, None), (tg, None)] + row_specs,
        [(shape((nh, 2, width, tok), bf), None)], scratch=[pltpu.VMEM((model, tok), f32)],
    )
    feed_near, feed_next = quarter("feed_pair", feed_keep, swap(feed_send, "dp", 1), feed_rows)
    feed_far = swap(feed_next, "dp", 2)
    last_got = [after(swap(last_parts[m], "head", m), chunks, feed_near) for m in peers]
    last_keep, last_send = halves_of(last_sum_body, "last_sum", (last_parts[0], *last_got), part_rows)
    last_keep, last_send = beyond_chip(last_keep), beyond_chip(last_send)
    last_pair = swap(last_send, "dp", 1)
    feed_one = (feed_near.astype(f32) + after(feed_far, last_pair).astype(f32)).astype(bf)
    last_near, last_next = quarter("last_pair", last_keep, last_pair, part_rows)
    last_one = (last_near.astype(f32) + swap(last_next, "dp", 2).astype(f32)).astype(bf)
    feed_total, last_total = spread(feed_one), spread(last_one)
    chunks = trade(after(chunks, last_keep), "head")
    block_out, tokens_grad = run_kernel(
        functools.partial(lay_out_body, nh), "lay_out", (1,), sc, [(chunks, None)],
        [(shape((width, length), bf), None)] * 2,
    )
    upweight_grad, downweight_grad = run_kernel(
        functools.partial(feed_out_body, nh, nz), "feed_result", (1,), sc, [(a, None) for a in feed_total] + [(swap(a, "seq", 1), None) for a in feed_total],
        [(shape((model, hidden), f32), None), (shape((hidden, model), f32), None)],
        scratch=[pltpu.VMEM((2, all_rows, hh), bf)],
    )
    last_total = [after(a, upweight_grad, block_out) for a in last_total]
    qkv_grad, outweight_grad, query_grad, key_grad, qkvbias_grad, upbias_grad, rows = run_kernel(
        functools.partial(last_out_body, hs, nh, nz), "last_result", (1,), sc, [(a, None) for a in last_total] + [(swap(a, "seq", 1), None) for a in last_total],
        [(shape((pc, model), f32), None), (shape((width, model), f32), None), (shape((hp, hs, hs), f32), None),
         (shape((hp, hs, hs), f32), None),
         (shape((1, pc), f32), None), (shape((1, hidden), f32), None), (shape((TILE, half), f32), None)],
        scratch=[pltpu.VMEM((2, last_rows, half), bf)],
    )
    vec = rows[4:10, 0:width]
    return (block_out.T[None], tokens_grad.T[None], vec[4], vec[5], qkv_grad.T, qkvbias_grad[0], query_grad, key_grad,
            outweight_grad, vec[2], vec[0], vec[1], upweight_grad, upbias_grad[0], downweight_grad, vec[3])


def solution(mesh):
    wide = P("dp", "seq", "head")
    return jax.shard_map(
        local,
        mesh=mesh,
        in_specs=(wide, P(), P(), P(None, "head"), P("head"), P("head", None, None), P("head", None, None),
                  P("head", None), P("head"), P(), P(), P(None, "head"), P("head"), P("head", None), P("head"),
                  P("dp", "seq"), wide),
        out_specs=(wide, wide, P("head"), P("head"), P(None, "head"), P("head"), P("head", None, None),
                   P("head", None, None), P("head", None), P("head"), P("head"), P("head"), P(None, "head"), P("head"),
                   P("head", None), P("head")),
        check_vma=False,
    )
```
